32 devices in a mesh: dp: 4 (over y, x), seq: 8 (over z, core).
Axes of the slice: x: 2, y: 2, z: 4, core: 2. Of those that a mesh axis runs over, the one named last changes fastest.
Arguments:
- tokens: bfloat16 [8, 1024, 2048], P('dp', 'seq'), may hold values from -6 to 6
- lengths: int32 [8], P('dp'), may hold values from 256 to 1024, as said below
- gains: bfloat16 [2, 2048], P(None, ('dp', 'seq')), may hold values from 0.5 to 1.5
- w_query: bfloat16 [2048, 1024], P(('dp', 'seq')), may hold values from -0.125 to 0.125
- w_keyval: bfloat16 [2048, 512], P(('dp', 'seq')), may hold values from -0.125 to 0.125
- w_attn_out: bfloat16 [1024, 2048], P(('dp', 'seq')), may hold values from -0.5 to 0.5
- w_in: bfloat16 [2048, 6656], P(('dp', 'seq')), may hold values from -0.125 to 0.125
- w_dt: bfloat16 [2048, 48], P(('dp', 'seq')), may hold values from -0.125 to 0.125
- conv_params: bfloat16 [5, 3584], P(None, ('dp', 'seq')), may hold values from -0.5 to 0.5
- head_params: float32 [3, 48], replicated, may hold values from -11 to 1.5, as said below
- w_mamba_out: bfloat16 [3072, 2048], P(('dp', 'seq')), may hold values from -0.013671875 to 0.013671875
- w_gate_up: bfloat16 [2048, 8192], P(('dp', 'seq')), may hold values from -0.125 to 0.125
- w_down: bfloat16 [4096, 2048], P(('dp', 'seq')), may hold values from -0.09375 to 0.09375
- cotangent: bfloat16 [8, 1024, 2048], P('dp', 'seq'), may hold values from -6 to 6
Outputs:
- mixed: bfloat16 [8, 1024, 2048], P('dp', 'seq')
- grad_tokens: bfloat16 [8, 1024, 2048], P('dp', 'seq')
- grad_gains: float32 [2, 2048], P(None, ('dp', 'seq'))
- grad_query: float32 [2048, 1024], P(('dp', 'seq'))
- grad_keyval: float32 [2048, 512], P(('dp', 'seq'))
- grad_attn_out: float32 [1024, 2048], P(('dp', 'seq'))
- grad_in: float32 [2048, 6656], P(('dp', 'seq'))
- grad_dt: float32 [2048, 48], P(('dp', 'seq'))
- grad_conv: float32 [5, 3584], P(None, ('dp', 'seq'))
- grad_head: float32 [2, 48], replicated
- grad_skip: float32 [48], replicated
- grad_mamba_out: float32 [3072, 2048], P(('dp', 'seq'))
- grad_gate_up: float32 [2048, 8192], P(('dp', 'seq'))
- grad_down: float32 [4096, 2048], P(('dp', 'seq'))
The draws below stay inside these ranges and needn't reach their ends.
Inputs may be any that keep to these rules, and one draw needn't show every extreme that they name: `lengths`: of the 2 sequences of each index of dp, one, drawn from the seed, has all 1024 positions valid. `head_params`: row 0 is the time-step bias, row 1 the logarithm of each head's decay rate, row 2 the skip coefficient.
All inputs are finite; a program needn't handle non-finite values.
Results may differ from the reference program's by a relative error of at most 0.015.
Values may be sent and summed in bfloat16 or wider, within the bound.
No kernel may reach another device: no remote copies, remote signals or barrier semaphores. Data moves between devices by JAX's collectives and lax.ppermute only.
A program may use at most 640 MiB of HBM per device.

```python
import math
import jax
import jax.numpy as jnp
from jax import lax

D = 2048
FF = 4096
HQ = 8
KV = 2
HD = 128
MH = 48
MP = 64
NS = 256
KW = 4
SEQS = 2
MI = 3072
XC = 3584
SEQ_LEN = 1024
SEQUENCES = 8


def draw_lengths(key, part):
    key = jax.random.fold_in(key, 11)
    pick_key, len_key = jax.random.split(key)
    groups = SEQUENCES // SEQS
    ragged = jax.random.randint(len_key, (groups, SEQS), SEQ_LEN // 4, SEQ_LEN + 1)
    full_slot = jax.random.randint(pick_key, (groups, 1), 0, SEQS)
    slots = jnp.arange(SEQS)[None, :]
    return jnp.where(slots == full_slot, SEQ_LEN, ragged).reshape(SEQUENCES).astype(jnp.int32)


def draw_head_params(key, part):
    key = jax.random.fold_in(key, 23)
    bias_key, rate_key, skip_key = jax.random.split(key, 3)
    bias = jax.random.uniform(bias_key, (MH,), jnp.float32, -1.0, 1.0)
    top_rate = 0.1
    rate_log = jax.random.uniform(rate_key, (MH,), jnp.float32, math.log(0.2 / SEQ_LEN), math.log(top_rate))
    skip = jax.random.uniform(skip_key, (MH,), jnp.float32, 0.5, 1.5)
    return jnp.stack([bias, rate_log, skip])


def shard_levels(rng, shape, pieces, least, top_value):
    def one(axis_at, blocks):
        draws = jax.random.uniform(jax.random.fold_in(jax.random.fold_in(rng, 6), axis_at), (blocks,), jnp.float32, least / len(pieces), top_value / len(pieces))
        return jnp.repeat(jnp.exp(draws), shape[axis_at] // blocks).reshape((-1,) + (1,) * (len(shape) - axis_at - 1))

    level = one(*pieces[0])
    for cut in pieces[1:]:
        level = level * one(*cut)
    return level


def centred(key, shape, spread, limit, pieces=(), kind=jnp.bfloat16):
    result = jax.random.normal(key, shape, jnp.float32) * spread
    if len(pieces) > 0:
        result = shard_levels(key, shape, pieces, -0.22, 0.18) * result
    return jnp.clip(result, min=-limit, max=limit).astype(kind)


def setup_inputs(seed: int = 0) -> dict:
    seeds = jax.random.split(jax.random.key(seed), 15)
    return {
        "tokens": centred(seeds[0], (SEQUENCES, SEQ_LEN, D), 1.0, 6.0, ((0, 4), (1, 8))),
        "lengths": draw_lengths(jax.random.fold_in(seeds[14], 71), 0),
        "gains": jnp.clip(1.0 + 0.1 * jax.random.normal(seeds[2], (2, D), jnp.float32), 0.5, 1.5).astype(jnp.bfloat16),
        "w_query": centred(seeds[3], (D, HQ * HD), D ** -0.5, 0.125, ((0, 32),)),
        "w_keyval": centred(seeds[4], (D, 2 * KV * HD), D ** -0.5, 0.125, ((0, 32),)),
        "w_attn_out": centred(seeds[5], (HQ * HD, D), (HQ * HD // 8) ** -0.5, 0.5, ((0, 32),)),
        "w_in": centred(seeds[6], (D, 2 * MI + 2 * NS), D ** -0.5, 0.125, ((0, 32),)),
        "w_dt": centred(seeds[7], (D, MH), D ** -0.5, 0.125, ((0, 32),)),
        "conv_params": jnp.clip(jax.random.uniform(seeds[8], (KW + 1, XC), jnp.float32, -0.5, 0.5) * shard_levels(seeds[8], (KW + 1, XC), ((1, 32),), -0.4, 0.0), -0.5, 0.5).astype(jnp.bfloat16),
        "head_params": draw_head_params(jax.random.fold_in(seeds[14], 71), 0),
        "w_mamba_out": centred(seeds[10], (MI, D), (64 * MI) ** -0.5, 0.013671875, ((0, 32),)),
        "w_gate_up": centred(seeds[11], (D, 2 * FF), D ** -0.5, 0.125, ((0, 32),)),
        "w_down": centred(seeds[12], (FF, D), FF ** -0.5, 0.09375, ((0, 32),)),
        "cotangent": centred(seeds[13], (SEQUENCES, SEQ_LEN, D), 1.0, 6.0, ((0, 4), (1, 8))),
    }


epsilon = 1e-05
rope_base = 100000000000.0
neg_big = -1e+30
highest = lax.Precision.HIGHEST

@jax.custom_vjp
def low(v):
    return lax.optimization_barrier(v.astype(jnp.bfloat16)).astype(jnp.float32)

@jax.custom_vjp
def low_back(v):
    return v

def low_keep(v):
    return (low(v), None)

def low_pass(kept, grad):
    return (grad,)

def back_keep(v):
    return (v, None)

def back_low(kept, grad):
    return (low(grad),)
low.defvjp(low_keep, low_pass)
low_back.defvjp(back_keep, back_low)

def rms_norm(values, gain):
    return values * lax.rsqrt(lax.optimization_barrier(jnp.mean(values * values, -1, keepdims=True)) + epsilon) * gain

def rope_tables(positions, head_size):
    half = head_size // 2
    freq = jnp.exp(jnp.arange(half, dtype=jnp.float32) * (-2.0 * math.log(rope_base) / head_size))
    angle = positions.astype(jnp.float32)[:, None] * freq[None, :]
    return (jnp.concatenate([jnp.cos(angle), jnp.cos(angle)], -1), jnp.concatenate([jnp.sin(angle), jnp.sin(angle)], -1))

def rotate(values, cosine, sine):
    half = values.shape[-1] // 2
    turned = jnp.concatenate([-values[..., half:], values[..., :half]], -1)
    return values * cosine + turned * sine

def conv_apply(extended, conv_params):
    width = conv_params.shape[0] - 1
    count = extended.shape[-2] - width + 1
    total = conv_params[width]
    for offset in range(width):
        total = total + conv_params[offset] * lax.slice_in_dim(extended, offset, offset + count, axis=extended.ndim - 2)
    return jax.nn.silu(total)

def ssd_span(inner_x, bmat, cmat, step, decay_log, state):
    cum = jnp.cumsum(decay_log, axis=0)
    index = jnp.arange(cum.shape[0])
    lower = index[:, None] >= index[None, :]
    diff = cum.T[:, :, None] - cum.T[:, None, :]
    decay = jnp.exp(jnp.where(lower[None], diff, neg_big))
    inner = jnp.dot(cmat, bmat.T, precision=highest)
    mixing = decay * inner[None] * step.T[:, None, :]
    intra = jnp.einsum('hts,shp->thp', mixing, inner_x, precision=highest)
    carried = jnp.einsum('tn,hpn->thp', cmat, state, precision=highest) * jnp.exp(cum)[:, :, None]
    tail = jnp.exp(cum[-1][None, :] - cum) * step
    new_state = jnp.exp(cum[-1])[:, None, None] * state + jnp.einsum('sh,shp,sn->hpn', tail, inner_x, bmat, precision=highest)
    return (intra + carried, new_state)

def mamba_core(cvals, dt_raw, head_params, state):
    heads, head_size, nstate = state.shape
    inner = heads * head_size
    count = cvals.shape[0]
    inner_x = cvals[:, :inner].reshape(count, heads, head_size)
    bmat = cvals[:, inner:inner + nstate]
    cmat = cvals[:, inner + nstate:]
    step = jax.nn.softplus(dt_raw + head_params[0])
    decay_log = -jnp.exp(head_params[1]) * step
    mixed, new_state = ssd_span(inner_x, bmat, cmat, step, decay_log, state)
    out = mixed + head_params[2][None, :, None] * inner_x
    return (out.reshape(count, inner), new_state)

def matmul(left, right):
    return jnp.dot(left, right, precision=highest)

def layer(seq_tokens, length, gains, w_query, w_keyval, w_attn_out, w_in, w_dt, conv_params, head_params, w_mamba_out, w_gate_up, w_down):
    seq_len = seq_tokens.shape[0]
    positions = jnp.arange(seq_len, dtype=jnp.int32)
    valid = (positions < length).astype(jnp.float32)[:, None]
    normed1 = low(rms_norm(seq_tokens, gains[0]))
    cosine, sine = rope_tables(positions, HD)
    cosine = cosine[:, None, :]
    sine = sine[:, None, :]
    q_raw = low_back(matmul(normed1, w_query)).reshape(seq_len, HQ, HD)
    queries = low(rotate(q_raw, cosine, sine))
    kv_raw = low_back(matmul(normed1, w_keyval)).reshape(seq_len, 2, KV, HD)
    keys = low(rotate(kv_raw[:, 0], cosine, sine))
    values = low(kv_raw[:, 1])
    keys_head = jnp.repeat(keys, HQ // KV, axis=1)
    values_head = jnp.repeat(values, HQ // KV, axis=1)
    block = math.gcd(512, seq_len)
    scale = 1.0 / math.sqrt(HD)

    def attend(inputs):
        qblock, qpos = inputs
        scores = jnp.einsum('qhd,khd->hqk', qblock, keys_head, precision=highest) * scale
        scores = low_back(scores)
        allowed = (positions[None, :] <= qpos[:, None]) & (positions[None, :] < length)
        scores = jnp.where(allowed[None], scores, neg_big)
        top = lax.optimization_barrier(jnp.max(scores, -1, keepdims=True))
        expo = jnp.exp(scores - top)
        prob = low(expo / lax.optimization_barrier(jnp.sum(expo, -1, keepdims=True)))
        return jnp.einsum('hqk,khd->qhd', prob, values_head, precision=highest)
    attn_raw = lax.map(jax.checkpoint(attend), (queries.reshape(seq_len // block, block, HQ, HD), positions.reshape(seq_len // block, block)))
    attn_o = low_back(low(attn_raw.reshape(seq_len, HQ * HD)))
    attn_part = low_back(matmul(attn_o, w_attn_out))
    proj = low_back(matmul(normed1, w_in))
    inner = MH * MP
    gate_z = proj[:, :inner]
    xbc = proj[:, inner:]
    dt_raw = low_back(matmul(normed1, w_dt))
    extended = jnp.concatenate([jnp.zeros((KW - 1, xbc.shape[1]), jnp.float32), xbc], 0)
    cvals = conv_apply(extended, conv_params)
    span = math.gcd(256, seq_len)
    count = seq_len // span

    def span_step(state, inputs):
        out, new_state = mamba_core(inputs[0], inputs[1], head_params, state)
        return (new_state, out)
    zero_state = jnp.zeros((MH, MP, NS), jnp.float32)
    _, outs = lax.scan(jax.checkpoint(span_step), zero_state, (cvals.reshape(count, span, -1), dt_raw.reshape(count, span, MH)))
    ssm_out = outs.reshape(seq_len, inner)
    gated = low(ssm_out * jax.nn.silu(gate_z))
    mamba_part = low_back(matmul(gated, w_mamba_out))
    hidden = seq_tokens + valid * (attn_part + mamba_part)
    normed2 = low(rms_norm(hidden, gains[1]))
    gate_up = low_back(matmul(normed2, w_gate_up))
    width = gate_up.shape[1] // 2
    act = low(jax.nn.silu(gate_up[:, :width]) * gate_up[:, width:])
    ffn_part = low_back(matmul(act, w_down))
    return hidden + valid * ffn_part

def reference(tokens, lengths, gains, w_query, w_keyval, w_attn_out, w_in, w_dt, conv_params, head_params, w_mamba_out, w_gate_up, w_down, cotangent):
    params = tuple((p.astype(jnp.float32) for p in (gains, w_query, w_keyval, w_attn_out, w_in, w_dt, conv_params, head_params, w_mamba_out, w_gate_up, w_down)))

    def one_sequence(totals, inputs):
        seq_tokens, seq_cot, length = inputs

        def apply(values, *weights):
            return layer(values, length, *weights)
        out, pull = jax.vjp(apply, seq_tokens.astype(jnp.float32), *params)
        grads = pull(seq_cot.astype(jnp.float32))
        new_totals = tuple((a + b for a, b in zip(totals, grads[1:])))
        return (new_totals, (out.astype(jnp.bfloat16), grads[0].astype(jnp.bfloat16)))
    zeros = tuple((jnp.zeros_like(p) for p in params))
    totals, (mixed, grad_tokens) = lax.scan(one_sequence, zeros, (tokens, cotangent, lengths))
    head_total = totals[7]
    return (mixed, grad_tokens, totals[0], totals[1], totals[2], totals[3], totals[4], totals[5], totals[6], head_total[:2], head_total[2], totals[8], totals[9], totals[10])
```

```python
import functools
import math

import jax
import jax.numpy as jnp
from jax import lax
from jax.experimental import pallas as pl
from jax.experimental.pallas import tpu as pltpu
from jax.sharding import Mesh
from jax.sharding import PartitionSpec as P

HQ = 8
KV = 2
HD = 128
MH = 48
MP = 64
NS = 256
KW = 4
MI = MH * MP

epsilon = 1e-05
rope_base = 100000000000.0
neg_big = -1e30
highest = lax.Precision.HIGHEST
bf16 = jnp.bfloat16
f32 = jnp.float32

ALL = ("dp", "g", "z", "c")
TEAM = ("z", "c")
PLANE = ("dp", "c")
LINE = ("g", "z")
SEQ = ("g", "z", "c")
SPREAD = ("dp", "g")


def rms_norm(values, gain):
    return values * lax.rsqrt(jnp.mean(values * values, -1, keepdims=True) + epsilon) * gain


def rope_tables(positions, head_size):
    half = head_size // 2
    freq = jnp.exp(jnp.arange(half, dtype=f32) * (-2.0 * math.log(rope_base) / head_size))
    angle = positions.astype(f32)[:, None] * freq[None, :]
    return (
        jnp.concatenate([jnp.cos(angle), jnp.cos(angle)], -1),
        jnp.concatenate([jnp.sin(angle), jnp.sin(angle)], -1),
    )


def rotate(values, cosine, sine):
    half = values.shape[-1] // 2
    turned = jnp.concatenate([-values[..., half:], values[..., :half]], -1)
    return values * cosine + turned * sine


def rotate_back(grads, cosine, sine):
    half = grads.shape[-1] // 2
    scaled = grads * sine
    return grads * cosine + jnp.concatenate([scaled[..., half:], -scaled[..., :half]], -1)


def dot(left, right, precision=None):
    return jnp.dot(left, right, preferred_element_type=f32, precision=precision)


def dot_first(left, right, precision=None):
    return lax.dot_general(
        left, right, (((0,), (0,)), ((), ())), preferred_element_type=f32, precision=precision
    )


def dot_last(left, right, precision=None):
    return lax.dot_general(
        left, right, (((1,), (1,)), ((), ())), preferred_element_type=f32, precision=precision
    )


def sigmoid(v):
    return 1.0 / (1.0 + jnp.exp(-v))


def softplus(v):
    return jnp.maximum(v, 0.0) + jnp.log(1.0 + jnp.exp(-jnp.abs(v)))


def params(count):
    return pltpu.CompilerParams(
        dimension_semantics=("arbitrary",) * count, vmem_limit_bytes=48 * 1024 * 1024
    )


def attend_mask(length_ref, start_ref, seq, block, width, first):
    qpos = start_ref[0] + first + lax.broadcasted_iota(jnp.int32, (block, width), 0)
    kpos = lax.broadcasted_iota(jnp.int32, (block, width), 1)
    return (kpos <= qpos) & (kpos < length_ref[seq])


def attend_fore_kernel(length_ref, start_ref, q_ref, k_ref, v_ref, o_ref, log_ref, *, scale, block):
    seq, at = pl.program_id(0), pl.program_id(1)
    keys = k_ref[0]
    scores = dot_last(q_ref[0], keys) * scale
    allowed = attend_mask(length_ref, start_ref, seq, block, keys.shape[0], at * block)
    scores = jnp.where(allowed, scores, neg_big)
    top = jnp.max(scores, -1, keepdims=True)
    expo = jnp.exp(scores - top)
    total = jnp.sum(expo, -1, keepdims=True)
    prob = (expo * (1.0 / total)).astype(bf16)
    o_ref[0] = dot(prob, v_ref[0]).astype(bf16)
    log_ref[0] = jnp.broadcast_to(top + jnp.log(total), log_ref.shape[1:])


def attend_fore(length, start, q, k, v, block):
    seqs, rows, width = q.shape
    kernel = functools.partial(attend_fore_kernel, scale=1.0 / math.sqrt(HD), block=block)
    qspec = pl.BlockSpec((1, block, width), lambda s, i: (s, i, 0))
    kspec = pl.BlockSpec((1, k.shape[1], width), lambda s, i: (s, 0, 0))
    smem = pl.BlockSpec(memory_space=pltpu.SMEM)
    return pl.pallas_call(
        kernel,
        grid=(seqs, rows // block),
        in_specs=[smem, smem, qspec, kspec, kspec],
        out_specs=[qspec, qspec],
        out_shape=[
            jax.ShapeDtypeStruct(q.shape, bf16),
            jax.ShapeDtypeStruct(q.shape, f32),
        ],
        compiler_params=params(2),
        name="attend_fore",
    )(length, start, q, k, v)


def attend_back_kernel(
    length_ref, start_ref, q_ref, k_ref, v_ref, do_ref, log_ref, dq_ref, dk_ref, dv_ref, *, scale, block
):
    seq, at = pl.program_id(0), pl.program_id(1)

    @pl.when(at == 0)
    def _():
        dk_ref[...] = jnp.zeros_like(dk_ref)
        dv_ref[...] = jnp.zeros_like(dv_ref)

    keys = k_ref[0]
    queries = q_ref[0]
    grad_out = do_ref[0]
    scores = dot_last(queries, keys) * scale
    allowed = attend_mask(length_ref, start_ref, seq, block, keys.shape[0], at * block)
    scores = jnp.where(allowed, scores, neg_big)
    prob = jnp.exp(scores - log_ref[0][:, :1])
    grad_prob = dot_last(grad_out, v_ref[0])
    centre = jnp.sum(prob * grad_prob, -1, keepdims=True)
    grad_score = (prob * (grad_prob - centre)).astype(bf16)
    dq_ref[0] = dot(grad_score, keys) * scale
    dk_ref[0] += dot_first(grad_score, queries) * scale
    dv_ref[0] += dot_first(prob.astype(bf16), grad_out)


def attend_back(length, start, q, k, v, grad_out, logs, block):
    seqs, rows, width = q.shape
    kernel = functools.partial(attend_back_kernel, scale=1.0 / math.sqrt(HD), block=block)
    qspec = pl.BlockSpec((1, block, width), lambda s, i: (s, i, 0))
    kspec = pl.BlockSpec((1, k.shape[1], width), lambda s, i: (s, 0, 0))
    smem = pl.BlockSpec(memory_space=pltpu.SMEM)
    return pl.pallas_call(
        kernel,
        grid=(seqs, rows // block),
        in_specs=[smem, smem, qspec, kspec, kspec, qspec, qspec],
        out_specs=[qspec, kspec, kspec],
        out_shape=[
            jax.ShapeDtypeStruct(q.shape, f32),
            jax.ShapeDtypeStruct(k.shape, f32),
            jax.ShapeDtypeStruct(k.shape, f32),
        ],
        compiler_params=params(2),
        name="attend_back",
    )(length, start, q, k, v, grad_out, logs)


def head_spread(heads):
    row = lax.broadcasted_iota(jnp.int32, (128, heads * MP), 0)
    col = lax.broadcasted_iota(jnp.int32, (128, heads * MP), 1)
    return (row == col // MP).astype(f32)


def triangle(span):
    row = lax.broadcasted_iota(jnp.int32, (span, span), 0)
    col = lax.broadcasted_iota(jnp.int32, (span, span), 1)
    return row >= col


def conv_pre(ext_ref, conv_ref, span):
    total = conv_ref[KW : KW + 1, :]
    for k in range(KW):
        total = total + conv_ref[k : k + 1, :] * ext_ref[pl.ds(8 - (KW - 1) + k, span), :]
    return total


def core_fore_kernel(
    x_ref, bc_ref, z_ref, dt_ref, halo_ref, conv_ref, head_ref, init_ref,
    gated_ref, y_ref, enter_ref, final_ref, decay_ref,
    ext, state, total, *, heads, span,
):
    inner = heads * MP
    at = pl.program_id(1)

    @pl.when(at == 0)
    def _():
        ext[0:8, :] = halo_ref[0]
        state[...] = init_ref[0]
        total[...] = jnp.zeros_like(total)

    ext[8:, :inner] = x_ref[...]
    ext[8:, inner:] = bc_ref[...]
    pre = conv_pre(ext, conv_ref, span)
    ext[0:8, :] = ext[span : span + 8, :]
    cv = pre * sigmoid(pre)
    xs = cv[:, :inner]
    bmat = cv[:, inner : inner + NS].astype(bf16)
    cmat = cv[:, inner + NS :].astype(bf16)
    spread = head_spread(heads)
    lower = triangle(span)
    step = softplus(dt_ref[...] + head_ref[0:1, :])
    decay_log = -jnp.exp(head_ref[1:2, :]) * step
    cum = dot(lower.astype(f32), decay_log, highest)
    cum_t = cum.T
    step_t = step.T
    last = cum[span - 1 : span, :]
    enter = state[...]
    enter_ref[0, 0] = enter
    pair = dot_last(cmat, bmat)
    xb = xs.astype(bf16)
    parts = []
    for h in range(heads):
        diff = cum[:, h : h + 1] - cum_t[h : h + 1, :]
        decay = jnp.exp(jnp.where(lower, diff, neg_big))
        mixing = (pair * decay * step_t[h : h + 1, :]).astype(bf16)
        parts.append(dot(mixing, xb[:, h * MP : (h + 1) * MP]))
    y = jnp.concatenate(parts, axis=1)
    y = y + dot_last(cmat, enter.astype(bf16)) * dot(jnp.exp(cum), spread, highest)
    y = y + xs * dot(jnp.broadcast_to(head_ref[2:3, :], (8, 128)), spread, highest)[0:1, :]
    tail = dot(jnp.exp(last - cum) * step, spread, highest)
    keep = jnp.broadcast_to(jnp.exp(cum_t[:, span - 1 : span]), (128, NS))
    new_state = dot_first(spread, keep, highest) * enter + dot_first((xs * tail).astype(bf16), bmat)
    state[...] = new_state
    final_ref[0] = new_state
    total[...] = total[...] + last
    decay_ref[0] = total[...]
    z = z_ref[...]
    y_ref[...] = y
    gated_ref[...] = (y * (z * sigmoid(z))).astype(bf16)


def core_fore(big, small, halo, conv, head, init, seqs, heads, span):
    rows = big.shape[0]
    inner = heads * MP
    wide = inner + 2 * NS
    count = rows // seqs // span
    dt_at = (small.shape[1] - 128) // 128

    def block(width, at):
        return pl.BlockSpec((span, width), lambda s, i: (s * count + i, at))

    state_spec = pl.BlockSpec((1, inner, NS), lambda s, i: (s, 0, 0))
    return pl.pallas_call(
        functools.partial(core_fore_kernel, heads=heads, span=span),
        grid=(seqs, count),
        in_specs=[
            block(inner, 1),
            block(2 * NS, 0),
            block(inner, 0),
            block(128, dt_at),
            pl.BlockSpec((1, 8, wide), lambda s, i: (s, 0, 0)),
            pl.BlockSpec((8, wide), lambda s, i: (0, 0)),
            pl.BlockSpec((8, 128), lambda s, i: (0, 0)),
            state_spec,
        ],
        out_specs=[
            block(inner, 0),
            block(inner, 0),
            pl.BlockSpec((1, 1, inner, NS), lambda s, i: (s, i, 0, 0)),
            state_spec,
            pl.BlockSpec((1, 8, 128), lambda s, i: (s, 0, 0)),
        ],
        out_shape=[
            jax.ShapeDtypeStruct((rows, inner), bf16),
            jax.ShapeDtypeStruct((rows, inner), f32),
            jax.ShapeDtypeStruct((seqs, count, inner, NS), f32),
            jax.ShapeDtypeStruct((seqs, inner, NS), f32),
            jax.ShapeDtypeStruct((seqs, 8, 128), f32),
        ],
        scratch_shapes=[
            pltpu.VMEM((span + 8, wide), f32),
            pltpu.VMEM((inner, NS), f32),
            pltpu.VMEM((8, 128), f32),
        ],
        compiler_params=params(2),
        name="core_fore",
    )(big, small, big, small, halo, conv, head, init)


def core_back_kernel(
    x_ref, bc_ref, z_ref, dt_ref, dg_ref, y_ref, enter_ref, halo_ref, conv_ref, head_ref, exit_ref,
    dzx_ref, dbc_ref, ddt_ref, gconv_ref, ghead_ref, dinit_ref, dfirst_ref,
    ext, dext, dstate, *, heads, span,
):
    inner = heads * MP
    seq, at = pl.program_id(0), pl.program_id(1)

    @pl.when((seq == 0) & (at == 0))
    def _():
        gconv_ref[...] = jnp.zeros_like(gconv_ref)
        ghead_ref[...] = jnp.zeros_like(ghead_ref)

    @pl.when(at == 0)
    def _():
        dext[span:, :] = jnp.zeros((8, dext.shape[1]), f32)
        dstate[...] = exit_ref[0]

    ext[0:8, :] = halo_ref[0, 0]
    ext[8:, :inner] = x_ref[...]
    ext[8:, inner:] = bc_ref[...]
    pre = conv_pre(ext, conv_ref, span)
    gate = sigmoid(pre)
    cv = pre * gate
    xs = cv[:, :inner]
    bmat = cv[:, inner : inner + NS].astype(bf16)
    cmat = cv[:, inner + NS :].astype(bf16)
    xb = xs.astype(bf16)
    z = z_ref[...]
    sig_z = sigmoid(z)
    grad_gated = dg_ref[...]
    dy = grad_gated * (z * sig_z)
    dzx_ref[:, :inner] = (grad_gated * y_ref[...] * (sig_z * (1.0 + z * (1.0 - sig_z)))).astype(bf16)
    dyb = dy.astype(bf16)
    spread = head_spread(heads)
    lower = triangle(span)
    raw = dt_ref[...] + head_ref[0:1, :]
    step = softplus(raw)
    rate = -jnp.exp(head_ref[1:2, :])
    decay_log = rate * step
    cum = dot(lower.astype(f32), decay_log, highest)
    cum_t = cum.T
    step_t = step.T
    last = cum[span - 1 : span, :]
    enter = enter_ref[0, 0]
    leave = dstate[...]
    pair = dot_last(cmat, bmat)
    dpair = jnp.zeros((span, span), f32)
    lane = lax.broadcasted_iota(jnp.int32, (span, 128), 1)
    line = lax.broadcasted_iota(jnp.int32, (128, span), 0)
    row_sums = jnp.zeros((span, 128), f32)
    col_sums = jnp.zeros((128, span), f32)
    parts = []
    for h in range(heads):
        diff = cum[:, h : h + 1] - cum_t[h : h + 1, :]
        decay = jnp.exp(jnp.where(lower, diff, neg_big))
        now = step_t[h : h + 1, :]
        cut = slice(h * MP, (h + 1) * MP)
        dmix = dot_last(dyb[:, cut], xb[:, cut]) * decay
        both = dmix * pair
        dmix_now = dmix * now
        dpair = dpair + dmix_now
        row_sums = jnp.where(lane == h, jnp.sum(both * now, 1, keepdims=True), row_sums)
        col_sums = jnp.where(line == h, jnp.sum(both, 0, keepdims=True), col_sums)
        mixing = (pair * decay * now).astype(bf16)
        parts.append(dot_first(mixing, dyb[:, cut]))
    dxs = jnp.concatenate(parts, axis=1)
    dstep = col_sums.T
    dcum = row_sums - dstep * step
    dpb = dpair.astype(bf16)
    dcm = dot(dpb, bmat)
    dbm = dot_first(dpb, cmat)
    grown = dot(jnp.exp(cum), spread, highest)
    enter_b = enter.astype(bf16)
    leave_b = leave.astype(bf16)
    dgrown = (dy * grown).astype(bf16)
    dcum = dcum + dot_last(dy * dot_last(cmat, enter_b) * grown, spread, highest)
    dcm = dcm + dot(dgrown, enter_b)
    fade = jnp.exp(last - cum)
    tail = dot(fade * step, spread, highest)
    into = dot_last(bmat, leave_b)
    dxs = dxs + into * tail
    owed = dot_last(xs * into, spread, highest) * fade
    dstep = dstep + owed
    owed = owed * step
    dcum = dcum - owed
    dbm = dbm + dot((xs * tail).astype(bf16), leave_b)
    held = dot(spread, enter * leave, highest)
    held = dot_last(jnp.ones((8, NS), f32), held, highest)[0:1, :]
    dlast = jnp.sum(owed, 0, keepdims=True) + jnp.exp(last) * held
    keep = jnp.broadcast_to(jnp.exp(cum_t[:, span - 1 : span]), (128, NS))
    new_dstate = dot_first(spread, keep, highest) * leave + dot_first(dgrown, cmat)
    dstate[...] = new_dstate
    dinit_ref[0] = new_dstate
    dlog = dot_first(lower.astype(f32), dcum, highest) + dlast
    dstep = dstep + dlog * rate
    ddt = dstep * sigmoid(raw)
    ddt_ref[...] = ddt.astype(bf16)
    skip = dot(jnp.broadcast_to(head_ref[2:3, :], (8, 128)), spread, highest)[0:1, :]
    dxs = dxs + skip * dy
    ghead_ref[0:1, :] += jnp.sum(ddt, 0, keepdims=True)
    ghead_ref[1:2, :] += jnp.sum(dlog * decay_log, 0, keepdims=True)
    ghead_ref[2:3, :] += jnp.sum(dot_last(dy * xs, spread, highest), 0, keepdims=True)
    slope = gate * (1.0 + pre * (1.0 - gate))
    dpre = jnp.concatenate([dxs, dbm, dcm], axis=1) * slope
    dext[0:span, :] = dpre
    gconv_ref[KW : KW + 1, :] += jnp.sum(dpre, 0, keepdims=True)
    dxbc = jnp.zeros_like(dpre)
    for k in range(KW):
        dxbc = dxbc + conv_ref[k : k + 1, :] * dext[pl.ds(KW - 1 - k, span), :]
        gconv_ref[k : k + 1, :] += jnp.sum(
            dpre * ext[pl.ds(8 - (KW - 1) + k, span), :], 0, keepdims=True
        )
    dzx_ref[:, inner:] = dxbc[:, :inner].astype(bf16)
    dbc_ref[...] = dxbc[:, inner:].astype(bf16)
    dext[span:, :] = dext[0:8, :]
    dfirst_ref[0] = dext[0:8, :]


def core_back(big, small, dmixed, y, enter, halos, conv, head, leave, seqs, heads, span):
    rows = big.shape[0]
    inner = heads * MP
    wide = inner + 2 * NS
    count = rows // seqs // span
    dt_at = (small.shape[1] - 128) // 128

    def block(width, at):
        return pl.BlockSpec((span, width), lambda s, i: (s * count + count - 1 - i, at))

    state_spec = pl.BlockSpec((1, inner, NS), lambda s, i: (s, 0, 0))
    return pl.pallas_call(
        functools.partial(core_back_kernel, heads=heads, span=span),
        grid=(seqs, count),
        in_specs=[
            block(inner, 1),
            block(2 * NS, 0),
            block(inner, 0),
            block(128, dt_at),
            block(inner, 0),
            block(inner, 0),
            pl.BlockSpec((1, 1, inner, NS), lambda s, i: (s, count - 1 - i, 0, 0)),
            pl.BlockSpec((1, 1, 8, wide), lambda s, i: (s, count - 1 - i, 0, 0)),
            pl.BlockSpec((8, wide), lambda s, i: (0, 0)),
            pl.BlockSpec((8, 128), lambda s, i: (0, 0)),
            state_spec,
        ],
        out_specs=[
            block(2 * inner, 0),
            block(2 * NS, 0),
            block(128, 0),
            pl.BlockSpec((8, wide), lambda s, i: (0, 0)),
            pl.BlockSpec((8, 128), lambda s, i: (0, 0)),
            state_spec,
            pl.BlockSpec((1, 8, wide), lambda s, i: (s, 0, 0)),
        ],
        out_shape=[
            jax.ShapeDtypeStruct((rows, 2 * inner), bf16),
            jax.ShapeDtypeStruct((rows, 2 * NS), bf16),
            jax.ShapeDtypeStruct((rows, 128), bf16),
            jax.ShapeDtypeStruct((8, wide), f32),
            jax.ShapeDtypeStruct((8, 128), f32),
            jax.ShapeDtypeStruct((seqs, inner, NS), f32),
            jax.ShapeDtypeStruct((seqs, 8, wide), f32),
        ],
        scratch_shapes=[
            pltpu.VMEM((span + 8, wide), f32),
            pltpu.VMEM((span + 8, wide), f32),
            pltpu.VMEM((inner, NS), f32),
        ],
        compiler_params=params(2),
        name="core_back",
    )(big, small, big, small, dmixed, y, enter, halos, conv, head, leave)


def passed_along(block, distance):
    devices = range(lax.axis_size("g"))
    route = [(i - distance, i) for i in devices if i - distance in devices]
    return lax.ppermute(block, "g", route)


def entering(decay, local, reverse):
    peers, here = lax.axis_size("g"), lax.axis_index("g")
    decays = lax.all_gather(decay, "g")
    locals_ = lax.all_gather(local.astype(bf16), "g")
    state = jnp.zeros_like(local)
    for k in range(peers):
        at = peers - 1 - k if reverse else k
        reached = (at > here) if reverse else (at < here)
        state = jnp.where(reached, decays[at] * state + locals_[at].astype(f32), state)
    return state


def head_decay(decay_log, heads):
    keep = jnp.exp(decay_log[:, 0, :heads])
    return jnp.repeat(keep, MP, axis=1)[:, :, None]


def body(
    tokens, lengths, gains, w_query, w_keyval, w_attn_out, w_in, w_dt, conv_params, head_params,
    w_mamba_out, w_gate_up, w_down, cotangent,
):
    seqs, rows_seq, width = tokens.shape
    own_rows = seqs * rows_seq
    dp, groups, team = lax.axis_size("dp"), lax.axis_size("g"), lax.axis_size(TEAM)
    devices, line, plane = lax.axis_size(ALL), lax.axis_size(LINE), lax.axis_size(PLANE)
    seq_size = groups * team
    me = lax.axis_index(TEAM)
    heads = MH // team
    inner = heads * MP
    query = HQ * HD // team
    block_len = rows_seq * team
    rows = seqs * block_len
    held = w_query.shape[0]
    span = math.gcd(256, block_len)
    start = (lax.axis_index("g") * block_len).astype(jnp.int32).reshape(1)
    kv_head = me * (HQ // team) * KV // HQ

    block_tokens = lax.all_gather(tokens, TEAM, axis=1, tiled=True).reshape(rows, width)
    conv_flat = conv_params.reshape(-1)
    conv_cols = -(-conv_flat.shape[0] // held)
    conv_flat = jnp.pad(conv_flat, (0, conv_cols * held - conv_flat.shape[0]))
    packed = jnp.concatenate(
        [w_in[:, 2 * MI :], w_keyval, w_dt, gains.T, conv_flat.reshape(held, conv_cols)], axis=1
    )
    packed = lax.all_gather(packed, ALL, axis=0, tiled=True)
    at = 2 * NS
    w_bc, at = packed[:, :at], at
    w_kv = packed[:, at : at + 2 * KV * HD].reshape(width, 2, KV, HD)
    at += 2 * KV * HD
    w_step = packed[:, at : at + MH]
    at += MH
    gain_all = packed[:, at : at + 2].astype(f32).T
    at += 2
    conv_size = conv_params.size
    conv_all = packed[:, at:].reshape(devices, held * conv_cols)[:, :conv_size]
    conv_all = (
        conv_all.reshape(devices, KW + 1, -1).transpose(1, 0, 2).reshape(KW + 1, -1).astype(f32)
    )
    conv_own = jnp.concatenate(
        [lax.dynamic_slice_in_dim(conv_all, me * inner, inner, 1), conv_all[:, MI:]], axis=1
    )
    conv_own = jnp.pad(conv_own, ((0, 8 - KW - 1), (0, 0)))
    head_own = jnp.pad(
        lax.dynamic_slice_in_dim(head_params, me * heads, heads, 1), ((0, 5), (0, 128 - heads))
    )
    w_small = jnp.concatenate(
        [
            w_bc,
            lax.dynamic_index_in_dim(w_kv, kv_head, 2, keepdims=False).reshape(width, 2 * HD),
            jnp.pad(
                lax.dynamic_slice_in_dim(w_step, me * heads, heads, 1), ((0, 0), (0, 128 - heads))
            ),
        ],
        axis=1,
    )
    w_big = jnp.concatenate(
        [
            w_in[:, :MI].reshape(held, team, inner),
            w_in[:, MI : 2 * MI].reshape(held, team, inner),
            w_query.reshape(held, team, query),
        ],
        axis=2,
    ).transpose(1, 0, 2)
    w_big = lax.all_to_all(w_big, TEAM, 0, 0, tiled=True).reshape(team * held, 2 * inner + query)
    w_big = lax.all_gather(w_big, SPREAD, axis=0, tiled=True)

    ratio = team // dp
    part = seq_size // ratio
    attn_rows, mamba_rows = w_attn_out.shape[0], w_mamba_out.shape[0]
    out_rows = attn_rows + mamba_rows
    cut = width // dp
    my_seq = lax.axis_index(SEQ)
    w_out = jnp.concatenate([w_attn_out, w_mamba_out], axis=0)
    w_out = w_out.reshape(out_rows, dp, cut).transpose(1, 0, 2)
    w_out = lax.all_to_all(w_out, "dp", 0, 0, tiled=True)
    mine = (jnp.arange(ratio) == my_seq // part)[None, :, None, None]
    w_out = jnp.where(mine, w_out[:, None], jnp.zeros((), bf16)).reshape(1, team, out_rows, cut)
    w_out = jnp.broadcast_to(w_out, (groups, team, out_rows, cut)).reshape(-1, out_rows, cut)
    w_out = lax.all_to_all(w_out, SEQ, 0, 0, tiled=True)
    w_out = lax.dynamic_slice_in_dim(w_out, (me % ratio) * part, part, 0)
    w_out = jnp.concatenate(
        [w_out[:, :attn_rows].reshape(-1, cut), w_out[:, attn_rows:].reshape(-1, cut)], axis=0
    )
    w_out = lax.all_gather(w_out, "dp", axis=1, tiled=True)

    ffn_block = w_down.shape[0]
    w_gu = w_gate_up.reshape(held, 2, dp, line, plane // dp, ffn_block).transpose(2, 4, 0, 1, 3, 5)
    w_gu = lax.all_to_all(
        w_gu.reshape(plane, held, 2 * line * ffn_block), PLANE, 0, 0, tiled=True
    ).reshape(dp, plane // dp, held, -1)
    w_gu = lax.all_gather(w_gu, LINE, axis=1, tiled=True).reshape(width, -1)
    w_dn = lax.all_gather(w_down, LINE, axis=0, tiled=True)

    norm1 = rms_norm(block_tokens.astype(f32), gain_all[0]).astype(bf16)
    big = dot(norm1, w_big)
    small = dot(norm1, w_small)
    positions = start[0] + jnp.arange(block_len, dtype=jnp.int32)
    cosine, sine = rope_tables(positions, HD)
    q = rotate(big[:, 2 * inner :].reshape(seqs, block_len, HD), cosine, sine).astype(bf16)
    k = rotate(
        small[:, 2 * NS : 2 * NS + HD].reshape(seqs, block_len, HD), cosine, sine
    ).astype(bf16)
    v = small[:, 2 * NS + HD : 2 * NS + 2 * HD].reshape(seqs, block_len, HD).astype(bf16)
    if groups > 1:
        k = lax.all_gather(k, "g", axis=1, tiled=True)
        v = lax.all_gather(v, "g", axis=1, tiled=True)
    attn, logs = attend_fore(lengths, start, q, k, v, span)
    wide = inner + 2 * NS
    xbc = jnp.concatenate([big[:, inner : 2 * inner], small[:, : 2 * NS]], axis=1)
    xbc = xbc.reshape(seqs, block_len // span, span, wide)
    ends = xbc[:, :, span - 8 :, :]
    if groups > 1:
        before = passed_along(ends[:, -1].astype(bf16), 1).astype(f32)
    else:
        before = jnp.zeros((seqs, 8, wide), f32)
    halos = jnp.concatenate([before[:, None], ends[:, :-1]], axis=1)
    init = jnp.zeros((seqs, inner, NS), f32)
    fore = functools.partial(core_fore, seqs=seqs, heads=heads, span=span)
    gated, y, enter, final, decay_log = fore(big, small, before, conv_own, head_own, init)
    if groups > 1:
        decay = head_decay(decay_log, heads)
        init = entering(decay, final, False)
        gated, y, enter, final, _ = fore(big, small, before, conv_own, head_own, init)
    mixed_in = jnp.concatenate([attn.reshape(rows, HD), gated], axis=1)
    mix = dot(mixed_in, w_out).astype(bf16).reshape(seqs, block_len, width)
    mix = lax.psum_scatter(mix, TEAM, scatter_dimension=1, tiled=True)
    own_positions = my_seq * rows_seq + jnp.arange(rows_seq, dtype=jnp.int32)
    valid = (own_positions[None, :] < lengths[:, None]).astype(f32).reshape(own_rows, 1)
    token_f = tokens.astype(f32).reshape(own_rows, width)
    hidden = token_f + valid * mix.astype(f32).reshape(own_rows, width)

    norm2_f, norm2_pull = jax.vjp(rms_norm, hidden, gain_all[1])
    norm2 = lax.all_gather(norm2_f.astype(bf16), PLANE, axis=0, tiled=True)
    cot = cotangent.astype(f32).reshape(own_rows, width)
    grad_ffn = lax.all_gather((valid * cot).astype(bf16), PLANE, axis=0, tiled=True)
    gate_up = dot(norm2, w_gu)
    units = gate_up.shape[1] // 2
    gate, upper = gate_up[:, :units], gate_up[:, units:]
    sig_gate = sigmoid(gate)
    act = (gate * sig_gate * upper).astype(bf16)
    ffn = dot(act, w_dn).astype(bf16)
    ffn = lax.psum_scatter(ffn, PLANE, scatter_dimension=0, tiled=True)
    mixed = (hidden + valid * ffn.astype(f32)).astype(bf16).reshape(seqs, rows_seq, width)
    grad_act = dot_last(grad_ffn, w_dn)
    grad_gate = grad_act * upper * (sig_gate * (1.0 + gate * (1.0 - sig_gate)))
    grad_upper = grad_act * gate * sig_gate
    grad_gu = jnp.concatenate([grad_gate, grad_upper], 1).astype(bf16)
    grad_norm2 = dot_last(grad_gu, w_gu).astype(bf16)
    grad_norm2 = lax.psum_scatter(grad_norm2, PLANE, scatter_dimension=0, tiled=True)
    grad_hidden_norm, grad_gain2 = norm2_pull(grad_norm2.astype(f32))
    grad_hidden = cot + grad_hidden_norm
    grad_mix = (valid * grad_hidden).astype(bf16).reshape(seqs, rows_seq, width)
    grad_mix = lax.all_gather(grad_mix, TEAM, axis=1, tiled=True).reshape(rows, width)

    grad_w_gu = dot_first(norm2, grad_gu).astype(bf16)
    grad_w_gu = grad_w_gu.reshape(dp, line, plane // dp, held, 2 * line * ffn_block)
    grad_w_gu = grad_w_gu.transpose(1, 0, 2, 3, 4)
    grad_w_gu = lax.psum_scatter(grad_w_gu, LINE, scatter_dimension=0, tiled=True)
    grad_w_gu = lax.all_to_all(
        grad_w_gu.reshape(plane, held, 2 * line * ffn_block), PLANE, 0, 0, tiled=True
    )
    grad_gate_up = (
        grad_w_gu.reshape(dp, plane // dp, held, 2, line, ffn_block)
        .transpose(2, 3, 0, 4, 1, 5)
        .reshape(held, -1)
        .astype(f32)
    )
    grad_w_dn = dot_first(act, grad_ffn).astype(bf16)
    grad_down = lax.psum_scatter(grad_w_dn, LINE, scatter_dimension=0, tiled=True).astype(f32)

    grad_mixed_in = dot_last(grad_mix, w_out)
    grad_o = grad_mixed_in[:, :HD].astype(bf16).reshape(seqs, block_len, HD)
    grad_w_out = dot_first(mixed_in, grad_mix).astype(bf16)
    grad_w_out = lax.psum_scatter(grad_w_out, "dp", scatter_dimension=1, tiled=True)
    if groups > 1:
        grad_w_out = lax.psum(grad_w_out.astype(f32), "g").astype(bf16)
    split = part * attn_rows
    grad_w_out = jnp.concatenate(
        [
            grad_w_out[:split].reshape(part, attn_rows, cut),
            grad_w_out[split:].reshape(part, mamba_rows, cut),
        ],
        axis=1,
    )
    grad_w_out = lax.dynamic_update_slice_in_dim(
        jnp.zeros((seq_size, out_rows, cut), bf16), grad_w_out, (me % ratio) * part, 0
    )
    grad_w_out = lax.all_to_all(grad_w_out, SEQ, 0, 0, tiled=True)
    grad_w_out = grad_w_out.reshape(groups, dp, ratio, out_rows, cut)[0]
    grad_w_out = lax.dynamic_index_in_dim(grad_w_out, my_seq // part, 1, keepdims=False)
    grad_w_out = lax.all_to_all(grad_w_out, "dp", 0, 0, tiled=True)
    grad_w_out = grad_w_out.transpose(1, 0, 2).reshape(out_rows, width).astype(f32)
    grad_attn_out, grad_mamba_out = grad_w_out[:attn_rows], grad_w_out[attn_rows:]

    dq, dk, dv = attend_back(lengths, start, q, k, v, grad_o, logs, span)
    if groups > 1:
        dk = lax.psum_scatter(dk, "g", scatter_dimension=1, tiled=True)
        dv = lax.psum_scatter(dv, "g", scatter_dimension=1, tiled=True)
    dq = rotate_back(dq, cosine, sine).astype(bf16).reshape(rows, HD)
    dk = rotate_back(dk, cosine, sine).astype(bf16).reshape(rows, HD)
    dv = dv.astype(bf16).reshape(rows, HD)
    leave = jnp.zeros((seqs, inner, NS), f32)
    back = functools.partial(core_back, seqs=seqs, heads=heads, span=span)
    grad_gated = grad_mixed_in[:, HD:]
    dzx, dbc, ddt, gconv, ghead, dinit, dfirst = back(
        big, small, grad_gated, y, enter, halos, conv_own, head_own, leave
    )
    if groups > 1:
        leave = entering(decay, dinit, True)
        dzx, dbc, ddt, gconv, ghead, dinit, dfirst = back(
            big, small, grad_gated, y, enter, halos, conv_own, head_own, leave
        )
        padded = jnp.concatenate([jnp.zeros((seqs, KW - 1, wide), f32), dfirst], axis=1)
        rim = sum(
            conv_own[j][None, None] * padded[:, KW - 1 - j : 2 * (KW - 1) - j] for j in range(KW)
        )
        rim = passed_along(rim.astype(bf16), -1).astype(f32)
        rim = jnp.pad(rim, ((0, 0), (block_len - KW + 1, 0), (0, 0))).reshape(rows, wide)
        dzx = jnp.concatenate(
            [dzx[:, :inner], (dzx[:, inner:].astype(f32) + rim[:, :inner]).astype(bf16)], axis=1
        )
        dbc = (dbc.astype(f32) + rim[:, inner:]).astype(bf16)
    dbig = jnp.concatenate([dzx, dq], axis=1)
    dsmall = jnp.concatenate([dbc, dk, dv, ddt], axis=1)
    grad_norm1 = (dot_last(dbig, w_big) + dot_last(dsmall, w_small)).astype(bf16)
    grad_norm1 = lax.psum_scatter(
        grad_norm1.reshape(seqs, block_len, width), TEAM, scatter_dimension=1, tiled=True
    )
    _, norm1_pull = jax.vjp(rms_norm, token_f, gain_all[0])
    grad_token_norm, grad_gain1 = norm1_pull(grad_norm1.astype(f32).reshape(own_rows, width))
    grad_tokens = (
        (grad_hidden + grad_token_norm).astype(bf16).reshape(seqs, rows_seq, width)
    )

    grad_w_big = dot_first(norm1, dbig).astype(bf16)
    grad_w_big = lax.psum_scatter(grad_w_big, SPREAD, scatter_dimension=0, tiled=True)
    grad_w_big = lax.all_to_all(
        grad_w_big.reshape(team, held, 2 * inner + query), TEAM, 0, 0, tiled=True
    )
    grad_w_big = grad_w_big.transpose(1, 0, 2).astype(f32)
    grad_z = grad_w_big[:, :, :inner].reshape(held, MI)
    grad_x = grad_w_big[:, :, inner : 2 * inner].reshape(held, MI)
    grad_query = grad_w_big[:, :, 2 * inner :].reshape(held, -1)

    grad_w_small = dot_first(norm1, dsmall).astype(bf16)
    grad_kv = lax.dynamic_update_slice_in_dim(
        jnp.zeros((width, 2, KV, HD), bf16),
        grad_w_small[:, 2 * NS : 2 * NS + 2 * HD].reshape(width, 2, 1, HD),
        kv_head,
        2,
    ).reshape(width, 2 * KV * HD)
    grad_step = lax.dynamic_update_slice_in_dim(
        jnp.zeros((width, MH), bf16),
        grad_w_small[:, 2 * NS + 2 * HD : 2 * NS + 2 * HD + heads],
        me * heads,
        1,
    )
    grad_pack = jnp.concatenate([grad_w_small[:, : 2 * NS], grad_kv, grad_step], axis=1)
    grad_pack = lax.all_to_all(
        grad_pack.reshape(devices, held, -1), ALL, 0, 0, tiled=True
    )
    grad_pack = jnp.sum(grad_pack.astype(f32), axis=0)
    grad_in = jnp.concatenate([grad_z, grad_x, grad_pack[:, : 2 * NS]], axis=1)
    grad_keyval = grad_pack[:, 2 * NS : 2 * NS + 2 * KV * HD]
    grad_dt = grad_pack[:, 2 * NS + 2 * KV * HD :]

    grad_gains = jnp.stack([grad_gain1, grad_gain2])
    grad_conv = jnp.concatenate(
        [
            lax.dynamic_update_slice_in_dim(
                jnp.zeros((KW + 1, MI), f32), gconv[: KW + 1, :inner], me * inner, 1
            ),
            gconv[: KW + 1, inner:],
        ],
        axis=1,
    )
    grad_head = lax.dynamic_update_slice_in_dim(
        jnp.zeros((3, MH), f32), ghead[:3, :heads], me * heads, 1
    )
    own_conv, own_gain = conv_params.shape[1], gains.shape[1]
    rest = jnp.concatenate(
        [
            grad_conv.reshape(KW + 1, devices, own_conv).transpose(1, 0, 2).reshape(devices, -1),
            grad_gains.reshape(2, devices, own_gain).transpose(1, 0, 2).reshape(devices, -1),
            jnp.broadcast_to(grad_head.reshape(1, -1), (devices, 3 * MH)),
        ],
        axis=1,
    )
    rest = jnp.sum(lax.all_to_all(rest, ALL, 0, 0, tiled=True), axis=0)
    conv_end = (KW + 1) * own_conv
    gain_end = conv_end + 2 * own_gain
    head_total = rest[gain_end:].reshape(3, MH)
    return (
        mixed,
        grad_tokens,
        rest[conv_end:gain_end].reshape(2, own_gain),
        grad_query,
        grad_keyval,
        grad_attn_out,
        grad_in,
        grad_dt,
        rest[:conv_end].reshape(KW + 1, own_conv),
        head_total[:2],
        head_total[2],
        grad_mamba_out,
        grad_gate_up,
        grad_down,
    )


def solution(mesh):
    dp, seq = mesh.shape["dp"], mesh.shape["seq"]
    team = math.gcd(math.gcd(HQ, MH), seq)
    split = Mesh(mesh.devices.reshape(dp, seq // team, team // 2, 2), ALL)
    rows = P(ALL, None)
    cols = P(None, ALL)
    acts = P("dp", SEQ, None)
    return jax.shard_map(
        body,
        mesh=split,
        in_specs=(
            acts, P("dp"), cols, rows, rows, rows, rows, rows, cols, P(), rows, rows, rows, acts,
        ),
        out_specs=(
            acts, acts, cols, rows, rows, rows, rows, rows, cols, P(), P(), rows, rows, rows,
        ),
        check_vma=False,
    )
```

```python
import functools
import math

import jax
import jax.numpy as jnp
from jax import lax
from jax.experimental import pallas as pl
from jax.experimental.pallas import tpu as pltpu
from jax.sharding import Mesh
from jax.sharding import PartitionSpec as P

HQ = 8
KV = 2
HD = 128
MH = 48
MP = 64
NS = 256
KW = 4
MI = MH * MP

epsilon = 1e-05
rope_base = 100000000000.0
neg_big = -1e30
highest = lax.Precision.HIGHEST
bf16 = jnp.bfloat16
f32 = jnp.float32

ALL = ("dp", "g", "z", "c")
TEAM = ("z", "c")
PLANE = ("dp", "c")
LINE = ("g", "z")
SEQ = ("g", "z", "c")
SPREAD = ("dp", "g")


def rms_norm(values, gain):
    return values * lax.rsqrt(jnp.mean(values * values, -1, keepdims=True) + epsilon) * gain


def rope_tables(positions, head_size):
    half = head_size // 2
    freq = jnp.exp(jnp.arange(half, dtype=f32) * (-2.0 * math.log(rope_base) / head_size))
    angle = positions.astype(f32)[:, None] * freq[None, :]
    return (
        jnp.concatenate([jnp.cos(angle), jnp.cos(angle)], -1),
        jnp.concatenate([jnp.sin(angle), jnp.sin(angle)], -1),
    )


def rotate(values, cosine, sine):
    half = values.shape[-1] // 2
    turned = jnp.concatenate([-values[..., half:], values[..., :half]], -1)
    return values * cosine + turned * sine


def rotate_back(grads, cosine, sine):
    half = grads.shape[-1] // 2
    scaled = grads * sine
    return grads * cosine + jnp.concatenate([scaled[..., half:], -scaled[..., :half]], -1)


def dot(left, right, precision=None):
    return jnp.dot(left, right, preferred_element_type=f32, precision=precision)


def dot_first(left, right, precision=None):
    return lax.dot_general(
        left, right, (((0,), (0,)), ((), ())), preferred_element_type=f32, precision=precision
    )


def dot_last(left, right, precision=None):
    return lax.dot_general(
        left, right, (((1,), (1,)), ((), ())), preferred_element_type=f32, precision=precision
    )


def sigmoid(v):
    return 1.0 / (1.0 + jnp.exp(-v))


def softplus(v):
    return jnp.maximum(v, 0.0) + jnp.log(1.0 + jnp.exp(-jnp.abs(v)))


def cost(rows, gigaflops, arrays):
    return pl.CostEstimate(
        flops=int(rows * gigaflops * 1e9 / 2048),
        bytes_accessed=sum(a.size * a.dtype.itemsize for a in arrays),
        transcendentals=0,
    )


def params(count):
    return pltpu.CompilerParams(
        dimension_semantics=("arbitrary",) * count, vmem_limit_bytes=48 * 1024 * 1024
    )


def after(value, *others):
    return lax.optimization_barrier((value, *others))[0]


def assemble(scalars, sources, shapes, plan, count, name):
    def kernel(scalar_ref, *refs):
        sems = refs[-1]
        plan(scalar_ref, refs[: len(sources)], refs[len(sources) : -1], sems)

    anywhere = pl.BlockSpec(memory_space=pl.ANY)
    return pl.pallas_call(
        kernel,
        in_specs=[pl.BlockSpec(memory_space=pltpu.SMEM)] + [anywhere] * len(sources),
        out_specs=[pl.BlockSpec(memory_space=pltpu.VMEM)] * len(shapes),
        out_shape=[jax.ShapeDtypeStruct(shape, bf16) for shape in shapes],
        scratch_shapes=[pltpu.SemaphoreType.DMA((count,))],
        compiler_params=pltpu.CompilerParams(vmem_limit_bytes=48 * 1024 * 1024),
        cost_estimate=pl.CostEstimate(
            flops=0, bytes_accessed=4 * sum(math.prod(shape) for shape in shapes), transcendentals=0
        ),
        name=name,
    )(jnp.stack([jnp.asarray(v, jnp.int32) for v in scalars]), *sources)


def run_copies(pairs, sems):
    copies = [pltpu.make_async_copy(a, b, sems.at[i]) for i, (a, b) in enumerate(pairs)]
    for copy in copies:
        copy.start()
    for copy in copies:
        copy.wait()


def join_weights(blocks, others, inner, key_at, shared, kv_head):
    peers, here = lax.axis_size("dp"), lax.axis_index("dp")
    size = sum(part.shape[0] for part, k, _ in blocks if k == 0)
    width = size * peers
    own = inner + key_at
    keys_size = 2 * KV * HD
    many = len(blocks)

    def plan(scalar_ref, sources, outs, sems):
        early, late, rest = outs

        def pairs(turned):
            moves = []
            for i, (part, k, first) in enumerate(blocks):
                rows = part.shape[0]
                at = pl.ds(pl.multiple_of(scalar_ref[k] * size + first, rows), rows)
                source = sources[i]
                near, far = source.at[:, pl.ds(own, shared)], sources[many + i]
                steps, keys = (far, near) if turned else (near, far)
                moves.append((source.at[:, pl.ds(0, key_at)], early.at[at, pl.ds(0, key_at)]))
                moves.append((source.at[:, pl.ds(key_at, inner)], late.at[at, pl.ds(0, inner)]))
                moves.append((steps, late.at[at, pl.ds(inner, shared)]))
                for j in range(2):
                    lane = (j * KV + scalar_ref[peers]) * HD
                    if not turned:
                        keys_at = pl.multiple_of(lane, HD)
                        key_view = keys.at[:, pl.ds(keys_at, HD)]
                    else:
                        key_view = source.at[:, pl.ds(pl.multiple_of(own + lane, HD), HD)]
                    moves.append((key_view, early.at[at, pl.ds(key_at + j * HD, HD)]))
                tail = far if not turned else source
                tail_at = keys_size if not turned else own + keys_size
                moves.append((tail.at[:, pl.ds(tail_at, 128)], rest.at[at, :]))
            return moves

        @pl.when(scalar_ref[peers + 1] == 0)
        def _():
            run_copies(pairs(False), sems)

        @pl.when(scalar_ref[peers + 1] != 0)
        def _():
            run_copies(pairs(True), sems)

    scalars = [here ^ k for k in range(peers)] + [kv_head, lax.axis_index("c")]
    shapes = [(width, key_at + 2 * HD), (width, inner + shared), (width, shared - keys_size)]
    sources = [part for part, _, _ in blocks] + others
    return assemble(scalars, sources, shapes, plan, 6 * many, "join_weights")


def join_hidden(gathered, count, held, dp, width):
    line, _, columns = gathered.shape
    low = count * held
    rows = (gathered.shape[1] - low) * columns // width
    folds = width // columns

    def plan(scalar_ref, sources, outs, sems):
        moves = [
            (
                sources[0].at[:, pl.ds(i * held, held)],
                outs[0].at[scalar_ref[i], :, scalar_ref[count + i]],
            )
            for i in range(count)
        ]
        for i in range(folds):
            moves.append(
                (
                    sources[0].at[:, pl.ds(low + i * rows, rows)],
                    outs[1].at[:, :, pl.ds(i * columns, columns)],
                )
            )
        run_copies(moves, sems)

    near, core = lax.axis_index("dp"), lax.axis_index("c")
    scalars = [near ^ (i % dp) for i in range(count)] + [core ^ (i // dp) for i in range(count)]
    shapes = [(dp, line, count // dp, held, columns), (line, rows, width)]
    return assemble(scalars, [gathered], shapes, plan, count + folds, "join_hidden")


def join_rows(slots, place):
    count, rows, width = len(slots), *slots[0].shape

    def plan(scalar_ref, sources, outs, sems):
        run_copies([(sources[k], outs[0].at[scalar_ref[k]]) for k in range(count)], sems)

    scalars = [place ^ k for k in range(count)]
    whole = assemble(scalars, slots, [(count, rows, width)], plan, count, "join_rows")[0]
    return whole.reshape(count * rows, width)


def join_columns(pieces):
    peers, here = lax.axis_size("dp"), lax.axis_index("dp")
    rows, cut = pieces[0].shape

    def plan(scalar_ref, sources, outs, sems):
        run_copies(
            [
                (sources[k], outs[0].at[:, pl.ds(pl.multiple_of(scalar_ref[k] * cut, cut), cut)])
                for k in range(peers)
            ],
            sems,
        )

    scalars = [here ^ k for k in range(peers)]
    return assemble(scalars, pieces, [(rows, cut * peers)], plan, peers, "join_columns")[0]


def join_out(blocks, place, attn_rows, mamba_rows):
    peers, here = lax.axis_size("dp"), lax.axis_index("dp")
    parts, rows, cut = blocks[0].shape

    def plan(scalar_ref, sources, outs, sems):
        moves = []
        for k in range(peers):
            lane = pl.ds(pl.multiple_of(scalar_ref[k] * cut, cut), cut)
            for i in range(parts):
                at = scalar_ref[peers + i]
                low = pl.multiple_of(at * mamba_rows, 16)
                high = pl.multiple_of(parts * mamba_rows + at * attn_rows, 16)
                moves.append(
                    (
                        sources[k].at[i, pl.ds(attn_rows, mamba_rows)],
                        outs[0].at[pl.ds(low, mamba_rows), lane],
                    )
                )
                moves.append(
                    (
                        sources[k].at[i, pl.ds(0, attn_rows)],
                        outs[0].at[pl.ds(high, attn_rows), lane],
                    )
                )
        run_copies(moves, sems)

    scalars = [here ^ k for k in range(peers)] + [place ^ i for i in range(parts)]
    shape = (parts * rows, cut * peers)
    return assemble(scalars, blocks, [shape], plan, 2 * peers * parts, "join_out")[0]


def swap(block, axis, distance):
    return lax.ppermute(block, axis, [(i, i ^ distance) for i in range(lax.axis_size(axis))])


def gather_plane(block):
    near = [block] + [swap(block, "dp", k) for k in range(1, lax.axis_size("dp"))]
    return jnp.concatenate(near + [swap(piece, "c", 1) for piece in near], axis=0)


def scatter_core(partial):
    half = partial.shape[0] // 2
    near = partial[:half].astype(f32) + swap(partial[half:], "c", 1).astype(f32)
    return near.astype(bf16)


def scatter_near(near):
    near = jnp.split(near, lax.axis_size("dp"), axis=0)
    return sum(
        (swap(near[k], "dp", k) if k else near[k]).astype(f32) for k in range(len(near))
    )


def scatter_plane(partial):
    return scatter_near(scatter_core(partial))


def from_dp(block):
    return [block] + [swap(block, "dp", k) for k in range(1, lax.axis_size("dp"))]


def parts_dp(block):
    if lax.axis_size("dp") != 4:
        return [(part, k, 0) for k, part in enumerate(from_dp(block))]
    half = block.shape[0] // 2
    one, two = swap(block, "dp", 1), swap(block, "dp", 2)
    top, bottom = swap(one[:half], "dp", 2), swap(two[half:], "dp", 1)
    return [(block, 0, 0), (one, 1, 0), (two, 2, 0), (top, 3, 0), (bottom, 3, half)]


def cuts_dp(partial, axis):
    peers, here = lax.axis_size("dp"), lax.axis_index("dp")
    size = partial.shape[axis] // peers
    return [lax.dynamic_slice_in_dim(partial, (here ^ k) * size, size, axis) for k in range(peers)]


def sum_cuts(cuts):
    return sum((swap(cut, "dp", k) if k else cut).astype(f32) for k, cut in enumerate(cuts))


def scatter_dp(partial, axis):
    return sum_cuts(cuts_dp(partial, axis))


def attend_mask(length_ref, start_ref, seq, block, width, first):
    qpos = start_ref[0] + first + lax.broadcasted_iota(jnp.int32, (block, width), 0)
    kpos = lax.broadcasted_iota(jnp.int32, (block, width), 1)
    return (kpos <= qpos) & (kpos < length_ref[seq])


def attend_fore_kernel(
    length_ref, start_ref, q_ref, k_ref, v_ref, o_ref, log_ref, *, scale, block, seq
):
    at = pl.program_id(0)
    keys = k_ref[0]
    scores = dot_last(q_ref[0], keys) * scale
    allowed = attend_mask(length_ref, start_ref, seq, block, keys.shape[0], at * block)
    scores = jnp.where(allowed, scores, neg_big)
    top = jnp.max(scores, -1, keepdims=True)
    expo = jnp.exp(scores - top)
    total = jnp.sum(expo, -1, keepdims=True)
    prob = (expo * (1.0 / total)).astype(bf16)
    o_ref[0] = dot(prob, v_ref[0]).astype(bf16)
    log_ref[0] = jnp.broadcast_to(top + jnp.log(total), log_ref.shape[1:])


def attend_fore(length, start, q, k, v, block, seq):
    _, rows, width = q.shape
    kernel = functools.partial(
        attend_fore_kernel, scale=1.0 / math.sqrt(HD), block=block, seq=seq
    )
    qspec = pl.BlockSpec((1, block, width), lambda i: (seq, i, 0))
    ospec = pl.BlockSpec((1, block, width), lambda i: (0, i, 0))
    kspec = pl.BlockSpec((1, k.shape[1], width), lambda i: (seq, 0, 0))
    smem = pl.BlockSpec(memory_space=pltpu.SMEM)
    return pl.pallas_call(
        kernel,
        grid=(rows // block,),
        in_specs=[smem, smem, qspec, kspec, kspec],
        out_specs=[ospec, ospec],
        out_shape=[
            jax.ShapeDtypeStruct((1, rows, width), bf16),
            jax.ShapeDtypeStruct((1, rows, width), f32),
        ],
        compiler_params=params(1),
        cost_estimate=cost(rows, 7, (q, k, v)),
        name="attend_fore",
    )(length, start, q, k, v)


def attend_back_kernel(
    length_ref, start_ref, q_ref, k_ref, v_ref, do_ref, log_ref, dq_ref, dk_ref, dv_ref,
    *, scale, block, seq,
):
    at = pl.program_id(0)

    @pl.when(at == 0)
    def _():
        dk_ref[...] = jnp.zeros_like(dk_ref)
        dv_ref[...] = jnp.zeros_like(dv_ref)

    keys = k_ref[0]
    queries = q_ref[0]
    grad_out = do_ref[0].astype(bf16)
    scores = dot_last(queries, keys) * scale
    allowed = attend_mask(length_ref, start_ref, seq, block, keys.shape[0], at * block)
    scores = jnp.where(allowed, scores, neg_big)
    prob = jnp.exp(scores - log_ref[0][:, :1])
    grad_prob = dot_last(grad_out, v_ref[0])
    centre = jnp.sum(prob * grad_prob, -1, keepdims=True)
    grad_score = (prob * (grad_prob - centre)).astype(bf16)
    dq_ref[0] = dot(grad_score, keys) * scale
    dk_ref[0] += dot_first(grad_score, queries) * scale
    dv_ref[0] += dot_first(prob.astype(bf16), grad_out)


def attend_back(length, start, q, k, v, grad_out, logs, block, seq):
    _, rows, width = q.shape
    out_at = grad_out.shape[1] // width - 1
    kernel = functools.partial(
        attend_back_kernel, scale=1.0 / math.sqrt(HD), block=block, seq=seq
    )
    qspec = pl.BlockSpec((1, block, width), lambda i: (seq, i, 0))
    ospec = pl.BlockSpec((1, block, width), lambda i: (0, i, 0))
    kspec = pl.BlockSpec((1, k.shape[1], width), lambda i: (seq, 0, 0))
    gspec = pl.BlockSpec((1, k.shape[1], width), lambda i: (0, 0, 0))
    smem = pl.BlockSpec(memory_space=pltpu.SMEM)
    return pl.pallas_call(
        kernel,
        grid=(rows // block,),
        in_specs=[
            smem,
            smem,
            qspec,
            kspec,
            kspec,
            pl.BlockSpec((1, block, width), lambda i: (0, i, out_at)),
            ospec,
        ],
        out_specs=[ospec, gspec, gspec],
        out_shape=[
            jax.ShapeDtypeStruct((1, rows, width), f32),
            jax.ShapeDtypeStruct((1, *k.shape[1:]), f32),
            jax.ShapeDtypeStruct((1, *k.shape[1:]), f32),
        ],
        compiler_params=params(1),
        cost_estimate=cost(rows, 11, (q, k, v, logs)),
        name="attend_back",
    )(length, start, q, k, v, grad_out[None], logs)


def head_spread(heads):
    row = lax.broadcasted_iota(jnp.int32, (128, heads * MP), 0)
    col = lax.broadcasted_iota(jnp.int32, (128, heads * MP), 1)
    return (row == col // MP).astype(f32)


def triangle(span):
    row = lax.broadcasted_iota(jnp.int32, (span, span), 0)
    col = lax.broadcasted_iota(jnp.int32, (span, span), 1)
    return row >= col


def conv_pre(ext_ref, conv_ref, span):
    total = conv_ref[KW : KW + 1, :]
    for k in range(KW):
        total = total + conv_ref[k : k + 1, :] * ext_ref[pl.ds(8 - (KW - 1) + k, span), :]
    return total


def core_fore_kernel(
    turn_ref, x_ref, bc_ref, z_ref, dt_ref, halo_ref, conv_ref, head_ref, init_ref,
    gated_ref, y_ref, enter_ref, final_ref, decay_ref,
    ext, state, total, *, heads, span,
):
    inner = heads * MP
    at = pl.program_id(0)

    @pl.when(at == 0)
    def _():
        ext[0:8, :] = halo_ref[0]
        state[...] = init_ref[0]
        total[...] = jnp.zeros_like(total)

    ext[8:, :inner] = x_ref[...]
    ext[8:, inner:] = bc_ref[...]
    pre = conv_pre(ext, conv_ref, span)
    ext[0:8, :] = ext[span : span + 8, :]
    cv = pre * sigmoid(pre)
    xs = cv[:, :inner]
    bmat = cv[:, inner : inner + NS].astype(bf16)
    cmat = cv[:, inner + NS :].astype(bf16)
    spread = head_spread(heads)
    lower = triangle(span)
    step = softplus(pltpu.roll(dt_ref[...], 128 - turn_ref[0], 1) + head_ref[0:1, :])
    decay_log = -jnp.exp(head_ref[1:2, :]) * step
    cum = dot(lower.astype(f32), decay_log, highest)
    cum_t = cum.T
    step_t = step.T
    last = cum[span - 1 : span, :]
    enter = state[...]
    enter_ref[0, 0] = enter
    pair = dot_last(cmat, bmat)
    xb = xs.astype(bf16)
    parts = []
    for h in range(heads):
        diff = cum[:, h : h + 1] - cum_t[h : h + 1, :]
        decay = jnp.exp(jnp.where(lower, diff, neg_big))
        mixing = (pair * decay * step_t[h : h + 1, :]).astype(bf16)
        parts.append(dot(mixing, xb[:, h * MP : (h + 1) * MP]))
    y = jnp.concatenate(parts, axis=1)
    y = y + dot_last(cmat, enter.astype(bf16)) * dot(jnp.exp(cum), spread, highest)
    y = y + xs * dot(jnp.broadcast_to(head_ref[2:3, :], (8, 128)), spread, highest)[0:1, :]
    tail = dot(jnp.exp(last - cum) * step, spread, highest)
    keep = jnp.broadcast_to(jnp.exp(cum_t[:, span - 1 : span]), (128, NS))
    new_state = dot_first(spread, keep, highest) * enter + dot_first((xs * tail).astype(bf16), bmat)
    state[...] = new_state
    final_ref[0] = new_state
    total[...] = total[...] + last
    decay_ref[0] = total[...]
    z = z_ref[...]
    y_ref[...] = y
    gated_ref[...] = (y * (z * sigmoid(z))).astype(bf16)


def core_fore(turn, early, late, halo, conv, head, init, seq, rows, heads, span):
    inner = heads * MP
    wide = inner + 2 * NS
    count = rows // span
    first = seq * count

    def block(width, at):
        return pl.BlockSpec((span, width), lambda i: (first + i, at))

    def whole(*shape):
        return pl.BlockSpec(shape, lambda i: (0,) * len(shape))

    out = pl.BlockSpec((span, inner), lambda i: (i, 0))
    return pl.pallas_call(
        functools.partial(core_fore_kernel, heads=heads, span=span),
        grid=(count,),
        in_specs=[
            pl.BlockSpec(memory_space=pltpu.SMEM),
            block(inner, 0),
            block(2 * NS, (inner + 128) // (2 * NS)),
            block(inner, 0),
            block(128, inner // 128),
            whole(1, 8, wide),
            whole(8, wide),
            whole(8, 128),
            whole(1, inner, NS),
        ],
        out_specs=[
            out,
            out,
            pl.BlockSpec((1, 1, inner, NS), lambda i: (0, i, 0, 0)),
            whole(1, inner, NS),
            whole(1, 8, 128),
        ],
        out_shape=[
            jax.ShapeDtypeStruct((rows, inner), bf16),
            jax.ShapeDtypeStruct((rows, inner), f32),
            jax.ShapeDtypeStruct((1, count, inner, NS), f32),
            jax.ShapeDtypeStruct((1, inner, NS), f32),
            jax.ShapeDtypeStruct((1, 8, 128), f32),
        ],
        scratch_shapes=[
            pltpu.VMEM((span + 8, wide), f32),
            pltpu.VMEM((inner, NS), f32),
            pltpu.VMEM((8, 128), f32),
        ],
        compiler_params=params(1),
        cost_estimate=cost(rows, 26, (late, init)),
        name="core_fore",
    )(turn, late, late, early, late, halo, conv, head, init)


def core_back_kernel(
    turn_ref, x_ref, bc_ref, z_ref, dt_ref, dg_ref, enter_ref, halo_ref, conv_ref, head_ref, exit_ref,
    dlate_ref, gconv_ref, ghead_ref, dinit_ref, dfirst_ref,
    ext, dext, dstate, *, heads, span,
):
    inner = heads * MP
    at = pl.program_id(0)

    @pl.when(at == 0)
    def _():
        gconv_ref[...] = jnp.zeros_like(gconv_ref)
        ghead_ref[...] = jnp.zeros_like(ghead_ref)

    @pl.when(at == 0)
    def _():
        dext[span:, :] = jnp.zeros((8, dext.shape[1]), f32)
        dstate[...] = exit_ref[0]

    ext[0:8, :] = halo_ref[0, 0]
    ext[8:, :inner] = x_ref[...]
    ext[8:, inner:] = bc_ref[...]
    pre = conv_pre(ext, conv_ref, span)
    gate = sigmoid(pre)
    cv = pre * gate
    xs = cv[:, :inner]
    bmat = cv[:, inner : inner + NS].astype(bf16)
    cmat = cv[:, inner + NS :].astype(bf16)
    xb = xs.astype(bf16)
    z = z_ref[...]
    dy = dg_ref[...] * (z * sigmoid(z))
    dyb = dy.astype(bf16)
    spread = head_spread(heads)
    lower = triangle(span)
    raw = pltpu.roll(dt_ref[...], 128 - turn_ref[0], 1) + head_ref[0:1, :]
    step = softplus(raw)
    rate = -jnp.exp(head_ref[1:2, :])
    decay_log = rate * step
    cum = dot(lower.astype(f32), decay_log, highest)
    cum_t = cum.T
    step_t = step.T
    last = cum[span - 1 : span, :]
    enter = enter_ref[0, 0]
    leave = dstate[...]
    pair = dot_last(cmat, bmat)
    dpair = jnp.zeros((span, span), f32)
    lane = lax.broadcasted_iota(jnp.int32, (span, 128), 1)
    line = lax.broadcasted_iota(jnp.int32, (128, span), 0)
    row_sums = jnp.zeros((span, 128), f32)
    col_sums = jnp.zeros((128, span), f32)
    parts = []
    for h in range(heads):
        diff = cum[:, h : h + 1] - cum_t[h : h + 1, :]
        decay = jnp.exp(jnp.where(lower, diff, neg_big))
        now = step_t[h : h + 1, :]
        cut = slice(h * MP, (h + 1) * MP)
        dmix = dot_last(dyb[:, cut], xb[:, cut]) * decay
        both = dmix * pair
        dmix_now = dmix * now
        dpair = dpair + dmix_now
        row_sums = jnp.where(lane == h, jnp.sum(both * now, 1, keepdims=True), row_sums)
        col_sums = jnp.where(line == h, jnp.sum(both, 0, keepdims=True), col_sums)
        mixing = (pair * decay * now).astype(bf16)
        parts.append(dot_first(mixing, dyb[:, cut]))
    dxs = jnp.concatenate(parts, axis=1)
    dstep = col_sums.T
    dcum = row_sums - dstep * step
    dpb = dpair.astype(bf16)
    dcm = dot(dpb, bmat)
    dbm = dot_first(dpb, cmat)
    grown = dot(jnp.exp(cum), spread, highest)
    enter_b = enter.astype(bf16)
    leave_b = leave.astype(bf16)
    dgrown = (dy * grown).astype(bf16)
    dcum = dcum + dot_last(dy * dot_last(cmat, enter_b) * grown, spread, highest)
    dcm = dcm + dot(dgrown, enter_b)
    fade = jnp.exp(last - cum)
    tail = dot(fade * step, spread, highest)
    into = dot_last(bmat, leave_b)
    dxs = dxs + into * tail
    owed = dot_last(xs * into, spread, highest) * fade
    dstep = dstep + owed
    owed = owed * step
    dcum = dcum - owed
    dbm = dbm + dot((xs * tail).astype(bf16), leave_b)
    held = dot(spread, enter * leave, highest)
    held = dot_last(jnp.ones((8, NS), f32), held, highest)[0:1, :]
    dlast = jnp.sum(owed, 0, keepdims=True) + jnp.exp(last) * held
    keep = jnp.broadcast_to(jnp.exp(cum_t[:, span - 1 : span]), (128, NS))
    new_dstate = dot_first(spread, keep, highest) * leave + dot_first(dgrown, cmat)
    dstate[...] = new_dstate
    dinit_ref[0] = new_dstate
    dlog = dot_first(lower.astype(f32), dcum, highest) + dlast
    dstep = dstep + dlog * rate
    ddt = dstep * sigmoid(raw)
    dlate_ref[:, inner : inner + 128] = pltpu.roll(ddt, turn_ref[0], 1).astype(bf16)
    skip = dot(jnp.broadcast_to(head_ref[2:3, :], (8, 128)), spread, highest)[0:1, :]
    dxs = dxs + skip * dy
    ghead_ref[0:1, :] += jnp.sum(ddt, 0, keepdims=True)
    ghead_ref[1:2, :] += jnp.sum(dlog * decay_log, 0, keepdims=True)
    ghead_ref[2:3, :] += jnp.sum(dot_last(dy * xs, spread, highest), 0, keepdims=True)
    slope = gate * (1.0 + pre * (1.0 - gate))
    dpre = jnp.concatenate([dxs, dbm, dcm], axis=1) * slope
    dext[0:span, :] = dpre
    gconv_ref[KW : KW + 1, :] += jnp.sum(dpre, 0, keepdims=True)
    dxbc = jnp.zeros_like(dpre)
    for k in range(KW):
        dxbc = dxbc + conv_ref[k : k + 1, :] * dext[pl.ds(KW - 1 - k, span), :]
        gconv_ref[k : k + 1, :] += jnp.sum(
            dpre * ext[pl.ds(8 - (KW - 1) + k, span), :], 0, keepdims=True
        )
    dlate_ref[:, :inner] = dxbc[:, :inner].astype(bf16)
    dlate_ref[:, inner + 128 :] = dxbc[:, inner:].astype(bf16)
    dext[span:, :] = dext[0:8, :]
    dfirst_ref[0] = dext[0:8, :]


def core_back(turn, early, late, dmixed, enter, halos, conv, head, leave, seq, heads, span):
    rows = dmixed.shape[0]
    inner = heads * MP
    wide = inner + 2 * NS
    count = rows // span
    first = seq * count

    def block(width, at):
        return pl.BlockSpec((span, width), lambda i: (first + count - 1 - i, at))

    def own(width):
        return pl.BlockSpec((span, width), lambda i: (count - 1 - i, 0))

    def whole(*shape):
        return pl.BlockSpec(shape, lambda i: (0,) * len(shape))

    return pl.pallas_call(
        functools.partial(core_back_kernel, heads=heads, span=span),
        grid=(count,),
        in_specs=[
            pl.BlockSpec(memory_space=pltpu.SMEM),
            block(inner, 0),
            block(2 * NS, (inner + 128) // (2 * NS)),
            block(inner, 0),
            block(128, inner // 128),
            own(inner),
            pl.BlockSpec((1, 1, inner, NS), lambda i: (0, count - 1 - i, 0, 0)),
            pl.BlockSpec((1, 1, 8, wide), lambda i: (0, count - 1 - i, 0, 0)),
            whole(8, wide),
            whole(8, 128),
            whole(1, inner, NS),
        ],
        out_specs=[
            own(late.shape[1]),
            whole(8, wide),
            whole(8, 128),
            whole(1, inner, NS),
            whole(1, 8, wide),
        ],
        out_shape=[
            jax.ShapeDtypeStruct((rows, late.shape[1]), bf16),
            jax.ShapeDtypeStruct((8, wide), f32),
            jax.ShapeDtypeStruct((8, 128), f32),
            jax.ShapeDtypeStruct((1, inner, NS), f32),
            jax.ShapeDtypeStruct((1, 8, wide), f32),
        ],
        scratch_shapes=[
            pltpu.VMEM((span + 8, wide), f32),
            pltpu.VMEM((span + 8, wide), f32),
            pltpu.VMEM((inner, NS), f32),
        ],
        compiler_params=params(1),
        cost_estimate=cost(rows, 60, (late, enter)),
        name="core_back",
    )(turn, late, late, early, late, dmixed, enter, halos, conv, head, leave)


def passed_along(block, distance):
    devices = range(lax.axis_size("g"))
    route = [(i - distance, i) for i in devices if i - distance in devices]
    return lax.ppermute(block, "g", route)


def entering(decay, local, reverse):
    peers, here = lax.axis_size("g"), lax.axis_index("g")
    decays = lax.all_gather(decay, "g")
    locals_ = lax.all_gather(local.astype(bf16), "g")
    state = jnp.zeros_like(local)
    for k in range(peers):
        at = peers - 1 - k if reverse else k
        reached = (at > here) if reverse else (at < here)
        state = jnp.where(reached, decays[at] * state + locals_[at].astype(f32), state)
    return state


def head_decay(decay_log, heads):
    keep = jnp.exp(decay_log[:, 0, :heads])
    return jnp.repeat(keep, MP, axis=1)[:, :, None]


def body(
    tokens, lengths, gains, w_query, w_keyval, w_attn_out, w_in, w_dt, conv_params, head_params,
    w_mamba_out, w_gate_up, w_down, cotangent,
):
    seqs, rows_seq, width = tokens.shape
    dp, groups, team = lax.axis_size("dp"), lax.axis_size("g"), lax.axis_size(TEAM)
    devices, line, plane = lax.axis_size(ALL), lax.axis_size(LINE), lax.axis_size(PLANE)
    seq_size = groups * team
    me = lax.axis_index(TEAM)
    heads = MH // team
    inner = heads * MP
    query = HQ * HD // team
    block_len = rows_seq * team
    rows = seqs * block_len
    held = w_query.shape[0]
    span = math.gcd(256, block_len)
    start = (lax.axis_index("g") * block_len).astype(jnp.int32).reshape(1)
    kv_head = me * (HQ // team) * KV // HQ

    core = lax.axis_index("c")
    conv_flat = conv_params.reshape(-1)
    conv_cols = -(-conv_flat.shape[0] // held)
    conv_flat = jnp.pad(conv_flat, (0, conv_cols * held - conv_flat.shape[0]))
    shared = 128 + 2 * NS
    keys_size = 2 * KV * HD
    packed = jnp.concatenate(
        [
            jnp.pad(w_dt, ((0, 0), (0, 128 - MH))),
            w_in[:, 2 * MI :],
            w_keyval,
            gains.T,
            conv_flat.reshape(held, conv_cols),
            jnp.zeros((held, shared - keys_size - 2 - conv_cols), bf16),
        ],
        axis=1,
    )
    w_big = jnp.concatenate(
        [
            w_in[:, :MI].reshape(held, team, inner),
            w_query.reshape(held, team, query),
            w_in[:, MI : 2 * MI].reshape(held, team, inner),
            jnp.tile(packed.reshape(held, 2, shared), (1, team // 2, 1)),
        ],
        axis=2,
    ).transpose(1, 0, 2)
    slots = []
    for k in range(team):
        slot = lax.dynamic_index_in_dim(w_big, me ^ k, 0, keepdims=False)
        route = [(i, i ^ k) for i in range(team)]
        slots.append(lax.ppermute(slot, TEAM, route) if k else slot)
    w_big = join_rows(slots, me)
    if groups > 1:
        w_big = lax.all_gather(w_big, "g", axis=0, tiled=True)
    block_tokens = lax.all_gather(after(tokens, w_big), TEAM, axis=1, tiled=True)
    block_tokens = block_tokens.reshape(rows, width)
    ffn_block = w_down.shape[0]
    w_gu = w_gate_up.reshape(held, 2, dp, line, plane // dp, ffn_block).transpose(4, 2, 0, 1, 3, 5)
    w_gu = w_gu.reshape(plane // dp, dp, held, 2 * line * ffn_block)
    mine_dp = lax.axis_index("dp")
    slots = []
    for j in range(2):
        for k in range(dp):
            slot = lax.dynamic_slice(
                w_gu, (core ^ j, mine_dp ^ k, 0, 0), (1, 1, held, 2 * line * ffn_block)
            )[0, 0]
            if j or k:
                route = [(2 * a + b, 2 * (a ^ k) + (b ^ j)) for a in range(dp) for b in range(2)]
                slot = lax.ppermute(slot, PLANE, route)
            slots.append(slot)
    w_gu = jnp.stack(slots)
    ratio = team // dp
    part = seq_size // ratio
    attn_rows, mamba_rows = w_attn_out.shape[0], w_mamba_out.shape[0]
    out_rows = attn_rows + mamba_rows
    cut = width // dp
    w_out = jnp.concatenate([w_attn_out, w_mamba_out], axis=0)
    w_out = w_out.reshape(out_rows, dp, cut)
    quarters = []
    for k in range(dp):
        quarter = lax.dynamic_index_in_dim(w_out, mine_dp ^ k, 1, keepdims=False)
        quarters.append(swap(quarter, "dp", k) if k else quarter)
    w_out = jnp.stack(quarters)
    positions = start[0] + jnp.arange(block_len, dtype=jnp.int32)
    cosine, sine = rope_tables(positions, HD)
    w_big, w_gu, w_out, cosine, sine = lax.optimization_barrier(
        (w_big, w_gu, w_out, cosine, sine)
    )
    blocks = parts_dp(w_big)
    key_at = inner + query
    others = [swap(part[:, inner + key_at :], "c", 1) for part, _, _ in blocks]
    w_early, w_late, rest = join_weights(blocks, others, inner, key_at, shared, kv_head)
    gain_all = rest[:, :2].astype(f32).T
    conv_all = rest[:, 2 : 2 + conv_cols]
    conv_all = conv_all.reshape(devices, held * conv_cols)[:, : conv_params.size]
    conv_all = (
        conv_all.reshape(devices, KW + 1, -1).transpose(1, 0, 2).reshape(KW + 1, -1).astype(f32)
    )
    conv_own = jnp.concatenate(
        [lax.dynamic_slice_in_dim(conv_all, me * inner, inner, 1), conv_all[:, MI:]], axis=1
    )
    conv_own = jnp.pad(conv_own, ((0, 8 - KW - 1), (0, 0)))
    head_own = jnp.pad(
        lax.dynamic_slice_in_dim(head_params, me * heads, heads, 1), ((0, 5), (0, 128 - heads))
    )
    turn = (me * heads).astype(jnp.int32).reshape(1)
    block_tokens, w_gu, w_early, w_late, gain_all = lax.optimization_barrier(
        (block_tokens, w_gu, w_early, w_late, gain_all)
    )
    columns = w_gu.shape[-1]
    folded = [w_down[:, i * columns : (i + 1) * columns] for i in range(width // columns)]
    w_ffn = jnp.concatenate([w_gu.reshape(-1, columns), *folded], axis=0)
    w_ffn = lax.all_gather(w_ffn, LINE, axis=0, tiled=False).reshape(line, -1, columns)
    my_seq = lax.axis_index(SEQ)
    w_out = after(w_out, block_tokens)
    if part == dp and groups == 1:
        parts = []
        for k in range(part):
            block = lax.dynamic_index_in_dim(w_out, mine_dp ^ (me % part) ^ k, 0, keepdims=False)
            route = [(i, ratio * ((i % part) ^ k) + i // part) for i in range(team)]
            parts.append(lax.ppermute(block, TEAM, route))
        w_out = jnp.stack(parts)
    else:
        order = mine_dp ^ jnp.arange(dp)
        w_out = jnp.take(w_out, order, axis=0)
        mine = (jnp.arange(ratio) == my_seq // part)[None, :, None, None]
        w_out = jnp.where(mine, w_out[:, None], jnp.zeros((), bf16))
        w_out = jnp.broadcast_to(
            w_out.reshape(1, team, out_rows, cut), (groups, team, out_rows, cut)
        ).reshape(-1, out_rows, cut)
        w_out = lax.all_to_all(w_out, SEQ, 0, 0, tiled=True)
        w_out = lax.dynamic_slice_in_dim(w_out, (me % ratio) * part, part, 0)
        w_out = jnp.concatenate(
            [w_out[:, attn_rows:].reshape(-1, cut), w_out[:, :attn_rows].reshape(-1, cut)], axis=0
        )

    own_positions = my_seq * rows_seq + jnp.arange(rows_seq, dtype=jnp.int32)
    valid = (own_positions[None, :] < lengths[:, None]).astype(f32)[:, :, None]
    cot = cotangent.astype(f32)

    norm1 = rms_norm(block_tokens.astype(f32), gain_all[0]).astype(bf16)
    early = dot(norm1, w_early)
    late = dot(norm1, w_late)
    early, late, w_out = lax.optimization_barrier((early, late, w_out))
    if w_out.ndim == 3:
        w_out = join_out(from_dp(w_out), me // ratio, attn_rows, mamba_rows)
    else:
        w_out = join_columns(from_dp(w_out))
    q = rotate(early[:, inner:key_at].reshape(seqs, block_len, HD), cosine, sine).astype(bf16)
    k = rotate(
        early[:, key_at : key_at + HD].reshape(seqs, block_len, HD), cosine, sine
    ).astype(bf16)
    v = early[:, key_at + HD :].reshape(seqs, block_len, HD).astype(bf16)
    if groups > 1:
        k = lax.all_gather(k, "g", axis=1, tiled=True)
        v = lax.all_gather(v, "g", axis=1, tiled=True)
    wide = inner + 2 * NS
    ends = late.reshape(seqs, block_len // span, span, -1)[:, :, span - 8 :, :]
    ends = jnp.concatenate([ends[..., :inner], ends[..., inner + 128 :]], axis=-1)
    if groups > 1:
        before = passed_along(ends[:, -1].astype(bf16), 1).astype(f32)
    else:
        before = jnp.zeros((seqs, 8, wide), f32)
    halos = jnp.concatenate([before[:, None], ends[:, :-1]], axis=1)
    nothing = jnp.zeros((1, inner, NS), f32)
    mixed_in, ys, enters, decays, logs, mix = [], [], [], [], [], []
    for s in range(seqs):
        fore = functools.partial(core_fore, seq=s, rows=block_len, heads=heads, span=span)
        halo = before[s : s + 1]
        gated, y, enter, final, decay_log = fore(
            turn, early, late, halo, conv_own, head_own, nothing
        )
        if groups > 1:
            decays.append(head_decay(decay_log, heads))
            init = entering(decays[s], final, False)
            gated, y, enter, final, _ = fore(turn, early, late, halo, conv_own, head_own, init)
        attn, log = attend_fore(lengths, start, q, k, v, span, s)
        mixed_in.append(jnp.concatenate([gated, attn[0]], axis=1))
        ys.append(y)
        enters.append(enter)
        logs.append(log)
        partial = dot(mixed_in[s], w_out).astype(bf16)
        mix.append(partial)
        if s == 0:
            early, late, _ = lax.optimization_barrier((early, late, partial))
            grad_ffn = [
                gather_plane((valid[n] * after(cot[n], partial)).astype(bf16)) for n in range(seqs)
            ]
    mix[0], mix[-1], w_ffn = lax.optimization_barrier((mix[0], mix[-1], w_ffn))
    mix = [lax.psum_scatter(partial, TEAM, scatter_dimension=0, tiled=True) for partial in mix]
    mix[0], *grad_ffn = lax.optimization_barrier((mix[0], *grad_ffn))
    w_gu, w_dn = join_hidden(w_ffn, plane, held, dp, width)
    w_gu, w_dn = w_gu.reshape(width, -1), w_dn.reshape(-1, width)

    units = w_dn.shape[0]
    hidden, norm2, act, ffn, grad_gu, grad_hidden, grad_mix = [], [], [], [], [], [], []
    for s in range(seqs):
        hidden.append(tokens[s].astype(f32) + valid[s] * mix[s].astype(f32))
        norm2_f, norm2_pull = jax.vjp(lambda h: rms_norm(h, gain_all[1]), hidden[s])
        norm2.append(gather_plane(norm2_f.astype(bf16)))
        if s > 0:
            norm2[s], local = lax.optimization_barrier((norm2[s], local))
            grad_mix.append(lax.all_gather(local, TEAM, axis=0, tiled=True))
        gate_up = dot(norm2[s], w_gu)
        gate, upper = gate_up[:, :units], gate_up[:, units:]
        sig_gate = sigmoid(gate)
        act.append((gate * sig_gate * upper).astype(bf16))
        grad_act = dot_last(grad_ffn[s], w_dn)
        grad_gate = grad_act * upper * (sig_gate * (1.0 + gate * (1.0 - sig_gate)))
        grad_upper = grad_act * gate * sig_gate
        grad_gu.append(jnp.concatenate([grad_gate, grad_upper], 1).astype(bf16))
        partial = dot_last(grad_gu[s], w_gu).astype(bf16)
        if s < seqs - 1:
            mix[s + 1] = after(mix[s + 1], partial)
        (grad_hidden_norm,) = norm2_pull(scatter_plane(partial))
        grad_hidden.append(cot[s] + grad_hidden_norm)
        local = (valid[s] * grad_hidden[s]).astype(bf16)
        ffn.append(dot(act[s], w_dn).astype(bf16))
    grad_w_gu = sum(map(dot_first, norm2, grad_gu)).astype(bf16)
    grad_w_dn = sum(map(dot_first, act, grad_ffn)).astype(bf16)
    grad_w_gu = grad_w_gu.reshape(dp, line, plane // dp, held, 2 * line * ffn_block)
    grad_w_gu = grad_w_gu.transpose(1, 0, 2, 3, 4).reshape(width, -1)
    local, grad_w_gu, grad_w_dn, *ffn = lax.optimization_barrier(
        (local, grad_w_gu, grad_w_dn, *ffn)
    )
    grad_mix.append(lax.all_gather(local, TEAM, axis=0, tiled=True))
    grad_mix[0], grad_w_gu, grad_w_dn = lax.optimization_barrier(
        (grad_mix[0], grad_w_gu, grad_w_dn)
    )
    grad_w_gu = lax.psum_scatter(grad_w_gu, LINE, scatter_dimension=0, tiled=True)
    grad_down = lax.psum_scatter(grad_w_dn, LINE, scatter_dimension=0, tiled=True).astype(f32)
    ffn = [scatter_core(after(partial, local)) for partial in ffn]

    def to_owners(partial):
        if groups > 1:
            partial = lax.psum_scatter(partial, "g", scatter_dimension=0, tiled=True)
        partial = partial.astype(bf16).reshape(team, held, -1)
        return lax.all_to_all(partial, TEAM, 0, 0, tiled=True).transpose(1, 0, 2).astype(f32)

    def small_grads(gconv, ghead):
        grad_conv = jnp.concatenate(
            [
                lax.dynamic_update_slice_in_dim(
                    jnp.zeros((KW + 1, MI), f32), gconv[: KW + 1, :inner], me * inner, 1
                ),
                gconv[: KW + 1, inner:],
            ],
            axis=1,
        )
        grad_head = lax.dynamic_update_slice_in_dim(
            jnp.zeros((3, MH), f32), ghead[:3, :heads], me * heads, 1
        )
        flat = jnp.concatenate([grad_conv.reshape(-1), grad_head.reshape(-1)])
        return jnp.pad(flat, (0, -flat.shape[0] % 1024)).reshape(-1, 128)

    dearly, dlate, grad_norm1 = [], [], []
    gconv, ghead = 0.0, 0.0
    for s in range(seqs):
        grad_mixed_in = dot_last(grad_mix[s], w_out)
        if s == 0:
            grad_mixed_in, *ffn = lax.optimization_barrier((grad_mixed_in, *ffn))
            ffn = [scatter_near(near) for near in ffn]
            mixed = [(hidden[n] + valid[n] * ffn[n]).astype(bf16) for n in range(seqs)]
            mixed = jnp.stack(mixed)
        if s == seqs - 1:
            grad_w_out = sum(map(dot_first, mixed_in, grad_mix)).astype(bf16)
            grad_mixed_in, grad_w_out = lax.optimization_barrier((grad_mixed_in, grad_w_out))
            grad_w_out = scatter_dp(grad_w_out, 1)
            if groups > 1:
                grad_w_out = lax.psum(grad_w_out, "g")
            grad_w_out = grad_w_out.astype(bf16)
        dq, dk, dv = attend_back(lengths, start, q, k, v, grad_mixed_in, logs[s], span, s)
        if groups > 1:
            dk = lax.psum_scatter(dk, "g", scatter_dimension=1, tiled=True)
            dv = lax.psum_scatter(dv, "g", scatter_dimension=1, tiled=True)
        dq = rotate_back(dq[0], cosine, sine).astype(bf16)
        dk = rotate_back(dk[0], cosine, sine).astype(bf16)
        z = early[s * block_len : (s + 1) * block_len, :inner]
        sig_z = sigmoid(z)
        dz = grad_mixed_in[:, :inner] * ys[s] * (sig_z * (1.0 + z * (1.0 - sig_z)))
        dearly.append(jnp.concatenate([dz.astype(bf16), dq, dk, dv[0].astype(bf16)], axis=1))
        if s == seqs - 1:
            grad_early = dot_first(norm1, jnp.concatenate(dearly, axis=0)).astype(bf16)
            grad_mixed_in, grad_early, grad_w_out, grad_w_gu = lax.optimization_barrier(
                (grad_mixed_in, grad_early, grad_w_out, grad_w_gu)
            )
            grad_w_gu = lax.all_to_all(
                grad_w_gu.reshape(plane, held, 2 * line * ffn_block), PLANE, 0, 0, tiled=True
            )
            grad_w_out = jnp.concatenate(
                [
                    grad_w_out[inner:].reshape(part, attn_rows, cut),
                    grad_w_out[:inner].reshape(part, mamba_rows, cut),
                ],
                axis=1,
            )
            if part == dp and groups == 1:
                parts = []
                for n in range(part):
                    piece = lax.dynamic_index_in_dim(
                        grad_w_out, (me // ratio) ^ n, 0, keepdims=False
                    )
                    route = [(ratio * ((i % part) ^ n) + i // part, i) for i in range(team)]
                    parts.append(lax.ppermute(piece, TEAM, route))
                grad_w_out = jnp.stack(parts)
            else:
                grad_w_out = lax.dynamic_update_slice_in_dim(
                    jnp.zeros((seq_size, out_rows, cut), bf16),
                    grad_w_out,
                    (me % ratio) * part,
                    0,
                )
                grad_w_out = lax.all_to_all(grad_w_out, SEQ, 0, 0, tiled=True)
                grad_w_out = grad_w_out.reshape(groups, dp, ratio, out_rows, cut)[0]
                grad_w_out = lax.dynamic_index_in_dim(
                    grad_w_out, my_seq // part, 1, keepdims=False
                )
                grad_w_out = jnp.take(grad_w_out, (my_seq % part % dp) ^ jnp.arange(dp), axis=0)
            grad_early = scatter_dp(grad_early, 0)
        back = functools.partial(core_back, seq=s, heads=heads, span=span)
        halo = halos[s : s + 1]
        dlate_s, gconv_s, ghead_s, dinit, dfirst = back(
            turn, early, late, grad_mixed_in, enters[s], halo, conv_own, head_own, nothing
        )
        if groups > 1:
            leave = entering(decays[s], dinit, True)
            dlate_s, gconv_s, ghead_s, dinit, dfirst = back(
                turn, early, late, grad_mixed_in, enters[s], halo, conv_own, head_own, leave
            )
            padded = jnp.concatenate([jnp.zeros((1, KW - 1, wide), f32), dfirst], axis=1)
            rim = sum(
                conv_own[j][None, None] * padded[:, KW - 1 - j : 2 * (KW - 1) - j]
                for j in range(KW)
            )
            rim = passed_along(rim.astype(bf16), -1).astype(f32)
            rim = jnp.pad(rim[0], ((block_len - KW + 1, 0), (0, 0)))
            step_gap = jnp.zeros((block_len, 128), f32)
            rim = jnp.concatenate([rim[:, :inner], step_gap, rim[:, inner:]], axis=1)
            dlate_s = (dlate_s.astype(f32) + rim).astype(bf16)
        gconv, ghead = gconv + gconv_s, ghead + ghead_s
        if s == seqs - 1:
            grad_late = dot_first(norm1, jnp.concatenate([*dlate, dlate_s], axis=0)).astype(bf16)
            small = small_grads(gconv, ghead)
            small = small + swap(small, "c", 1)
            late_cuts = cuts_dp(grad_late, 0)
            parts = []
            for n in range(dp):
                piece = lax.dynamic_index_in_dim(
                    grad_w_out, (my_seq % part % dp) ^ mine_dp ^ n, 0, keepdims=False
                )
                parts.append(swap(piece, "dp", n) if n else piece)
            dlate_s, small, grad_early, parts, late_cuts, grad_w_gu = lax.optimization_barrier(
                (dlate_s, small, grad_early, parts, late_cuts, grad_w_gu)
            )
            grad_late = sum_cuts(late_cuts)
            small = sum(swap(small, "dp", n) if n else small for n in range(dp))
        dlate.append(dlate_s)
        partial = (dot_last(dearly[s], w_early) + dot_last(dlate_s, w_late)).astype(bf16)
        if s == seqs - 1:
            grad_w_out = jnp.take(jnp.stack(parts), mine_dp ^ jnp.arange(dp), axis=0)
            grad_w_out = grad_w_out.transpose(1, 0, 2).reshape(out_rows, width).astype(f32)
            partial, grad_down, small = lax.optimization_barrier((partial, grad_down, small))
            size_z = lax.axis_size("z")
            small = sum(
                lax.ppermute(small, "z", [(i, (i + n) % size_z) for i in range(size_z)])
                if n
                else small
                for n in range(size_z)
            )
            if groups > 1:
                small = lax.psum(small, "g")
            grad_early = to_owners(grad_early)
        grad_norm1.append(lax.psum_scatter(partial, TEAM, scatter_dimension=0, tiled=True))
        if s == 0:
            grad_mix[1:], mixed, _ = lax.optimization_barrier((grad_mix[1:], mixed, partial))
    grad_gate_up = (
        grad_w_gu.reshape(dp, plane // dp, held, 2, line, ffn_block)
        .transpose(2, 3, 0, 4, 1, 5)
        .reshape(held, -1)
        .astype(f32)
    )
    grad_late, grad_w_out, grad_early, small = lax.optimization_barrier(
        (grad_late, grad_w_out, grad_early, small)
    )
    grad_late = to_owners(grad_late)
    grad_z = grad_early[:, :, :inner].reshape(held, MI)
    grad_query = grad_early[:, :, inner:key_at].reshape(held, -1)
    grad_keyval = grad_early[:, :, key_at:].reshape(held, KV, team // KV, 2, HD)
    grad_keyval = jnp.sum(grad_keyval, axis=2).transpose(0, 2, 1, 3).reshape(held, -1)
    grad_x = grad_late[:, :, :inner].reshape(held, MI)
    grad_dt = jnp.sum(grad_late[:, :, inner : inner + MH], axis=1)
    grad_bc = jnp.sum(grad_late[:, :, inner + 128 :], axis=1)
    grad_in = jnp.concatenate([grad_z, grad_x, grad_bc], axis=1)

    grad_gains = [
        jnp.sum(w_in.astype(f32) * grad_in, 1)
        + jnp.sum(w_query.astype(f32) * grad_query, 1)
        + jnp.sum(w_keyval.astype(f32) * grad_keyval, 1)
        + jnp.sum(w_dt.astype(f32) * grad_dt, 1),
        jnp.sum(w_gate_up.astype(f32) * grad_gate_up, 1),
    ]
    grad_gains = jnp.stack(grad_gains) / gains.astype(f32)
    own_conv = conv_params.shape[1]
    small = small.reshape(-1)
    conv_end = (KW + 1) * conv_params.shape[1] * devices
    grad_conv = lax.dynamic_slice_in_dim(
        small[:conv_end].reshape(KW + 1, -1), lax.axis_index(ALL) * own_conv, own_conv, 1
    )
    head_total = small[conv_end : conv_end + 3 * MH].reshape(3, MH)
    grad_tokens = []
    for s in range(seqs):
        _, norm1_pull = jax.vjp(lambda v: rms_norm(v, gain_all[0]), tokens[s].astype(f32))
        (grad_token_norm,) = norm1_pull(grad_norm1[s].astype(f32))
        grad_tokens.append((grad_hidden[s] + grad_token_norm).astype(bf16))
    grad_tokens = jnp.stack(grad_tokens)
    grad_attn_out, grad_mamba_out = grad_w_out[:attn_rows], grad_w_out[attn_rows:]
    return (
        mixed,
        grad_tokens,
        grad_gains,
        grad_query,
        grad_keyval,
        grad_attn_out,
        grad_in,
        grad_dt,
        grad_conv,
        head_total[:2],
        head_total[2],
        grad_mamba_out,
        grad_gate_up,
        grad_down,
    )


def solution(mesh):
    dp, seq = mesh.shape["dp"], mesh.shape["seq"]
    team = math.gcd(math.gcd(HQ, MH), seq)
    split = Mesh(mesh.devices.reshape(dp, seq // team, team // 2, 2), ALL)
    rows = P(ALL, None)
    cols = P(None, ALL)
    acts = P("dp", SEQ, None)
    return jax.shard_map(
        body,
        mesh=split,
        in_specs=(
            acts, P("dp"), cols, rows, rows, rows, rows, rows, cols, P(), rows, rows, rows, acts,
        ),
        out_specs=(
            acts, acts, cols, rows, rows, rows, rows, rows, cols, P(), P(), rows, rows, rows,
        ),
        check_vma=False,
    )
```

```python
import functools
import math

import jax
import jax.numpy as jnp
from jax import lax
from jax.experimental import pallas as pl
from jax.experimental.pallas import tpu as pltpu
from jax.sharding import Mesh
from jax.sharding import PartitionSpec as P

HQ = 8
KV = 2
HD = 128
MH = 48
MP = 64
NS = 256
KW = 4
MI = MH * MP

epsilon = 1e-05
rope_base = 100000000000.0
neg_big = -1e30
highest = lax.Precision.HIGHEST
bf16 = jnp.bfloat16
f32 = jnp.float32

ALL = ("dp", "g", "z", "c")
TEAM = ("z", "c")
PLANE = ("dp", "c")
LINE = ("g", "z")
SEQ = ("g", "z", "c")
SPREAD = ("dp", "g")


def rms_norm(values, gain):
    return values * lax.rsqrt(jnp.mean(values * values, -1, keepdims=True) + epsilon) * gain


def rope_tables(positions, head_size):
    half = head_size // 2
    freq = jnp.exp(jnp.arange(half, dtype=f32) * (-2.0 * math.log(rope_base) / head_size))
    angle = positions.astype(f32)[:, None] * freq[None, :]
    return (
        jnp.concatenate([jnp.cos(angle), jnp.cos(angle)], -1),
        jnp.concatenate([jnp.sin(angle), jnp.sin(angle)], -1),
    )


def rotate(values, cosine, sine):
    half = values.shape[-1] // 2
    turned = jnp.concatenate([-values[..., half:], values[..., :half]], -1)
    return values * cosine + turned * sine


def rotate_back(grads, cosine, sine):
    half = grads.shape[-1] // 2
    scaled = grads * sine
    return grads * cosine + jnp.concatenate([scaled[..., half:], -scaled[..., :half]], -1)


def dot(left, right, precision=None):
    return jnp.dot(left, right, preferred_element_type=f32, precision=precision)


def dot_first(left, right, precision=None):
    return lax.dot_general(
        left, right, (((0,), (0,)), ((), ())), preferred_element_type=f32, precision=precision
    )


def dot_last(left, right, precision=None):
    return lax.dot_general(
        left, right, (((1,), (1,)), ((), ())), preferred_element_type=f32, precision=precision
    )


def sigmoid(v):
    return 1.0 / (1.0 + jnp.exp(-v))


def softplus(v):
    return jnp.maximum(v, 0.0) + jnp.log(1.0 + jnp.exp(-jnp.abs(v)))


def cost(rows, gigaflops, arrays):
    return pl.CostEstimate(
        flops=int(rows * gigaflops * 1e9 / 2048),
        bytes_accessed=sum(a.size * a.dtype.itemsize for a in arrays),
        transcendentals=0,
    )


def params(count):
    return pltpu.CompilerParams(
        dimension_semantics=("arbitrary",) * count, vmem_limit_bytes=48 * 1024 * 1024
    )


def after(value, *others):
    return lax.optimization_barrier((value, *others))[0]


def assemble(scalars, sources, shapes, plan, count, name):
    def kernel(scalar_ref, *refs):
        sems = refs[-1]
        plan(scalar_ref, refs[: len(sources)], refs[len(sources) : -1], sems)

    anywhere = pl.BlockSpec(memory_space=pl.ANY)
    return pl.pallas_call(
        kernel,
        in_specs=[pl.BlockSpec(memory_space=pltpu.SMEM)] + [anywhere] * len(sources),
        out_specs=[pl.BlockSpec(memory_space=pltpu.VMEM)] * len(shapes),
        out_shape=[jax.ShapeDtypeStruct(shape, bf16) for shape in shapes],
        scratch_shapes=[pltpu.SemaphoreType.DMA((count,))],
        compiler_params=pltpu.CompilerParams(vmem_limit_bytes=48 * 1024 * 1024),
        cost_estimate=pl.CostEstimate(
            flops=0, bytes_accessed=4 * sum(math.prod(shape) for shape in shapes), transcendentals=0
        ),
        name=name,
    )(jnp.stack([jnp.asarray(v, jnp.int32) for v in scalars]), *sources)


def run_copies(pairs, sems):
    copies = [pltpu.make_async_copy(a, b, sems.at[i]) for i, (a, b) in enumerate(pairs)]
    for copy in copies:
        copy.start()
    for copy in copies:
        copy.wait()


def join_weights(blocks, others, inner, key_at, shared, kv_head):
    peers, here = lax.axis_size("dp"), lax.axis_index("dp")
    size = sum(part.shape[0] for part, k, _ in blocks if k == 0)
    width = size * peers
    own = inner + key_at
    keys_size = 2 * KV * HD
    many = len(blocks)

    def plan(scalar_ref, sources, outs, sems):
        early, late, rest = outs

        def pairs(turned):
            moves = []
            for i, (part, k, first) in enumerate(blocks):
                rows = part.shape[0]
                at = pl.ds(pl.multiple_of(scalar_ref[k] * size + first, rows), rows)
                source = sources[i]
                near, far = source.at[:, pl.ds(own, shared)], sources[many + i]
                steps, keys = (far, near) if turned else (near, far)
                moves.append((source.at[:, pl.ds(0, key_at)], early.at[at, pl.ds(0, key_at)]))
                moves.append((source.at[:, pl.ds(key_at, inner)], late.at[at, pl.ds(0, inner)]))
                moves.append((steps, late.at[at, pl.ds(inner, shared)]))
                for j in range(2):
                    lane = (j * KV + scalar_ref[peers]) * HD
                    if not turned:
                        keys_at = pl.multiple_of(lane, HD)
                        key_view = keys.at[:, pl.ds(keys_at, HD)]
                    else:
                        key_view = source.at[:, pl.ds(pl.multiple_of(own + lane, HD), HD)]
                    moves.append((key_view, early.at[at, pl.ds(key_at + j * HD, HD)]))
                tail = far if not turned else source
                tail_at = keys_size if not turned else own + keys_size
                moves.append((tail.at[:, pl.ds(tail_at, 128)], rest.at[at, :]))
            return moves

        @pl.when(scalar_ref[peers + 1] == 0)
        def _():
            run_copies(pairs(False), sems)

        @pl.when(scalar_ref[peers + 1] != 0)
        def _():
            run_copies(pairs(True), sems)

    scalars = [here ^ k for k in range(peers)] + [kv_head, lax.axis_index("c")]
    shapes = [(width, key_at + 2 * HD), (width, inner + shared), (width, shared - keys_size)]
    sources = [part for part, _, _ in blocks] + others
    return assemble(scalars, sources, shapes, plan, 6 * many, "join_weights")


def join_hidden(gathered, count, held, dp, width):
    line, _, columns = gathered.shape
    low = count * held
    rows = (gathered.shape[1] - low) * columns // width
    folds = width // columns

    def plan(scalar_ref, sources, outs, sems):
        moves = [
            (
                sources[0].at[:, pl.ds(i * held, held)],
                outs[0].at[scalar_ref[i], :, scalar_ref[count + i]],
            )
            for i in range(count)
        ]
        for i in range(folds):
            moves.append(
                (
                    sources[0].at[:, pl.ds(low + i * rows, rows)],
                    outs[1].at[:, :, pl.ds(i * columns, columns)],
                )
            )
        run_copies(moves, sems)

    near, core = lax.axis_index("dp"), lax.axis_index("c")
    scalars = [near ^ (i % dp) for i in range(count)] + [core ^ (i // dp) for i in range(count)]
    shapes = [(dp, line, count // dp, held, columns), (line, rows, width)]
    return assemble(scalars, [gathered], shapes, plan, count + folds, "join_hidden")


def join_rows(slots, place):
    count, rows, width = len(slots), *slots[0].shape

    def plan(scalar_ref, sources, outs, sems):
        run_copies([(sources[k], outs[0].at[scalar_ref[k]]) for k in range(count)], sems)

    scalars = [place ^ k for k in range(count)]
    whole = assemble(scalars, slots, [(count, rows, width)], plan, count, "join_rows")[0]
    return whole.reshape(count * rows, width)


def join_columns(pieces):
    peers, here = lax.axis_size("dp"), lax.axis_index("dp")
    rows, cut = pieces[0].shape

    def plan(scalar_ref, sources, outs, sems):
        run_copies(
            [
                (sources[k], outs[0].at[:, pl.ds(pl.multiple_of(scalar_ref[k] * cut, cut), cut)])
                for k in range(peers)
            ],
            sems,
        )

    scalars = [here ^ k for k in range(peers)]
    return assemble(scalars, pieces, [(rows, cut * peers)], plan, peers, "join_columns")[0]


def join_out(blocks, place, attn_rows, mamba_rows):
    peers, here = lax.axis_size("dp"), lax.axis_index("dp")
    parts, rows, cut = blocks[0].shape

    def plan(scalar_ref, sources, outs, sems):
        moves = []
        for k in range(peers):
            lane = pl.ds(pl.multiple_of(scalar_ref[k] * cut, cut), cut)
            for i in range(parts):
                at = scalar_ref[peers + i]
                low = pl.multiple_of(at * mamba_rows, 16)
                high = pl.multiple_of(parts * mamba_rows + at * attn_rows, 16)
                moves.append(
                    (
                        sources[k].at[i, pl.ds(attn_rows, mamba_rows)],
                        outs[0].at[pl.ds(low, mamba_rows), lane],
                    )
                )
                moves.append(
                    (
                        sources[k].at[i, pl.ds(0, attn_rows)],
                        outs[0].at[pl.ds(high, attn_rows), lane],
                    )
                )
        run_copies(moves, sems)

    scalars = [here ^ k for k in range(peers)] + [place ^ i for i in range(parts)]
    shape = (parts * rows, cut * peers)
    return assemble(scalars, blocks, [shape], plan, 2 * peers * parts, "join_out")[0]


def swap(block, axis, distance):
    return lax.ppermute(block, axis, [(i, i ^ distance) for i in range(lax.axis_size(axis))])


def gather_core(near):
    return jnp.concatenate(near + [swap(piece, "c", 1) for piece in near], axis=0)


def gather_plane(block):
    return gather_core(from_dp(block))


def scatter_core(partial):
    half = partial.shape[0] // 2
    near = partial[:half].astype(f32) + swap(partial[half:], "c", 1).astype(f32)
    return near.astype(bf16)


def scatter_near(near):
    near = jnp.split(near, lax.axis_size("dp"), axis=0)
    return sum(
        (swap(near[k], "dp", k) if k else near[k]).astype(f32) for k in range(len(near))
    )


def scatter_plane(partial):
    return scatter_near(scatter_core(partial))


def from_dp(block):
    return [block] + [swap(block, "dp", k) for k in range(1, lax.axis_size("dp"))]


def parts_dp(block):
    if lax.axis_size("dp") != 4:
        return [(part, k, 0) for k, part in enumerate(from_dp(block))]
    half = block.shape[0] // 2
    one, two = swap(block, "dp", 1), swap(block, "dp", 2)
    top, bottom = swap(one[:half], "dp", 2), swap(two[half:], "dp", 1)
    return [(block, 0, 0), (one, 1, 0), (two, 2, 0), (top, 3, 0), (bottom, 3, half)]


def cuts_dp(partial, axis):
    peers, here = lax.axis_size("dp"), lax.axis_index("dp")
    size = partial.shape[axis] // peers
    return [lax.dynamic_slice_in_dim(partial, (here ^ k) * size, size, axis) for k in range(peers)]


def sum_cuts(cuts):
    return sum((swap(cut, "dp", k) if k else cut).astype(f32) for k, cut in enumerate(cuts))


def scatter_dp(partial, axis):
    return sum_cuts(cuts_dp(partial, axis))


def attend_mask(length_ref, start_ref, seq, block, width, first):
    qpos = start_ref[0] + first + lax.broadcasted_iota(jnp.int32, (block, width), 0)
    kpos = lax.broadcasted_iota(jnp.int32, (block, width), 1)
    return (kpos <= qpos) & (kpos < length_ref[seq])


def attend_fore_kernel(
    length_ref, start_ref, q_ref, k_ref, v_ref, o_ref, log_ref, *, scale, block, seq
):
    at = pl.program_id(0)
    keys = k_ref[0]
    scores = dot_last(q_ref[0], keys) * scale
    allowed = attend_mask(length_ref, start_ref, seq, block, keys.shape[0], at * block)
    scores = jnp.where(allowed, scores, neg_big)
    top = jnp.max(scores, -1, keepdims=True)
    expo = jnp.exp(scores - top)
    total = jnp.sum(expo, -1, keepdims=True)
    prob = (expo * (1.0 / total)).astype(bf16)
    o_ref[0] = dot(prob, v_ref[0]).astype(bf16)
    log_ref[0] = jnp.broadcast_to(top + jnp.log(total), log_ref.shape[1:])


def attend_fore(length, start, q, k, v, block, seq):
    _, rows, width = q.shape
    kernel = functools.partial(
        attend_fore_kernel, scale=1.0 / math.sqrt(HD), block=block, seq=seq
    )
    qspec = pl.BlockSpec((1, block, width), lambda i: (seq, i, 0))
    ospec = pl.BlockSpec((1, block, width), lambda i: (0, i, 0))
    kspec = pl.BlockSpec((1, k.shape[1], width), lambda i: (seq, 0, 0))
    smem = pl.BlockSpec(memory_space=pltpu.SMEM)
    return pl.pallas_call(
        kernel,
        grid=(rows // block,),
        in_specs=[smem, smem, qspec, kspec, kspec],
        out_specs=[ospec, ospec],
        out_shape=[
            jax.ShapeDtypeStruct((1, rows, width), bf16),
            jax.ShapeDtypeStruct((1, rows, width), f32),
        ],
        compiler_params=params(1),
        cost_estimate=cost(rows, 7, (q, k, v)),
        name="attend_fore",
    )(length, start, q, k, v)


def attend_back_kernel(
    length_ref, start_ref, q_ref, k_ref, v_ref, do_ref, log_ref, dq_ref, dk_ref, dv_ref,
    *, scale, block, seq,
):
    at = pl.program_id(0)

    @pl.when(at == 0)
    def _():
        dk_ref[...] = jnp.zeros_like(dk_ref)
        dv_ref[...] = jnp.zeros_like(dv_ref)

    keys = k_ref[0]
    queries = q_ref[0]
    grad_out = do_ref[0].astype(bf16)
    scores = dot_last(queries, keys) * scale
    allowed = attend_mask(length_ref, start_ref, seq, block, keys.shape[0], at * block)
    scores = jnp.where(allowed, scores, neg_big)
    prob = jnp.exp(scores - log_ref[0][:, :1])
    grad_prob = dot_last(grad_out, v_ref[0])
    centre = jnp.sum(prob * grad_prob, -1, keepdims=True)
    grad_score = (prob * (grad_prob - centre)).astype(bf16)
    dq_ref[0] = dot(grad_score, keys) * scale
    dk_ref[0] += dot_first(grad_score, queries) * scale
    dv_ref[0] += dot_first(prob.astype(bf16), grad_out)


def attend_back(length, start, q, k, v, grad_out, logs, block, seq):
    _, rows, width = q.shape
    out_at = grad_out.shape[1] // width - 1
    kernel = functools.partial(
        attend_back_kernel, scale=1.0 / math.sqrt(HD), block=block, seq=seq
    )
    qspec = pl.BlockSpec((1, block, width), lambda i: (seq, i, 0))
    ospec = pl.BlockSpec((1, block, width), lambda i: (0, i, 0))
    kspec = pl.BlockSpec((1, k.shape[1], width), lambda i: (seq, 0, 0))
    gspec = pl.BlockSpec((1, k.shape[1], width), lambda i: (0, 0, 0))
    smem = pl.BlockSpec(memory_space=pltpu.SMEM)
    return pl.pallas_call(
        kernel,
        grid=(rows // block,),
        in_specs=[
            smem,
            smem,
            qspec,
            kspec,
            kspec,
            pl.BlockSpec((1, block, width), lambda i: (0, i, out_at)),
            ospec,
        ],
        out_specs=[ospec, gspec, gspec],
        out_shape=[
            jax.ShapeDtypeStruct((1, rows, width), f32),
            jax.ShapeDtypeStruct((1, *k.shape[1:]), f32),
            jax.ShapeDtypeStruct((1, *k.shape[1:]), f32),
        ],
        compiler_params=params(1),
        cost_estimate=cost(rows, 11, (q, k, v, logs)),
        name="attend_back",
    )(length, start, q, k, v, grad_out[None], logs)


def head_spread(heads):
    row = lax.broadcasted_iota(jnp.int32, (128, heads * MP), 0)
    col = lax.broadcasted_iota(jnp.int32, (128, heads * MP), 1)
    return (row == col // MP).astype(f32)


def triangle(span):
    row = lax.broadcasted_iota(jnp.int32, (span, span), 0)
    col = lax.broadcasted_iota(jnp.int32, (span, span), 1)
    return row >= col


def conv_pre(ext_ref, conv_ref, span):
    total = conv_ref[KW : KW + 1, :]
    for k in range(KW):
        total = total + conv_ref[k : k + 1, :] * ext_ref[pl.ds(8 - (KW - 1) + k, span), :]
    return total


def core_fore_kernel(
    turn_ref, x_ref, bc_ref, z_ref, dt_ref, halo_ref, conv_ref, head_ref, init_ref,
    gated_ref, y_ref, enter_ref, final_ref, decay_ref,
    ext, state, total, *, heads, span,
):
    inner = heads * MP
    at = pl.program_id(0)

    @pl.when(at == 0)
    def _():
        ext[0:8, :] = halo_ref[0]
        state[...] = init_ref[0]
        total[...] = jnp.zeros_like(total)

    ext[8:, :inner] = x_ref[...]
    ext[8:, inner:] = bc_ref[...]
    pre = conv_pre(ext, conv_ref, span)
    ext[0:8, :] = ext[span : span + 8, :]
    cv = pre * sigmoid(pre)
    xs = cv[:, :inner]
    bmat = cv[:, inner : inner + NS].astype(bf16)
    cmat = cv[:, inner + NS :].astype(bf16)
    spread = head_spread(heads)
    lower = triangle(span)
    step = softplus(pltpu.roll(dt_ref[...], 128 - turn_ref[0], 1) + head_ref[0:1, :])
    decay_log = -jnp.exp(head_ref[1:2, :]) * step
    cum = dot(lower.astype(f32), decay_log, highest)
    cum_t = cum.T
    step_t = step.T
    last = cum[span - 1 : span, :]
    enter = state[...]
    enter_ref[0, 0] = enter
    pair = dot_last(cmat, bmat)
    xb = xs.astype(bf16)
    parts = []
    for h in range(heads):
        diff = cum[:, h : h + 1] - cum_t[h : h + 1, :]
        decay = jnp.exp(jnp.where(lower, diff, neg_big))
        mixing = (pair * decay * step_t[h : h + 1, :]).astype(bf16)
        parts.append(dot(mixing, xb[:, h * MP : (h + 1) * MP]))
    y = jnp.concatenate(parts, axis=1)
    y = y + dot_last(cmat, enter.astype(bf16)) * dot(jnp.exp(cum), spread, highest)
    y = y + xs * dot(jnp.broadcast_to(head_ref[2:3, :], (8, 128)), spread, highest)[0:1, :]
    tail = dot(jnp.exp(last - cum) * step, spread, highest)
    keep = jnp.broadcast_to(jnp.exp(cum_t[:, span - 1 : span]), (128, NS))
    new_state = dot_first(spread, keep, highest) * enter + dot_first((xs * tail).astype(bf16), bmat)
    state[...] = new_state
    final_ref[0] = new_state
    total[...] = total[...] + last
    decay_ref[0] = total[...]
    z = z_ref[...]
    y_ref[...] = y
    gated_ref[...] = (y * (z * sigmoid(z))).astype(bf16)


def core_fore(turn, early, late, halo, conv, head, init, seq, rows, heads, span):
    inner = heads * MP
    wide = inner + 2 * NS
    count = rows // span
    first = seq * count

    def block(width, at):
        return pl.BlockSpec((span, width), lambda i: (first + i, at))

    def whole(*shape):
        return pl.BlockSpec(shape, lambda i: (0,) * len(shape))

    out = pl.BlockSpec((span, inner), lambda i: (i, 0))
    return pl.pallas_call(
        functools.partial(core_fore_kernel, heads=heads, span=span),
        grid=(count,),
        in_specs=[
            pl.BlockSpec(memory_space=pltpu.SMEM),
            block(inner, 0),
            block(2 * NS, (inner + 128) // (2 * NS)),
            block(inner, 0),
            block(128, inner // 128),
            whole(1, 8, wide),
            whole(8, wide),
            whole(8, 128),
            whole(1, inner, NS),
        ],
        out_specs=[
            out,
            out,
            pl.BlockSpec((1, 1, inner, NS), lambda i: (0, i, 0, 0)),
            whole(1, inner, NS),
            whole(1, 8, 128),
        ],
        out_shape=[
            jax.ShapeDtypeStruct((rows, inner), bf16),
            jax.ShapeDtypeStruct((rows, inner), f32),
            jax.ShapeDtypeStruct((1, count, inner, NS), f32),
            jax.ShapeDtypeStruct((1, inner, NS), f32),
            jax.ShapeDtypeStruct((1, 8, 128), f32),
        ],
        scratch_shapes=[
            pltpu.VMEM((span + 8, wide), f32),
            pltpu.VMEM((inner, NS), f32),
            pltpu.VMEM((8, 128), f32),
        ],
        compiler_params=params(1),
        cost_estimate=cost(rows, 26, (late, init)),
        name="core_fore",
    )(turn, late, late, early, late, halo, conv, head, init)


def core_back_kernel(
    turn_ref, x_ref, bc_ref, z_ref, dt_ref, dg_ref, enter_ref, halo_ref, conv_ref, head_ref, exit_ref,
    dlate_ref, gconv_ref, ghead_ref, dinit_ref, dfirst_ref,
    ext, dext, dstate, *, heads, span,
):
    inner = heads * MP
    at = pl.program_id(0)

    @pl.when(at == 0)
    def _():
        gconv_ref[...] = jnp.zeros_like(gconv_ref)
        ghead_ref[...] = jnp.zeros_like(ghead_ref)

    @pl.when(at == 0)
    def _():
        dext[span:, :] = jnp.zeros((8, dext.shape[1]), f32)
        dstate[...] = exit_ref[0]

    ext[0:8, :] = halo_ref[0, 0]
    ext[8:, :inner] = x_ref[...]
    ext[8:, inner:] = bc_ref[...]
    pre = conv_pre(ext, conv_ref, span)
    gate = sigmoid(pre)
    cv = pre * gate
    xs = cv[:, :inner]
    bmat = cv[:, inner : inner + NS].astype(bf16)
    cmat = cv[:, inner + NS :].astype(bf16)
    xb = xs.astype(bf16)
    z = z_ref[...]
    dy = dg_ref[...] * (z * sigmoid(z))
    dyb = dy.astype(bf16)
    spread = head_spread(heads)
    lower = triangle(span)
    raw = pltpu.roll(dt_ref[...], 128 - turn_ref[0], 1) + head_ref[0:1, :]
    step = softplus(raw)
    rate = -jnp.exp(head_ref[1:2, :])
    decay_log = rate * step
    cum = dot(lower.astype(f32), decay_log, highest)
    cum_t = cum.T
    step_t = step.T
    last = cum[span - 1 : span, :]
    enter = enter_ref[0, 0]
    leave = dstate[...]
    pair = dot_last(cmat, bmat)
    dpair = jnp.zeros((span, span), f32)
    lane = lax.broadcasted_iota(jnp.int32, (span, 128), 1)
    line = lax.broadcasted_iota(jnp.int32, (128, span), 0)
    row_sums = jnp.zeros((span, 128), f32)
    col_sums = jnp.zeros((128, span), f32)
    parts = []
    for h in range(heads):
        diff = cum[:, h : h + 1] - cum_t[h : h + 1, :]
        decay = jnp.exp(jnp.where(lower, diff, neg_big))
        now = step_t[h : h + 1, :]
        cut = slice(h * MP, (h + 1) * MP)
        dmix = dot_last(dyb[:, cut], xb[:, cut]) * decay
        both = dmix * pair
        dmix_now = dmix * now
        dpair = dpair + dmix_now
        row_sums = jnp.where(lane == h, jnp.sum(both * now, 1, keepdims=True), row_sums)
        col_sums = jnp.where(line == h, jnp.sum(both, 0, keepdims=True), col_sums)
        mixing = (pair * decay * now).astype(bf16)
        parts.append(dot_first(mixing, dyb[:, cut]))
    dxs = jnp.concatenate(parts, axis=1)
    dstep = col_sums.T
    dcum = row_sums - dstep * step
    dpb = dpair.astype(bf16)
    dcm = dot(dpb, bmat)
    dbm = dot_first(dpb, cmat)
    grown = dot(jnp.exp(cum), spread, highest)
    enter_b = enter.astype(bf16)
    leave_b = leave.astype(bf16)
    dgrown = (dy * grown).astype(bf16)
    dcum = dcum + dot_last(dy * dot_last(cmat, enter_b) * grown, spread, highest)
    dcm = dcm + dot(dgrown, enter_b)
    fade = jnp.exp(last - cum)
    tail = dot(fade * step, spread, highest)
    into = dot_last(bmat, leave_b)
    dxs = dxs + into * tail
    owed = dot_last(xs * into, spread, highest) * fade
    dstep = dstep + owed
    owed = owed * step
    dcum = dcum - owed
    dbm = dbm + dot((xs * tail).astype(bf16), leave_b)
    held = dot(spread, enter * leave, highest)
    held = dot_last(jnp.ones((8, NS), f32), held, highest)[0:1, :]
    dlast = jnp.sum(owed, 0, keepdims=True) + jnp.exp(last) * held
    keep = jnp.broadcast_to(jnp.exp(cum_t[:, span - 1 : span]), (128, NS))
    new_dstate = dot_first(spread, keep, highest) * leave + dot_first(dgrown, cmat)
    dstate[...] = new_dstate
    dinit_ref[0] = new_dstate
    dlog = dot_first(lower.astype(f32), dcum, highest) + dlast
    dstep = dstep + dlog * rate
    ddt = dstep * sigmoid(raw)
    dlate_ref[:, inner : inner + 128] = pltpu.roll(ddt, turn_ref[0], 1).astype(bf16)
    skip = dot(jnp.broadcast_to(head_ref[2:3, :], (8, 128)), spread, highest)[0:1, :]
    dxs = dxs + skip * dy
    ghead_ref[0:1, :] += jnp.sum(ddt, 0, keepdims=True)
    ghead_ref[1:2, :] += jnp.sum(dlog * decay_log, 0, keepdims=True)
    ghead_ref[2:3, :] += jnp.sum(dot_last(dy * xs, spread, highest), 0, keepdims=True)
    slope = gate * (1.0 + pre * (1.0 - gate))
    dpre = jnp.concatenate([dxs, dbm, dcm], axis=1) * slope
    dext[0:span, :] = dpre
    gconv_ref[KW : KW + 1, :] += jnp.sum(dpre, 0, keepdims=True)
    dxbc = jnp.zeros_like(dpre)
    for k in range(KW):
        dxbc = dxbc + conv_ref[k : k + 1, :] * dext[pl.ds(KW - 1 - k, span), :]
        gconv_ref[k : k + 1, :] += jnp.sum(
            dpre * ext[pl.ds(8 - (KW - 1) + k, span), :], 0, keepdims=True
        )
    dlate_ref[:, :inner] = dxbc[:, :inner].astype(bf16)
    dlate_ref[:, inner + 128 :] = dxbc[:, inner:].astype(bf16)
    dext[span:, :] = dext[0:8, :]
    dfirst_ref[0] = dext[0:8, :]


def core_back(turn, early, late, dmixed, enter, halos, conv, head, leave, seq, heads, span):
    rows = dmixed.shape[0]
    inner = heads * MP
    wide = inner + 2 * NS
    count = rows // span
    first = seq * count

    def block(width, at):
        return pl.BlockSpec((span, width), lambda i: (first + count - 1 - i, at))

    def own(width):
        return pl.BlockSpec((span, width), lambda i: (count - 1 - i, 0))

    def whole(*shape):
        return pl.BlockSpec(shape, lambda i: (0,) * len(shape))

    return pl.pallas_call(
        functools.partial(core_back_kernel, heads=heads, span=span),
        grid=(count,),
        in_specs=[
            pl.BlockSpec(memory_space=pltpu.SMEM),
            block(inner, 0),
            block(2 * NS, (inner + 128) // (2 * NS)),
            block(inner, 0),
            block(128, inner // 128),
            own(inner),
            pl.BlockSpec((1, 1, inner, NS), lambda i: (0, count - 1 - i, 0, 0)),
            pl.BlockSpec((1, 1, 8, wide), lambda i: (0, count - 1 - i, 0, 0)),
            whole(8, wide),
            whole(8, 128),
            whole(1, inner, NS),
        ],
        out_specs=[
            own(late.shape[1]),
            whole(8, wide),
            whole(8, 128),
            whole(1, inner, NS),
            whole(1, 8, wide),
        ],
        out_shape=[
            jax.ShapeDtypeStruct((rows, late.shape[1]), bf16),
            jax.ShapeDtypeStruct((8, wide), f32),
            jax.ShapeDtypeStruct((8, 128), f32),
            jax.ShapeDtypeStruct((1, inner, NS), f32),
            jax.ShapeDtypeStruct((1, 8, wide), f32),
        ],
        scratch_shapes=[
            pltpu.VMEM((span + 8, wide), f32),
            pltpu.VMEM((span + 8, wide), f32),
            pltpu.VMEM((inner, NS), f32),
        ],
        compiler_params=params(1),
        cost_estimate=cost(rows, 60, (late, enter)),
        name="core_back",
    )(turn, late, late, early, late, dmixed, enter, halos, conv, head, leave)


def passed_along(block, distance):
    devices = range(lax.axis_size("g"))
    route = [(i - distance, i) for i in devices if i - distance in devices]
    return lax.ppermute(block, "g", route)


def entering(decay, local, reverse):
    peers, here = lax.axis_size("g"), lax.axis_index("g")
    decays = lax.all_gather(decay, "g")
    locals_ = lax.all_gather(local.astype(bf16), "g")
    state = jnp.zeros_like(local)
    for k in range(peers):
        at = peers - 1 - k if reverse else k
        reached = (at > here) if reverse else (at < here)
        state = jnp.where(reached, decays[at] * state + locals_[at].astype(f32), state)
    return state


def head_decay(decay_log, heads):
    keep = jnp.exp(decay_log[:, 0, :heads])
    return jnp.repeat(keep, MP, axis=1)[:, :, None]


def body(
    tokens, lengths, gains, w_query, w_keyval, w_attn_out, w_in, w_dt, conv_params, head_params,
    w_mamba_out, w_gate_up, w_down, cotangent,
):
    seqs, rows_seq, width = tokens.shape
    dp, groups, team = lax.axis_size("dp"), lax.axis_size("g"), lax.axis_size(TEAM)
    devices, line, plane = lax.axis_size(ALL), lax.axis_size(LINE), lax.axis_size(PLANE)
    seq_size = groups * team
    me = lax.axis_index(TEAM)
    heads = MH // team
    inner = heads * MP
    query = HQ * HD // team
    block_len = rows_seq * team
    rows = seqs * block_len
    held = w_query.shape[0]
    span = math.gcd(256, block_len)
    start = (lax.axis_index("g") * block_len).astype(jnp.int32).reshape(1)
    kv_head = me * (HQ // team) * KV // HQ

    core = lax.axis_index("c")
    conv_flat = conv_params.reshape(-1)
    conv_cols = -(-conv_flat.shape[0] // held)
    conv_flat = jnp.pad(conv_flat, (0, conv_cols * held - conv_flat.shape[0]))
    shared = 128 + 2 * NS
    keys_size = 2 * KV * HD
    packed = jnp.concatenate(
        [
            jnp.pad(w_dt, ((0, 0), (0, 128 - MH))),
            w_in[:, 2 * MI :],
            w_keyval,
            gains.T,
            conv_flat.reshape(held, conv_cols),
            jnp.zeros((held, shared - keys_size - 2 - conv_cols), bf16),
        ],
        axis=1,
    )
    w_big = jnp.concatenate(
        [
            w_in[:, :MI].reshape(held, team, inner),
            w_query.reshape(held, team, query),
            w_in[:, MI : 2 * MI].reshape(held, team, inner),
            jnp.tile(packed.reshape(held, 2, shared), (1, team // 2, 1)),
        ],
        axis=2,
    ).transpose(1, 0, 2)
    slots = []
    for k in range(team):
        slot = lax.dynamic_index_in_dim(w_big, me ^ k, 0, keepdims=False)
        route = [(i, i ^ k) for i in range(team)]
        slots.append(lax.ppermute(slot, TEAM, route) if k else slot)
    w_big = slots
    ffn_block = w_down.shape[0]
    w_gu = w_gate_up.reshape(held, 2, dp, line, plane // dp, ffn_block).transpose(4, 2, 0, 1, 3, 5)
    w_gu = w_gu.reshape(plane // dp, dp, held, 2 * line * ffn_block)
    mine_dp = lax.axis_index("dp")
    slots = []
    for j in range(2):
        for k in range(dp):
            slot = lax.dynamic_slice(
                w_gu, (core ^ j, mine_dp ^ k, 0, 0), (1, 1, held, 2 * line * ffn_block)
            )[0, 0]
            if j or k:
                route = [(2 * a + b, 2 * (a ^ k) + (b ^ j)) for a in range(dp) for b in range(2)]
                slot = lax.ppermute(slot, PLANE, route)
            slots.append(slot)
    w_gu = slots
    ratio = team // dp
    part = seq_size // ratio
    attn_rows, mamba_rows = w_attn_out.shape[0], w_mamba_out.shape[0]
    out_rows = attn_rows + mamba_rows
    cut = width // dp
    w_out = jnp.concatenate([w_attn_out, w_mamba_out], axis=0)
    w_out = w_out.reshape(out_rows, dp, cut)
    quarters = []
    for k in range(dp):
        quarter = lax.dynamic_index_in_dim(w_out, mine_dp ^ k, 1, keepdims=False)
        quarters.append(swap(quarter, "dp", k) if k else quarter)
    w_big, w_gu, quarters = lax.optimization_barrier((w_big, w_gu, quarters))
    w_big = join_rows(w_big, me)
    if groups > 1:
        w_big = lax.all_gather(w_big, "g", axis=0, tiled=True)
    block_tokens = lax.all_gather(after(tokens, w_big), TEAM, axis=1, tiled=True)
    block_tokens = block_tokens.reshape(rows, width)
    positions = start[0] + jnp.arange(block_len, dtype=jnp.int32)
    cosine, sine = rope_tables(positions, HD)
    blocks = parts_dp(w_big)
    key_at = inner + query
    others = [swap(part[:, inner + key_at :], "c", 1) for part, _, _ in blocks]
    columns = 2 * line * ffn_block
    folded = [w_down[:, i * columns : (i + 1) * columns] for i in range(width // columns)]
    w_ffn = jnp.concatenate([*w_gu, *folded], axis=0)
    w_out = jnp.stack(quarters)
    others, w_ffn, w_out, cosine, sine = lax.optimization_barrier(
        (others, w_ffn, w_out, cosine, sine)
    )
    w_early, w_late, rest = join_weights(blocks, others, inner, key_at, shared, kv_head)
    gain_all = rest[:, :2].astype(f32).T
    conv_all = rest[:, 2 : 2 + conv_cols]
    conv_all = conv_all.reshape(devices, held * conv_cols)[:, : conv_params.size]
    conv_all = (
        conv_all.reshape(devices, KW + 1, -1).transpose(1, 0, 2).reshape(KW + 1, -1).astype(f32)
    )
    conv_own = jnp.concatenate(
        [lax.dynamic_slice_in_dim(conv_all, me * inner, inner, 1), conv_all[:, MI:]], axis=1
    )
    conv_own = jnp.pad(conv_own, ((0, 8 - KW - 1), (0, 0)))
    head_own = jnp.pad(
        lax.dynamic_slice_in_dim(head_params, me * heads, heads, 1), ((0, 5), (0, 128 - heads))
    )
    turn = (me * heads).astype(jnp.int32).reshape(1)
    block_tokens, w_ffn, w_early, w_late, gain_all = lax.optimization_barrier(
        (block_tokens, w_ffn, w_early, w_late, gain_all)
    )
    w_ffn = lax.all_gather(w_ffn, LINE, axis=0, tiled=False).reshape(line, -1, columns)
    my_seq = lax.axis_index(SEQ)
    w_out = after(w_out, block_tokens)
    if part == dp and groups == 1:
        parts = []
        for k in range(part):
            block = lax.dynamic_index_in_dim(w_out, mine_dp ^ (me % part) ^ k, 0, keepdims=False)
            route = [(i, ratio * ((i % part) ^ k) + i // part) for i in range(team)]
            parts.append(lax.ppermute(block, TEAM, route))
        w_out = jnp.stack(parts)
    else:
        order = mine_dp ^ jnp.arange(dp)
        w_out = jnp.take(w_out, order, axis=0)
        mine = (jnp.arange(ratio) == my_seq // part)[None, :, None, None]
        w_out = jnp.where(mine, w_out[:, None], jnp.zeros((), bf16))
        w_out = jnp.broadcast_to(
            w_out.reshape(1, team, out_rows, cut), (groups, team, out_rows, cut)
        ).reshape(-1, out_rows, cut)
        w_out = lax.all_to_all(w_out, SEQ, 0, 0, tiled=True)
        w_out = lax.dynamic_slice_in_dim(w_out, (me % ratio) * part, part, 0)
        w_out = jnp.concatenate(
            [w_out[:, attn_rows:].reshape(-1, cut), w_out[:, :attn_rows].reshape(-1, cut)], axis=0
        )

    own_positions = my_seq * rows_seq + jnp.arange(rows_seq, dtype=jnp.int32)
    valid = (own_positions[None, :] < lengths[:, None]).astype(f32)[:, :, None]
    cot = cotangent.astype(f32)

    norm1 = rms_norm(block_tokens.astype(f32), gain_all[0]).astype(bf16)
    early = dot(norm1, w_early)
    late = dot(norm1, w_late)
    early, late, w_out = lax.optimization_barrier((early, late, w_out))
    if w_out.ndim == 3:
        w_out = join_out(from_dp(w_out), me // ratio, attn_rows, mamba_rows)
    else:
        w_out = join_columns(from_dp(w_out))
    q = rotate(early[:, inner:key_at].reshape(seqs, block_len, HD), cosine, sine).astype(bf16)
    k = rotate(
        early[:, key_at : key_at + HD].reshape(seqs, block_len, HD), cosine, sine
    ).astype(bf16)
    v = early[:, key_at + HD :].reshape(seqs, block_len, HD).astype(bf16)
    if groups > 1:
        k = lax.all_gather(k, "g", axis=1, tiled=True)
        v = lax.all_gather(v, "g", axis=1, tiled=True)
    wide = inner + 2 * NS
    ends = late.reshape(seqs, block_len // span, span, -1)[:, :, span - 8 :, :]
    ends = jnp.concatenate([ends[..., :inner], ends[..., inner + 128 :]], axis=-1)
    if groups > 1:
        before = passed_along(ends[:, -1].astype(bf16), 1).astype(f32)
    else:
        before = jnp.zeros((seqs, 8, wide), f32)
    halos = jnp.concatenate([before[:, None], ends[:, :-1]], axis=1)
    nothing = jnp.zeros((1, inner, NS), f32)
    mixed_in, ys, enters, decays, logs, mix = [], [], [], [], [], []
    for s in range(seqs):
        fore = functools.partial(core_fore, seq=s, rows=block_len, heads=heads, span=span)
        halo = before[s : s + 1]
        gated, y, enter, final, decay_log = fore(
            turn, early, late, halo, conv_own, head_own, nothing
        )
        if groups > 1:
            decays.append(head_decay(decay_log, heads))
            init = entering(decays[s], final, False)
            gated, y, enter, final, _ = fore(turn, early, late, halo, conv_own, head_own, init)
        attn, log = attend_fore(lengths, start, q, k, v, span, s)
        mixed_in.append(jnp.concatenate([gated, attn[0]], axis=1))
        ys.append(y)
        enters.append(enter)
        logs.append(log)
        partial = dot(mixed_in[s], w_out).astype(bf16)
        mix.append(partial)
        if s == 0:
            early, late, _ = lax.optimization_barrier((early, late, partial))
            grad_ffn = [
                gather_plane((valid[n] * after(cot[n], partial)).astype(bf16)) for n in range(seqs)
            ]
    mix[0], mix[-1], w_ffn = lax.optimization_barrier((mix[0], mix[-1], w_ffn))
    mix = [lax.psum_scatter(partial, TEAM, scatter_dimension=0, tiled=True) for partial in mix]
    mix[0], *grad_ffn = lax.optimization_barrier((mix[0], *grad_ffn))
    w_gu, w_dn = join_hidden(w_ffn, plane, held, dp, width)
    w_gu, w_dn = w_gu.reshape(width, -1), w_dn.reshape(-1, width)

    units = w_dn.shape[0]
    hidden, norm2, act, ffn, grad_gu, grad_hidden, grad_mix = [], [], [], [], [], [], []
    for s in range(seqs):
        hidden.append(tokens[s].astype(f32) + valid[s] * mix[s].astype(f32))
        norm2_f, norm2_pull = jax.vjp(lambda h: rms_norm(h, gain_all[1]), hidden[s])
        near = from_dp(norm2_f.astype(bf16))
        if s > 0:
            near, local = lax.optimization_barrier((near, local))
            grad_mix.append(lax.all_gather(local, TEAM, axis=0, tiled=True))
        norm2.append(gather_core(near))
        gate_up = dot(norm2[s], w_gu)
        gate, upper = gate_up[:, :units], gate_up[:, units:]
        sig_gate = sigmoid(gate)
        act.append((gate * sig_gate * upper).astype(bf16))
        grad_act = dot_last(grad_ffn[s], w_dn)
        grad_gate = grad_act * upper * (sig_gate * (1.0 + gate * (1.0 - sig_gate)))
        grad_upper = grad_act * gate * sig_gate
        grad_gu.append(jnp.concatenate([grad_gate, grad_upper], 1).astype(bf16))
        partial = dot_last(grad_gu[s], w_gu).astype(bf16)
        if s < seqs - 1:
            mix[s + 1] = after(mix[s + 1], partial)
        ffn.append(dot(act[s], w_dn).astype(bf16))
        near = scatter_core(partial)
        if s == seqs - 1:
            ffn = [scatter_core(part_ffn) for part_ffn in ffn]
            grad_mix[0], near, ffn = lax.optimization_barrier((grad_mix[0], near, ffn))
        (grad_hidden_norm,) = norm2_pull(scatter_near(near))
        grad_hidden.append(cot[s] + grad_hidden_norm)
        local = (valid[s] * grad_hidden[s]).astype(bf16)

    own_conv = conv_params.shape[1]
    rest_size = (KW + 1) * own_conv + 3 * MH
    rest_cols = -(-rest_size // held)

    def to_owners(partial):
        if groups > 1:
            partial = lax.psum_scatter(partial, "g", scatter_dimension=0, tiled=True)
        partial = partial.astype(bf16).reshape(team, held, -1)
        return lax.all_to_all(partial, TEAM, 0, 0, tiled=True).transpose(1, 0, 2).astype(f32)

    def small_grads(gconv, ghead):
        grad_conv = jnp.concatenate(
            [
                lax.dynamic_update_slice_in_dim(
                    jnp.zeros((KW + 1, MI), f32), gconv[: KW + 1, :inner], me * inner, 1
                ),
                gconv[: KW + 1, inner:],
            ],
            axis=1,
        )
        grad_head = lax.dynamic_update_slice_in_dim(
            jnp.zeros((3, MH), f32), ghead[:3, :heads], me * heads, 1
        )
        rest = jnp.concatenate(
            [
                grad_conv.reshape(KW + 1, devices, -1).transpose(1, 0, 2).reshape(devices, -1),
                jnp.broadcast_to(grad_head.reshape(1, -1), (devices, 3 * MH)),
            ],
            axis=1,
        )
        rest = jnp.pad(rest, ((0, 0), (0, held * rest_cols - rest_size)))
        return rest.reshape(width, rest_cols)

    dearly, dlate, grad_norm1 = [], [], []
    gconv, ghead = 0.0, 0.0
    for s in range(seqs):
        grad_mixed_in = dot_last(grad_mix[s], w_out)
        if s == seqs - 1:
            grad_w_out = sum(map(dot_first, mixed_in, grad_mix)).astype(bf16)
            grad_mixed_in, grad_w_out = lax.optimization_barrier((grad_mixed_in, grad_w_out))
            grad_w_out = scatter_dp(grad_w_out, 1)
            if groups > 1:
                grad_w_out = lax.psum(grad_w_out, "g")
            grad_w_out = grad_w_out.astype(bf16)
        if s == 0:
            grad_mixed_in, local = lax.optimization_barrier((grad_mixed_in, local))
            if seqs > 1:
                grad_mix.append(lax.all_gather(local, TEAM, axis=0, tiled=True))
            ffn = [scatter_near(near) for near in after(ffn, local)]
            mixed = [(hidden[n] + valid[n] * ffn[n]).astype(bf16) for n in range(seqs)]
            mixed = jnp.stack(mixed)
        dq, dk, dv = attend_back(lengths, start, q, k, v, grad_mixed_in, logs[s], span, s)
        if groups > 1:
            dk = lax.psum_scatter(dk, "g", scatter_dimension=1, tiled=True)
            dv = lax.psum_scatter(dv, "g", scatter_dimension=1, tiled=True)
        dq = rotate_back(dq[0], cosine, sine).astype(bf16)
        dk = rotate_back(dk[0], cosine, sine).astype(bf16)
        z = early[s * block_len : (s + 1) * block_len, :inner]
        sig_z = sigmoid(z)
        dz = grad_mixed_in[:, :inner] * ys[s] * (sig_z * (1.0 + z * (1.0 - sig_z)))
        dearly.append(jnp.concatenate([dz.astype(bf16), dq, dk, dv[0].astype(bf16)], axis=1))
        if s == seqs - 1:
            grad_early = dot_first(norm1, jnp.concatenate(dearly, axis=0)).astype(bf16)
            early_cuts = cuts_dp(grad_early, 0)
            grad_w_out = jnp.concatenate(
                [
                    grad_w_out[inner:].reshape(part, attn_rows, cut),
                    grad_w_out[:inner].reshape(part, mamba_rows, cut),
                ],
                axis=1,
            )
            grad_w_out = lax.dynamic_update_slice_in_dim(
                jnp.zeros((seq_size, out_rows, cut), bf16), grad_w_out, (me % ratio) * part, 0
            )
            grad_w_gu = lax.all_to_all(
                grad_w_gu.reshape(plane, held, 2 * line * ffn_block), PLANE, 0, 0, tiled=True
            )
            grad_mixed_in, early_cuts, grad_w_out, grad_w_gu = lax.optimization_barrier(
                (grad_mixed_in, early_cuts, grad_w_out, grad_w_gu)
            )
            grad_early = sum_cuts(early_cuts)
            grad_w_out = lax.all_to_all(grad_w_out, SEQ, 0, 0, tiled=True)
        back = functools.partial(core_back, seq=s, heads=heads, span=span)
        halo = halos[s : s + 1]
        dlate_s, gconv_s, ghead_s, dinit, dfirst = back(
            turn, early, late, grad_mixed_in, enters[s], halo, conv_own, head_own, nothing
        )
        if groups > 1:
            leave = entering(decays[s], dinit, True)
            dlate_s, gconv_s, ghead_s, dinit, dfirst = back(
                turn, early, late, grad_mixed_in, enters[s], halo, conv_own, head_own, leave
            )
            padded = jnp.concatenate([jnp.zeros((1, KW - 1, wide), f32), dfirst], axis=1)
            rim = sum(
                conv_own[j][None, None] * padded[:, KW - 1 - j : 2 * (KW - 1) - j]
                for j in range(KW)
            )
            rim = passed_along(rim.astype(bf16), -1).astype(f32)
            rim = jnp.pad(rim[0], ((block_len - KW + 1, 0), (0, 0)))
            step_gap = jnp.zeros((block_len, 128), f32)
            rim = jnp.concatenate([rim[:, :inner], step_gap, rim[:, inner:]], axis=1)
            dlate_s = (dlate_s.astype(f32) + rim).astype(bf16)
        gconv, ghead = gconv + gconv_s, ghead + ghead_s
        if s == 0:
            dlate_s, norm2, act = lax.optimization_barrier((dlate_s, norm2, act))
            grad_w_gu = sum(map(dot_first, norm2, grad_gu)).astype(bf16)
            grad_w_gu = grad_w_gu.reshape(dp, line, plane // dp, held, 2 * line * ffn_block)
            grad_w_gu = grad_w_gu.transpose(1, 0, 2, 3, 4).reshape(width, -1)
            dlate_s, grad_w_gu = lax.optimization_barrier((dlate_s, grad_w_gu))
            grad_w_gu = lax.psum_scatter(grad_w_gu, LINE, scatter_dimension=0, tiled=True)
        if s == seqs - 1:
            dlate_s, grad_early, grad_w_out = lax.optimization_barrier(
                (dlate_s, grad_early, grad_w_out)
            )
            grad_late = dot_first(norm1, jnp.concatenate([*dlate, dlate_s], axis=0))
            rest_at = inner + MH
            grad_late = grad_late + jnp.pad(
                small_grads(gconv, ghead),
                ((0, 0), (rest_at, grad_late.shape[1] - rest_at - rest_cols)),
            )
            late_cuts = cuts_dp(grad_late.astype(bf16), 0)
            dlate_s, late_cuts = lax.optimization_barrier((dlate_s, late_cuts))
            grad_late = sum_cuts(late_cuts)
        dlate.append(dlate_s)
        partial = (dot_last(dearly[s], w_early) + dot_last(dlate_s, w_late)).astype(bf16)
        if s == seqs - 1:
            grad_w_out = grad_w_out.reshape(groups, dp, ratio, out_rows, cut)[0]
            grad_w_out = lax.dynamic_index_in_dim(grad_w_out, my_seq // part, 1, keepdims=False)
            grad_w_out = lax.all_to_all(after(grad_w_out, partial), "dp", 0, 0, tiled=True)
            grad_w_out = grad_w_out.transpose(1, 0, 2).reshape(out_rows, width).astype(f32)
            grad_early = to_owners(grad_early)
        grad_norm1.append(lax.psum_scatter(partial, TEAM, scatter_dimension=0, tiled=True))
        if s == 0:
            grad_w_dn = sum(map(dot_first, act, after(grad_ffn, partial))).astype(bf16)
            grad_mix[1:], grad_w_dn, mixed = lax.optimization_barrier(
                (grad_mix[1:], grad_w_dn, mixed)
            )
            grad_down = lax.psum_scatter(grad_w_dn, LINE, scatter_dimension=0, tiled=True)
            grad_down = grad_down.astype(f32)
    grad_gate_up = (
        grad_w_gu.reshape(dp, plane // dp, held, 2, line, ffn_block)
        .transpose(2, 3, 0, 4, 1, 5)
        .reshape(held, -1)
        .astype(f32)
    )
    grad_late, grad_w_out, grad_early = lax.optimization_barrier(
        (grad_late, grad_w_out, grad_early)
    )
    grad_late = to_owners(grad_late)
    grad_z = grad_early[:, :, :inner].reshape(held, MI)
    grad_query = grad_early[:, :, inner:key_at].reshape(held, -1)
    grad_keyval = grad_early[:, :, key_at:].reshape(held, KV, team // KV, 2, HD)
    grad_keyval = jnp.sum(grad_keyval, axis=2).transpose(0, 2, 1, 3).reshape(held, -1)
    grad_x = grad_late[:, :, :inner].reshape(held, MI)
    grad_dt = jnp.sum(grad_late[:, :, inner : inner + MH], axis=1)
    grad_bc = jnp.sum(grad_late[:, :, inner + 128 :], axis=1)
    grad_in = jnp.concatenate([grad_z, grad_x, grad_bc], axis=1)

    grad_gains = [
        jnp.sum(w_in.astype(f32) * grad_in, 1)
        + jnp.sum(w_query.astype(f32) * grad_query, 1)
        + jnp.sum(w_keyval.astype(f32) * grad_keyval, 1)
        + jnp.sum(w_dt.astype(f32) * grad_dt, 1),
        jnp.sum(w_gate_up.astype(f32) * grad_gate_up, 1),
    ]
    grad_gains = jnp.stack(grad_gains) / gains.astype(f32)
    rest = jnp.sum(grad_late[:, :, rest_at : rest_at + rest_cols], axis=1).reshape(-1)
    conv_end = (KW + 1) * own_conv
    grad_conv = rest[:conv_end].reshape(KW + 1, own_conv)
    head_total = rest[conv_end:rest_size].reshape(3, MH)
    grad_tokens = []
    for s in range(seqs):
        _, norm1_pull = jax.vjp(lambda v: rms_norm(v, gain_all[0]), tokens[s].astype(f32))
        (grad_token_norm,) = norm1_pull(grad_norm1[s].astype(f32))
        grad_tokens.append((grad_hidden[s] + grad_token_norm).astype(bf16))
    grad_tokens = jnp.stack(grad_tokens)
    grad_attn_out, grad_mamba_out = grad_w_out[:attn_rows], grad_w_out[attn_rows:]
    return (
        mixed,
        grad_tokens,
        grad_gains,
        grad_query,
        grad_keyval,
        grad_attn_out,
        grad_in,
        grad_dt,
        grad_conv,
        head_total[:2],
        head_total[2],
        grad_mamba_out,
        grad_gate_up,
        grad_down,
    )


def solution(mesh):
    dp, seq = mesh.shape["dp"], mesh.shape["seq"]
    team = math.gcd(math.gcd(HQ, MH), seq)
    split = Mesh(mesh.devices.reshape(dp, seq // team, team // 2, 2), ALL)
    rows = P(ALL, None)
    cols = P(None, ALL)
    acts = P("dp", SEQ, None)
    return jax.shard_map(
        body,
        mesh=split,
        in_specs=(
            acts, P("dp"), cols, rows, rows, rows, rows, rows, cols, P(), rows, rows, rows, acts,
        ),
        out_specs=(
            acts, acts, cols, rows, rows, rows, rows, rows, cols, P(), P(), rows, rows, rows,
        ),
        check_vma=False,
    )
```

```python
import functools
import math

import jax
import jax.numpy as jnp
from jax import lax
from jax.experimental import pallas as pl
from jax.experimental.pallas import tpu as pltpu
from jax.sharding import Mesh
from jax.sharding import PartitionSpec as P

HQ = 8
KV = 2
HD = 128
MH = 48
MP = 64
NS = 256
KW = 4
MI = MH * MP

epsilon = 1e-05
rope_base = 100000000000.0
neg_big = -1e30
highest = lax.Precision.HIGHEST
bf16 = jnp.bfloat16
f32 = jnp.float32

ALL = ("dp", "g", "z", "c")
TEAM = ("z", "c")
PLANE = ("dp", "c")
LINE = ("g", "z")
SEQ = ("g", "z", "c")
SPREAD = ("dp", "g")


def rms_norm(values, gain):
    return values * lax.rsqrt(jnp.mean(values * values, -1, keepdims=True) + epsilon) * gain


def rope_tables(positions, head_size):
    half = head_size // 2
    freq = jnp.exp(jnp.arange(half, dtype=f32) * (-2.0 * math.log(rope_base) / head_size))
    angle = positions.astype(f32)[:, None] * freq[None, :]
    return (
        jnp.concatenate([jnp.cos(angle), jnp.cos(angle)], -1),
        jnp.concatenate([jnp.sin(angle), jnp.sin(angle)], -1),
    )


def rotate(values, cosine, sine):
    half = values.shape[-1] // 2
    turned = jnp.concatenate([-values[..., half:], values[..., :half]], -1)
    return values * cosine + turned * sine


def rotate_back(grads, cosine, sine):
    half = grads.shape[-1] // 2
    scaled = grads * sine
    return grads * cosine + jnp.concatenate([scaled[..., half:], -scaled[..., :half]], -1)


def dot(left, right, precision=None):
    return jnp.dot(left, right, preferred_element_type=f32, precision=precision)


def dot_first(left, right, precision=None):
    return lax.dot_general(
        left, right, (((0,), (0,)), ((), ())), preferred_element_type=f32, precision=precision
    )


def dot_last(left, right, precision=None):
    return lax.dot_general(
        left, right, (((1,), (1,)), ((), ())), preferred_element_type=f32, precision=precision
    )


def sigmoid(v):
    return 1.0 / (1.0 + jnp.exp(-v))


def softplus(v):
    return jnp.maximum(v, 0.0) + jnp.log(1.0 + jnp.exp(-jnp.abs(v)))


def cost(rows, gigaflops, arrays):
    return pl.CostEstimate(
        flops=int(rows * gigaflops * 1e9 / 2048),
        bytes_accessed=sum(a.size * a.dtype.itemsize for a in arrays),
        transcendentals=0,
    )


def params(count):
    return pltpu.CompilerParams(
        dimension_semantics=("arbitrary",) * count, vmem_limit_bytes=48 * 1024 * 1024
    )


def after(value, *others):
    return lax.optimization_barrier((value, *others))[0]


def assemble(scalars, sources, shapes, plan, count, name):
    def kernel(scalar_ref, *refs):
        sems = refs[-1]
        plan(scalar_ref, refs[: len(sources)], refs[len(sources) : -1], sems)

    anywhere = pl.BlockSpec(memory_space=pl.ANY)
    return pl.pallas_call(
        kernel,
        in_specs=[pl.BlockSpec(memory_space=pltpu.SMEM)] + [anywhere] * len(sources),
        out_specs=[pl.BlockSpec(memory_space=pltpu.VMEM)] * len(shapes),
        out_shape=[jax.ShapeDtypeStruct(shape, bf16) for shape in shapes],
        scratch_shapes=[pltpu.SemaphoreType.DMA((count,))],
        compiler_params=pltpu.CompilerParams(vmem_limit_bytes=48 * 1024 * 1024),
        cost_estimate=pl.CostEstimate(
            flops=0, bytes_accessed=4 * sum(math.prod(shape) for shape in shapes), transcendentals=0
        ),
        name=name,
    )(jnp.stack([jnp.asarray(v, jnp.int32) for v in scalars]), *sources)


def run_copies(pairs, sems):
    copies = [pltpu.make_async_copy(a, b, sems.at[i]) for i, (a, b) in enumerate(pairs)]
    for copy in copies:
        copy.start()
    for copy in copies:
        copy.wait()


def join_weights(blocks, others, inner, key_at, shared, kv_head):
    peers, here = lax.axis_size("dp"), lax.axis_index("dp")
    size = sum(part.shape[0] for part, k, _ in blocks if k == 0)
    width = size * peers
    own = inner + key_at
    keys_size = 2 * KV * HD
    many = len(blocks)

    def plan(scalar_ref, sources, outs, sems):
        early, late, rest = outs

        def pairs(turned):
            moves = []
            for i, (part, k, first) in enumerate(blocks):
                rows = part.shape[0]
                at = pl.ds(pl.multiple_of(scalar_ref[k] * size + first, rows), rows)
                source = sources[i]
                near, far = source.at[:, pl.ds(own, shared)], sources[many + i]
                steps, keys = (far, near) if turned else (near, far)
                moves.append((source.at[:, pl.ds(0, key_at)], early.at[at, pl.ds(0, key_at)]))
                moves.append((source.at[:, pl.ds(key_at, inner)], late.at[at, pl.ds(0, inner)]))
                moves.append((steps, late.at[at, pl.ds(inner, shared)]))
                for j in range(2):
                    lane = (j * KV + scalar_ref[peers]) * HD
                    if not turned:
                        keys_at = pl.multiple_of(lane, HD)
                        key_view = keys.at[:, pl.ds(keys_at, HD)]
                    else:
                        key_view = source.at[:, pl.ds(pl.multiple_of(own + lane, HD), HD)]
                    moves.append((key_view, early.at[at, pl.ds(key_at + j * HD, HD)]))
                tail = far if not turned else source
                tail_at = keys_size if not turned else own + keys_size
                moves.append((tail.at[:, pl.ds(tail_at, 128)], rest.at[at, :]))
            return moves

        @pl.when(scalar_ref[peers + 1] == 0)
        def _():
            run_copies(pairs(False), sems)

        @pl.when(scalar_ref[peers + 1] != 0)
        def _():
            run_copies(pairs(True), sems)

    scalars = [here ^ k for k in range(peers)] + [kv_head, lax.axis_index("c")]
    shapes = [(width, key_at + 2 * HD), (width, inner + shared), (width, shared - keys_size)]
    sources = [part for part, _, _ in blocks] + others
    return assemble(scalars, sources, shapes, plan, 6 * many, "join_weights")


def join_hidden(gathered, count, held, dp, width):
    line, _, columns = gathered.shape
    low = count * held
    rows = (gathered.shape[1] - low) * columns // width
    folds = width // columns

    def plan(scalar_ref, sources, outs, sems):
        moves = [
            (
                sources[0].at[:, pl.ds(i * held, held)],
                outs[0].at[scalar_ref[i], :, scalar_ref[count + i]],
            )
            for i in range(count)
        ]
        for i in range(folds):
            moves.append(
                (
                    sources[0].at[:, pl.ds(low + i * rows, rows)],
                    outs[1].at[:, :, pl.ds(i * columns, columns)],
                )
            )
        run_copies(moves, sems)

    near, core = lax.axis_index("dp"), lax.axis_index("c")
    scalars = [near ^ (i % dp) for i in range(count)] + [core ^ (i // dp) for i in range(count)]
    shapes = [(dp, line, count // dp, held, columns), (line, rows, width)]
    return assemble(scalars, [gathered], shapes, plan, count + folds, "join_hidden")


def join_rows(slots, place):
    count, rows, width = len(slots), *slots[0].shape

    def plan(scalar_ref, sources, outs, sems):
        run_copies([(sources[k], outs[0].at[scalar_ref[k]]) for k in range(count)], sems)

    scalars = [place ^ k for k in range(count)]
    whole = assemble(scalars, slots, [(count, rows, width)], plan, count, "join_rows")[0]
    return whole.reshape(count * rows, width)


def join_columns(pieces):
    peers, here = lax.axis_size("dp"), lax.axis_index("dp")
    rows, cut = pieces[0].shape

    def plan(scalar_ref, sources, outs, sems):
        run_copies(
            [
                (sources[k], outs[0].at[:, pl.ds(pl.multiple_of(scalar_ref[k] * cut, cut), cut)])
                for k in range(peers)
            ],
            sems,
        )

    scalars = [here ^ k for k in range(peers)]
    return assemble(scalars, pieces, [(rows, cut * peers)], plan, peers, "join_columns")[0]


def join_out(blocks, place, attn_rows, mamba_rows):
    peers, here = lax.axis_size("dp"), lax.axis_index("dp")
    parts, rows, cut = blocks[0].shape

    def plan(scalar_ref, sources, outs, sems):
        moves = []
        for k in range(peers):
            lane = pl.ds(pl.multiple_of(scalar_ref[k] * cut, cut), cut)
            for i in range(parts):
                at = scalar_ref[peers + i]
                low = pl.multiple_of(at * mamba_rows, 16)
                high = pl.multiple_of(parts * mamba_rows + at * attn_rows, 16)
                moves.append(
                    (
                        sources[k].at[i, pl.ds(attn_rows, mamba_rows)],
                        outs[0].at[pl.ds(low, mamba_rows), lane],
                    )
                )
                moves.append(
                    (
                        sources[k].at[i, pl.ds(0, attn_rows)],
                        outs[0].at[pl.ds(high, attn_rows), lane],
                    )
                )
        run_copies(moves, sems)

    scalars = [here ^ k for k in range(peers)] + [place ^ i for i in range(parts)]
    shape = (parts * rows, cut * peers)
    return assemble(scalars, blocks, [shape], plan, 2 * peers * parts, "join_out")[0]


def join_blocks(blocks):
    rows, width = blocks[0].shape

    def plan(scalar_ref, sources, outs, sems):
        run_copies(
            [(source, outs[0].at[pl.ds(i * rows, rows)]) for i, source in enumerate(sources)], sems
        )

    count = len(blocks)
    return assemble([0], blocks, [(count * rows, width)], plan, count, "join_blocks")[0]


def swap(block, axis, distance):
    return lax.ppermute(block, axis, [(i, i ^ distance) for i in range(lax.axis_size(axis))])


def gather_core(near):
    return join_blocks(near + [swap(piece, "c", 1) for piece in near])


def gather_plane(block):
    return gather_core(from_dp(block))


def scatter_core(partial):
    half = partial.shape[0] // 2
    near = partial[:half].astype(f32) + swap(partial[half:], "c", 1).astype(f32)
    return near.astype(bf16)


def scatter_near(near):
    near = jnp.split(near, lax.axis_size("dp"), axis=0)
    return sum(
        (swap(near[k], "dp", k) if k else near[k]).astype(f32) for k in range(len(near))
    )


def scatter_plane(partial):
    return scatter_near(scatter_core(partial))


def from_dp(block):
    return [block] + [swap(block, "dp", k) for k in range(1, lax.axis_size("dp"))]


def parts_dp(block):
    if lax.axis_size("dp") != 4:
        return [(part, k, 0) for k, part in enumerate(from_dp(block))]
    half = block.shape[0] // 2
    one, two = swap(block, "dp", 1), swap(block, "dp", 2)
    top, bottom = swap(one[:half], "dp", 2), swap(two[half:], "dp", 1)
    return [(block, 0, 0), (one, 1, 0), (two, 2, 0), (top, 3, 0), (bottom, 3, half)]


def cuts_dp(partial, axis):
    peers, here = lax.axis_size("dp"), lax.axis_index("dp")
    size = partial.shape[axis] // peers
    return [lax.dynamic_slice_in_dim(partial, (here ^ k) * size, size, axis) for k in range(peers)]


def sum_cuts(cuts):
    return sum((swap(cut, "dp", k) if k else cut).astype(f32) for k, cut in enumerate(cuts))


def scatter_dp(partial, axis):
    return sum_cuts(cuts_dp(partial, axis))


def attend_mask(length_ref, start_ref, seq, block, width, first):
    qpos = start_ref[0] + first + lax.broadcasted_iota(jnp.int32, (block, width), 0)
    kpos = lax.broadcasted_iota(jnp.int32, (block, width), 1)
    return (kpos <= qpos) & (kpos < length_ref[seq])


def attend_fore_kernel(
    length_ref, start_ref, q_ref, k_ref, v_ref, o_ref, log_ref, *, scale, block, seq
):
    at = pl.program_id(0)
    keys = k_ref[0]
    scores = dot_last(q_ref[0], keys) * scale
    allowed = attend_mask(length_ref, start_ref, seq, block, keys.shape[0], at * block)
    scores = jnp.where(allowed, scores, neg_big)
    top = jnp.max(scores, -1, keepdims=True)
    expo = jnp.exp(scores - top)
    total = jnp.sum(expo, -1, keepdims=True)
    prob = (expo * (1.0 / total)).astype(bf16)
    o_ref[0] = dot(prob, v_ref[0]).astype(bf16)
    log_ref[0] = jnp.broadcast_to(top + jnp.log(total), log_ref.shape[1:])


def attend_fore(length, start, q, k, v, block, seq):
    _, rows, width = q.shape
    kernel = functools.partial(
        attend_fore_kernel, scale=1.0 / math.sqrt(HD), block=block, seq=seq
    )
    qspec = pl.BlockSpec((1, block, width), lambda i: (seq, i, 0))
    ospec = pl.BlockSpec((1, block, width), lambda i: (0, i, 0))
    kspec = pl.BlockSpec((1, k.shape[1], width), lambda i: (seq, 0, 0))
    smem = pl.BlockSpec(memory_space=pltpu.SMEM)
    return pl.pallas_call(
        kernel,
        grid=(rows // block,),
        in_specs=[smem, smem, qspec, kspec, kspec],
        out_specs=[ospec, ospec],
        out_shape=[
            jax.ShapeDtypeStruct((1, rows, width), bf16),
            jax.ShapeDtypeStruct((1, rows, width), f32),
        ],
        compiler_params=params(1),
        cost_estimate=cost(rows, 7, (q, k, v)),
        name="attend_fore",
    )(length, start, q, k, v)


def attend_back_kernel(
    length_ref, start_ref, q_ref, k_ref, v_ref, do_ref, log_ref, dq_ref, dk_ref, dv_ref,
    *, scale, block, seq,
):
    at = pl.program_id(0)

    @pl.when(at == 0)
    def _():
        dk_ref[...] = jnp.zeros_like(dk_ref)
        dv_ref[...] = jnp.zeros_like(dv_ref)

    keys = k_ref[0]
    queries = q_ref[0]
    grad_out = do_ref[0].astype(bf16)
    scores = dot_last(queries, keys) * scale
    allowed = attend_mask(length_ref, start_ref, seq, block, keys.shape[0], at * block)
    scores = jnp.where(allowed, scores, neg_big)
    prob = jnp.exp(scores - log_ref[0][:, :1])
    grad_prob = dot_last(grad_out, v_ref[0])
    centre = jnp.sum(prob * grad_prob, -1, keepdims=True)
    grad_score = (prob * (grad_prob - centre)).astype(bf16)
    dq_ref[0] = dot(grad_score, keys) * scale
    dk_ref[0] += dot_first(grad_score, queries) * scale
    dv_ref[0] += dot_first(prob.astype(bf16), grad_out)


def attend_back(length, start, q, k, v, grad_out, logs, block, seq):
    _, rows, width = q.shape
    out_at = grad_out.shape[1] // width - 1
    kernel = functools.partial(
        attend_back_kernel, scale=1.0 / math.sqrt(HD), block=block, seq=seq
    )
    qspec = pl.BlockSpec((1, block, width), lambda i: (seq, i, 0))
    ospec = pl.BlockSpec((1, block, width), lambda i: (0, i, 0))
    kspec = pl.BlockSpec((1, k.shape[1], width), lambda i: (seq, 0, 0))
    gspec = pl.BlockSpec((1, k.shape[1], width), lambda i: (0, 0, 0))
    smem = pl.BlockSpec(memory_space=pltpu.SMEM)
    return pl.pallas_call(
        kernel,
        grid=(rows // block,),
        in_specs=[
            smem,
            smem,
            qspec,
            kspec,
            kspec,
            pl.BlockSpec((1, block, width), lambda i: (0, i, out_at)),
            ospec,
        ],
        out_specs=[ospec, gspec, gspec],
        out_shape=[
            jax.ShapeDtypeStruct((1, rows, width), f32),
            jax.ShapeDtypeStruct((1, *k.shape[1:]), f32),
            jax.ShapeDtypeStruct((1, *k.shape[1:]), f32),
        ],
        compiler_params=params(1),
        cost_estimate=cost(rows, 11, (q, k, v, logs)),
        name="attend_back",
    )(length, start, q, k, v, grad_out[None], logs)


def head_spread(heads):
    row = lax.broadcasted_iota(jnp.int32, (128, heads * MP), 0)
    col = lax.broadcasted_iota(jnp.int32, (128, heads * MP), 1)
    return (row == col // MP).astype(f32)


def triangle(span):
    row = lax.broadcasted_iota(jnp.int32, (span, span), 0)
    col = lax.broadcasted_iota(jnp.int32, (span, span), 1)
    return row >= col


def conv_pre(ext_ref, conv_ref, span):
    total = conv_ref[KW : KW + 1, :]
    for k in range(KW):
        total = total + conv_ref[k : k + 1, :] * ext_ref[pl.ds(8 - (KW - 1) + k, span), :]
    return total


def core_fore_kernel(
    turn_ref, x_ref, bc_ref, z_ref, dt_ref, halo_ref, conv_ref, head_ref, init_ref,
    gated_ref, y_ref, enter_ref, final_ref, decay_ref,
    ext, state, total, *, heads, span,
):
    inner = heads * MP
    at = pl.program_id(0)

    @pl.when(at == 0)
    def _():
        ext[0:8, :] = halo_ref[0]
        state[...] = init_ref[0]
        total[...] = jnp.zeros_like(total)

    ext[8:, :inner] = x_ref[...]
    ext[8:, inner:] = bc_ref[...]
    pre = conv_pre(ext, conv_ref, span)
    ext[0:8, :] = ext[span : span + 8, :]
    cv = pre * sigmoid(pre)
    xs = cv[:, :inner]
    bmat = cv[:, inner : inner + NS].astype(bf16)
    cmat = cv[:, inner + NS :].astype(bf16)
    spread = head_spread(heads)
    lower = triangle(span)
    step = softplus(pltpu.roll(dt_ref[...], 128 - turn_ref[0], 1) + head_ref[0:1, :])
    decay_log = -jnp.exp(head_ref[1:2, :]) * step
    cum = dot(lower.astype(f32), decay_log, highest)
    cum_t = cum.T
    step_t = step.T
    last = cum[span - 1 : span, :]
    enter = state[...]
    enter_ref[0, 0] = enter
    pair = dot_last(cmat, bmat)
    xb = xs.astype(bf16)
    parts = []
    for h in range(heads):
        diff = cum[:, h : h + 1] - cum_t[h : h + 1, :]
        decay = jnp.exp(jnp.where(lower, diff, neg_big))
        mixing = (pair * decay * step_t[h : h + 1, :]).astype(bf16)
        parts.append(dot(mixing, xb[:, h * MP : (h + 1) * MP]))
    y = jnp.concatenate(parts, axis=1)
    y = y + dot_last(cmat, enter.astype(bf16)) * dot(jnp.exp(cum), spread, highest)
    y = y + xs * dot(jnp.broadcast_to(head_ref[2:3, :], (8, 128)), spread, highest)[0:1, :]
    tail = dot(jnp.exp(last - cum) * step, spread, highest)
    keep = jnp.broadcast_to(jnp.exp(cum_t[:, span - 1 : span]), (128, NS))
    new_state = dot_first(spread, keep, highest) * enter + dot_first((xs * tail).astype(bf16), bmat)
    state[...] = new_state
    final_ref[0] = new_state
    total[...] = total[...] + last
    decay_ref[0] = total[...]
    z = z_ref[...]
    y_ref[...] = y
    gated_ref[...] = (y * (z * sigmoid(z))).astype(bf16)


def core_fore(turn, early, late, halo, conv, head, init, seq, rows, heads, span):
    inner = heads * MP
    wide = inner + 2 * NS
    count = rows // span
    first = seq * count

    def block(width, at):
        return pl.BlockSpec((span, width), lambda i: (first + i, at))

    def whole(*shape):
        return pl.BlockSpec(shape, lambda i: (0,) * len(shape))

    out = pl.BlockSpec((span, inner), lambda i: (i, 0))
    return pl.pallas_call(
        functools.partial(core_fore_kernel, heads=heads, span=span),
        grid=(count,),
        in_specs=[
            pl.BlockSpec(memory_space=pltpu.SMEM),
            block(inner, 0),
            block(2 * NS, (inner + 128) // (2 * NS)),
            block(inner, 0),
            block(128, inner // 128),
            whole(1, 8, wide),
            whole(8, wide),
            whole(8, 128),
            whole(1, inner, NS),
        ],
        out_specs=[
            out,
            out,
            pl.BlockSpec((1, 1, inner, NS), lambda i: (0, i, 0, 0)),
            whole(1, inner, NS),
            whole(1, 8, 128),
        ],
        out_shape=[
            jax.ShapeDtypeStruct((rows, inner), bf16),
            jax.ShapeDtypeStruct((rows, inner), f32),
            jax.ShapeDtypeStruct((1, count, inner, NS), f32),
            jax.ShapeDtypeStruct((1, inner, NS), f32),
            jax.ShapeDtypeStruct((1, 8, 128), f32),
        ],
        scratch_shapes=[
            pltpu.VMEM((span + 8, wide), f32),
            pltpu.VMEM((inner, NS), f32),
            pltpu.VMEM((8, 128), f32),
        ],
        compiler_params=params(1),
        cost_estimate=cost(rows, 26, (late, init)),
        name="core_fore",
    )(turn, late, late, early, late, halo, conv, head, init)


def core_back_kernel(
    turn_ref, x_ref, bc_ref, z_ref, dt_ref, dg_ref, enter_ref, halo_ref, conv_ref, head_ref, exit_ref,
    dlate_ref, gconv_ref, ghead_ref, dinit_ref, dfirst_ref,
    ext, dext, dstate, *, heads, span,
):
    inner = heads * MP
    at = pl.program_id(0)

    @pl.when(at == 0)
    def _():
        gconv_ref[...] = jnp.zeros_like(gconv_ref)
        ghead_ref[...] = jnp.zeros_like(ghead_ref)

    @pl.when(at == 0)
    def _():
        dext[span:, :] = jnp.zeros((8, dext.shape[1]), f32)
        dstate[...] = exit_ref[0]

    ext[0:8, :] = halo_ref[0, 0]
    ext[8:, :inner] = x_ref[...]
    ext[8:, inner:] = bc_ref[...]
    pre = conv_pre(ext, conv_ref, span)
    gate = sigmoid(pre)
    cv = pre * gate
    xs = cv[:, :inner]
    bmat = cv[:, inner : inner + NS].astype(bf16)
    cmat = cv[:, inner + NS :].astype(bf16)
    xb = xs.astype(bf16)
    z = z_ref[...]
    dy = dg_ref[...] * (z * sigmoid(z))
    dyb = dy.astype(bf16)
    spread = head_spread(heads)
    lower = triangle(span)
    raw = pltpu.roll(dt_ref[...], 128 - turn_ref[0], 1) + head_ref[0:1, :]
    step = softplus(raw)
    rate = -jnp.exp(head_ref[1:2, :])
    decay_log = rate * step
    cum = dot(lower.astype(f32), decay_log, highest)
    cum_t = cum.T
    step_t = step.T
    last = cum[span - 1 : span, :]
    enter = enter_ref[0, 0]
    leave = dstate[...]
    pair = dot_last(cmat, bmat)
    dpair = jnp.zeros((span, span), f32)
    lane = lax.broadcasted_iota(jnp.int32, (span, 128), 1)
    line = lax.broadcasted_iota(jnp.int32, (128, span), 0)
    row_sums = jnp.zeros((span, 128), f32)
    col_sums = jnp.zeros((128, span), f32)
    parts = []
    for h in range(heads):
        diff = cum[:, h : h + 1] - cum_t[h : h + 1, :]
        decay = jnp.exp(jnp.where(lower, diff, neg_big))
        now = step_t[h : h + 1, :]
        cut = slice(h * MP, (h + 1) * MP)
        dmix = dot_last(dyb[:, cut], xb[:, cut]) * decay
        both = dmix * pair
        dmix_now = dmix * now
        dpair = dpair + dmix_now
        row_sums = jnp.where(lane == h, jnp.sum(both * now, 1, keepdims=True), row_sums)
        col_sums = jnp.where(line == h, jnp.sum(both, 0, keepdims=True), col_sums)
        mixing = (pair * decay * now).astype(bf16)
        parts.append(dot_first(mixing, dyb[:, cut]))
    dxs = jnp.concatenate(parts, axis=1)
    dstep = col_sums.T
    dcum = row_sums - dstep * step
    dpb = dpair.astype(bf16)
    dcm = dot(dpb, bmat)
    dbm = dot_first(dpb, cmat)
    grown = dot(jnp.exp(cum), spread, highest)
    enter_b = enter.astype(bf16)
    leave_b = leave.astype(bf16)
    dgrown = (dy * grown).astype(bf16)
    dcum = dcum + dot_last(dy * dot_last(cmat, enter_b) * grown, spread, highest)
    dcm = dcm + dot(dgrown, enter_b)
    fade = jnp.exp(last - cum)
    tail = dot(fade * step, spread, highest)
    into = dot_last(bmat, leave_b)
    dxs = dxs + into * tail
    owed = dot_last(xs * into, spread, highest) * fade
    dstep = dstep + owed
    owed = owed * step
    dcum = dcum - owed
    dbm = dbm + dot((xs * tail).astype(bf16), leave_b)
    held = dot(spread, enter * leave, highest)
    held = dot_last(jnp.ones((8, NS), f32), held, highest)[0:1, :]
    dlast = jnp.sum(owed, 0, keepdims=True) + jnp.exp(last) * held
    keep = jnp.broadcast_to(jnp.exp(cum_t[:, span - 1 : span]), (128, NS))
    new_dstate = dot_first(spread, keep, highest) * leave + dot_first(dgrown, cmat)
    dstate[...] = new_dstate
    dinit_ref[0] = new_dstate
    dlog = dot_first(lower.astype(f32), dcum, highest) + dlast
    dstep = dstep + dlog * rate
    ddt = dstep * sigmoid(raw)
    dlate_ref[:, inner : inner + 128] = pltpu.roll(ddt, turn_ref[0], 1).astype(bf16)
    skip = dot(jnp.broadcast_to(head_ref[2:3, :], (8, 128)), spread, highest)[0:1, :]
    dxs = dxs + skip * dy
    ghead_ref[0:1, :] += jnp.sum(ddt, 0, keepdims=True)
    ghead_ref[1:2, :] += jnp.sum(dlog * decay_log, 0, keepdims=True)
    ghead_ref[2:3, :] += jnp.sum(dot_last(dy * xs, spread, highest), 0, keepdims=True)
    slope = gate * (1.0 + pre * (1.0 - gate))
    dpre = jnp.concatenate([dxs, dbm, dcm], axis=1) * slope
    dext[0:span, :] = dpre
    gconv_ref[KW : KW + 1, :] += jnp.sum(dpre, 0, keepdims=True)
    dxbc = jnp.zeros_like(dpre)
    for k in range(KW):
        dxbc = dxbc + conv_ref[k : k + 1, :] * dext[pl.ds(KW - 1 - k, span), :]
        gconv_ref[k : k + 1, :] += jnp.sum(
            dpre * ext[pl.ds(8 - (KW - 1) + k, span), :], 0, keepdims=True
        )
    dlate_ref[:, :inner] = dxbc[:, :inner].astype(bf16)
    dlate_ref[:, inner + 128 :] = dxbc[:, inner:].astype(bf16)
    dext[span:, :] = dext[0:8, :]
    dfirst_ref[0] = dext[0:8, :]


def core_back(turn, early, late, dmixed, enter, halos, conv, head, leave, seq, heads, span):
    rows = dmixed.shape[0]
    inner = heads * MP
    wide = inner + 2 * NS
    count = rows // span
    first = seq * count

    def block(width, at):
        return pl.BlockSpec((span, width), lambda i: (first + count - 1 - i, at))

    def own(width):
        return pl.BlockSpec((span, width), lambda i: (count - 1 - i, 0))

    def whole(*shape):
        return pl.BlockSpec(shape, lambda i: (0,) * len(shape))

    return pl.pallas_call(
        functools.partial(core_back_kernel, heads=heads, span=span),
        grid=(count,),
        in_specs=[
            pl.BlockSpec(memory_space=pltpu.SMEM),
            block(inner, 0),
            block(2 * NS, (inner + 128) // (2 * NS)),
            block(inner, 0),
            block(128, inner // 128),
            own(inner),
            pl.BlockSpec((1, 1, inner, NS), lambda i: (0, count - 1 - i, 0, 0)),
            pl.BlockSpec((1, 1, 8, wide), lambda i: (0, count - 1 - i, 0, 0)),
            whole(8, wide),
            whole(8, 128),
            whole(1, inner, NS),
        ],
        out_specs=[
            own(late.shape[1]),
            whole(8, wide),
            whole(8, 128),
            whole(1, inner, NS),
            whole(1, 8, wide),
        ],
        out_shape=[
            jax.ShapeDtypeStruct((rows, late.shape[1]), bf16),
            jax.ShapeDtypeStruct((8, wide), f32),
            jax.ShapeDtypeStruct((8, 128), f32),
            jax.ShapeDtypeStruct((1, inner, NS), f32),
            jax.ShapeDtypeStruct((1, 8, wide), f32),
        ],
        scratch_shapes=[
            pltpu.VMEM((span + 8, wide), f32),
            pltpu.VMEM((span + 8, wide), f32),
            pltpu.VMEM((inner, NS), f32),
        ],
        compiler_params=params(1),
        cost_estimate=cost(rows, 60, (late, enter)),
        name="core_back",
    )(turn, late, late, early, late, dmixed, enter, halos, conv, head, leave)


def passed_along(block, distance):
    devices = range(lax.axis_size("g"))
    route = [(i - distance, i) for i in devices if i - distance in devices]
    return lax.ppermute(block, "g", route)


def entering(decay, local, reverse):
    peers, here = lax.axis_size("g"), lax.axis_index("g")
    decays = lax.all_gather(decay, "g")
    locals_ = lax.all_gather(local.astype(bf16), "g")
    state = jnp.zeros_like(local)
    for k in range(peers):
        at = peers - 1 - k if reverse else k
        reached = (at > here) if reverse else (at < here)
        state = jnp.where(reached, decays[at] * state + locals_[at].astype(f32), state)
    return state


def head_decay(decay_log, heads):
    keep = jnp.exp(decay_log[:, 0, :heads])
    return jnp.repeat(keep, MP, axis=1)[:, :, None]


def body(
    tokens, lengths, gains, w_query, w_keyval, w_attn_out, w_in, w_dt, conv_params, head_params,
    w_mamba_out, w_gate_up, w_down, cotangent,
):
    seqs, rows_seq, width = tokens.shape
    dp, groups, team = lax.axis_size("dp"), lax.axis_size("g"), lax.axis_size(TEAM)
    devices, line, plane = lax.axis_size(ALL), lax.axis_size(LINE), lax.axis_size(PLANE)
    seq_size = groups * team
    me = lax.axis_index(TEAM)
    heads = MH // team
    inner = heads * MP
    query = HQ * HD // team
    block_len = rows_seq * team
    rows = seqs * block_len
    held = w_query.shape[0]
    span = math.gcd(256, block_len)
    start = (lax.axis_index("g") * block_len).astype(jnp.int32).reshape(1)
    kv_head = me * (HQ // team) * KV // HQ

    core = lax.axis_index("c")
    conv_flat = conv_params.reshape(-1)
    conv_cols = -(-conv_flat.shape[0] // held)
    conv_flat = jnp.pad(conv_flat, (0, conv_cols * held - conv_flat.shape[0]))
    shared = 128 + 2 * NS
    keys_size = 2 * KV * HD
    packed = jnp.concatenate(
        [
            jnp.pad(w_dt, ((0, 0), (0, 128 - MH))),
            w_in[:, 2 * MI :],
            w_keyval,
            gains.T,
            conv_flat.reshape(held, conv_cols),
            jnp.zeros((held, shared - keys_size - 2 - conv_cols), bf16),
        ],
        axis=1,
    )
    w_big = jnp.concatenate(
        [
            w_in[:, :MI].reshape(held, team, inner),
            w_query.reshape(held, team, query),
            w_in[:, MI : 2 * MI].reshape(held, team, inner),
            jnp.tile(packed.reshape(held, 2, shared), (1, team // 2, 1)),
        ],
        axis=2,
    ).transpose(1, 0, 2)
    slots = []
    for k in range(team):
        slot = lax.dynamic_index_in_dim(w_big, me ^ k, 0, keepdims=False)
        route = [(i, i ^ k) for i in range(team)]
        slots.append(lax.ppermute(slot, TEAM, route) if k else slot)
    w_big = slots
    ffn_block = w_down.shape[0]
    w_gu = w_gate_up.reshape(held, 2, dp, line, plane // dp, ffn_block).transpose(4, 2, 0, 1, 3, 5)
    w_gu = w_gu.reshape(plane // dp, dp, held, 2 * line * ffn_block)
    mine_dp = lax.axis_index("dp")
    slots = []
    for j in range(2):
        for k in range(dp):
            slot = lax.dynamic_slice(
                w_gu, (core ^ j, mine_dp ^ k, 0, 0), (1, 1, held, 2 * line * ffn_block)
            )[0, 0]
            if j or k:
                route = [(2 * a + b, 2 * (a ^ k) + (b ^ j)) for a in range(dp) for b in range(2)]
                slot = lax.ppermute(slot, PLANE, route)
            slots.append(slot)
    w_gu = slots
    ratio = team // dp
    part = seq_size // ratio
    attn_rows, mamba_rows = w_attn_out.shape[0], w_mamba_out.shape[0]
    out_rows = attn_rows + mamba_rows
    cut = width // dp
    w_out = jnp.concatenate([w_attn_out, w_mamba_out], axis=0)
    w_out = w_out.reshape(out_rows, dp, cut)
    quarters = []
    for k in range(dp):
        quarter = lax.dynamic_index_in_dim(w_out, mine_dp ^ k, 1, keepdims=False)
        quarters.append(swap(quarter, "dp", k) if k else quarter)
    w_big, w_gu, quarters = lax.optimization_barrier((w_big, w_gu, quarters))
    w_big = join_rows(w_big, me)
    if groups > 1:
        w_big = lax.all_gather(w_big, "g", axis=0, tiled=True)
    block_tokens = lax.all_gather(after(tokens, w_big), TEAM, axis=1, tiled=True)
    block_tokens = block_tokens.reshape(rows, width)
    positions = start[0] + jnp.arange(block_len, dtype=jnp.int32)
    cosine, sine = rope_tables(positions, HD)
    blocks = parts_dp(w_big)
    key_at = inner + query
    others = [swap(part[:, inner + key_at :], "c", 1) for part, _, _ in blocks]
    columns = 2 * line * ffn_block
    folded = [w_down[:, i * columns : (i + 1) * columns] for i in range(width // columns)]
    w_ffn = jnp.concatenate([*w_gu, *folded], axis=0)
    w_out = jnp.stack(quarters)
    others, w_ffn, w_out, cosine, sine = lax.optimization_barrier(
        (others, w_ffn, w_out, cosine, sine)
    )
    w_early, w_late, rest = join_weights(blocks, others, inner, key_at, shared, kv_head)
    gain_all = rest[:, :2].astype(f32).T
    conv_all = rest[:, 2 : 2 + conv_cols]
    conv_all = conv_all.reshape(devices, held * conv_cols)[:, : conv_params.size]
    conv_all = (
        conv_all.reshape(devices, KW + 1, -1).transpose(1, 0, 2).reshape(KW + 1, -1).astype(f32)
    )
    conv_own = jnp.concatenate(
        [lax.dynamic_slice_in_dim(conv_all, me * inner, inner, 1), conv_all[:, MI:]], axis=1
    )
    conv_own = jnp.pad(conv_own, ((0, 8 - KW - 1), (0, 0)))
    head_own = jnp.pad(
        lax.dynamic_slice_in_dim(head_params, me * heads, heads, 1), ((0, 5), (0, 128 - heads))
    )
    turn = (me * heads).astype(jnp.int32).reshape(1)
    block_tokens, w_ffn, w_early, w_late, gain_all = lax.optimization_barrier(
        (block_tokens, w_ffn, w_early, w_late, gain_all)
    )
    w_ffn = lax.all_gather(w_ffn, LINE, axis=0, tiled=False).reshape(line, -1, columns)
    my_seq = lax.axis_index(SEQ)
    w_out = after(w_out, block_tokens)
    if part == dp and groups == 1:
        parts = []
        for k in range(part):
            block = lax.dynamic_index_in_dim(w_out, mine_dp ^ (me % part) ^ k, 0, keepdims=False)
            route = [(i, ratio * ((i % part) ^ k) + i // part) for i in range(team)]
            parts.append(lax.ppermute(block, TEAM, route))
        w_out = jnp.stack(parts)
    else:
        order = mine_dp ^ jnp.arange(dp)
        w_out = jnp.take(w_out, order, axis=0)
        mine = (jnp.arange(ratio) == my_seq // part)[None, :, None, None]
        w_out = jnp.where(mine, w_out[:, None], jnp.zeros((), bf16))
        w_out = jnp.broadcast_to(
            w_out.reshape(1, team, out_rows, cut), (groups, team, out_rows, cut)
        ).reshape(-1, out_rows, cut)
        w_out = lax.all_to_all(w_out, SEQ, 0, 0, tiled=True)
        w_out = lax.dynamic_slice_in_dim(w_out, (me % ratio) * part, part, 0)
        w_out = jnp.concatenate(
            [w_out[:, attn_rows:].reshape(-1, cut), w_out[:, :attn_rows].reshape(-1, cut)], axis=0
        )

    own_positions = my_seq * rows_seq + jnp.arange(rows_seq, dtype=jnp.int32)
    valid = (own_positions[None, :] < lengths[:, None]).astype(f32)[:, :, None]
    cot = cotangent.astype(f32)

    norm1 = rms_norm(block_tokens.astype(f32), gain_all[0]).astype(bf16)
    early = dot(norm1, w_early)
    late = dot(norm1, w_late)
    early, late, w_out = lax.optimization_barrier((early, late, w_out))
    if w_out.ndim == 3:
        w_out = join_out(from_dp(w_out), me // ratio, attn_rows, mamba_rows)
    else:
        w_out = join_columns(from_dp(w_out))
    q = rotate(early[:, inner:key_at].reshape(seqs, block_len, HD), cosine, sine).astype(bf16)
    k = rotate(
        early[:, key_at : key_at + HD].reshape(seqs, block_len, HD), cosine, sine
    ).astype(bf16)
    v = early[:, key_at + HD :].reshape(seqs, block_len, HD).astype(bf16)
    if groups > 1:
        k = lax.all_gather(k, "g", axis=1, tiled=True)
        v = lax.all_gather(v, "g", axis=1, tiled=True)
    wide = inner + 2 * NS
    ends = late.reshape(seqs, block_len // span, span, -1)[:, :, span - 8 :, :]
    ends = jnp.concatenate([ends[..., :inner], ends[..., inner + 128 :]], axis=-1)
    if groups > 1:
        before = passed_along(ends[:, -1].astype(bf16), 1).astype(f32)
    else:
        before = jnp.zeros((seqs, 8, wide), f32)
    halos = jnp.concatenate([before[:, None], ends[:, :-1]], axis=1)
    nothing = jnp.zeros((1, inner, NS), f32)
    mixed_in, ys, enters, decays, logs, mix = [], [], [], [], [], []
    for s in range(seqs):
        fore = functools.partial(core_fore, seq=s, rows=block_len, heads=heads, span=span)
        halo = before[s : s + 1]
        gated, y, enter, final, decay_log = fore(
            turn, early, late, halo, conv_own, head_own, nothing
        )
        if groups > 1:
            decays.append(head_decay(decay_log, heads))
            init = entering(decays[s], final, False)
            gated, y, enter, final, _ = fore(turn, early, late, halo, conv_own, head_own, init)
        attn, log = attend_fore(lengths, start, q, k, v, span, s)
        mixed_in.append(jnp.concatenate([gated, attn[0]], axis=1))
        ys.append(y)
        enters.append(enter)
        logs.append(log)
        partial = dot(mixed_in[s], w_out).astype(bf16)
        mix.append(partial)
        if s == 0:
            early, late, _ = lax.optimization_barrier((early, late, partial))
            grad_ffn = [
                gather_plane((valid[n] * after(cot[n], partial)).astype(bf16)) for n in range(seqs)
            ]
    mix[0], mix[-1], w_ffn = lax.optimization_barrier((mix[0], mix[-1], w_ffn))
    mix = [lax.psum_scatter(partial, TEAM, scatter_dimension=0, tiled=True) for partial in mix]
    mix[0], *grad_ffn = lax.optimization_barrier((mix[0], *grad_ffn))
    w_gu, w_dn = join_hidden(w_ffn, plane, held, dp, width)
    w_gu, w_dn = w_gu.reshape(width, -1), w_dn.reshape(-1, width)

    units = w_dn.shape[0]
    hidden, norm2, act, ffn, grad_gu, grad_hidden, grad_mix = [], [], [], [], [], [], []
    def enter_ffn(s):
        hidden.append(tokens[s].astype(f32) + valid[s] * mix[s].astype(f32))
        norm2_f, pull = jax.vjp(lambda h: rms_norm(h, gain_all[1]), hidden[s])
        return norm2_f.astype(bf16), pull

    block, pull = enter_ffn(0)
    for s in range(seqs):
        near = from_dp(block)
        if s > 0:
            near, local = lax.optimization_barrier((near, local))
            grad_mix.append(lax.all_gather(local, TEAM, axis=0, tiled=True))
        norm2.append(gather_core(near))
        gate_up = dot(norm2[s], w_gu)
        gate, upper = gate_up[:, :units], gate_up[:, units:]
        sig_gate = sigmoid(gate)
        act.append((gate * sig_gate * upper).astype(bf16))
        grad_act = dot_last(grad_ffn[s], w_dn)
        grad_gate = grad_act * upper * (sig_gate * (1.0 + gate * (1.0 - sig_gate)))
        grad_upper = grad_act * gate * sig_gate
        grad_gu.append(jnp.concatenate([grad_gate, grad_upper], 1).astype(bf16))
        partial = dot_last(grad_gu[s], w_gu).astype(bf16)
        ffn.append(dot(act[s], w_dn).astype(bf16))
        near = scatter_core(partial)
        if s < seqs - 1:
            mix[s + 1] = after(mix[s + 1], partial)
            block, next_pull = enter_ffn(s + 1)
            block, near = lax.optimization_barrier((block, near))
        else:
            ffn = [scatter_core(part_ffn) for part_ffn in ffn]
            grad_mix[0], near, ffn = lax.optimization_barrier((grad_mix[0], near, ffn))
        (grad_hidden_norm,) = pull(scatter_near(near))
        if s < seqs - 1:
            pull = next_pull
        grad_hidden.append(cot[s] + grad_hidden_norm)
        local = (valid[s] * grad_hidden[s]).astype(bf16)

    own_conv = conv_params.shape[1]
    rest_size = (KW + 1) * own_conv + 3 * MH
    rest_cols = -(-rest_size // held)

    def to_owners(partial):
        if groups > 1:
            partial = lax.psum_scatter(partial, "g", scatter_dimension=0, tiled=True)
        partial = partial.astype(bf16).reshape(team, held, -1)
        return lax.all_to_all(partial, TEAM, 0, 0, tiled=True).transpose(1, 0, 2).astype(f32)

    def small_grads(gconv, ghead):
        grad_conv = jnp.concatenate(
            [
                lax.dynamic_update_slice_in_dim(
                    jnp.zeros((KW + 1, MI), f32), gconv[: KW + 1, :inner], me * inner, 1
                ),
                gconv[: KW + 1, inner:],
            ],
            axis=1,
        )
        grad_head = lax.dynamic_update_slice_in_dim(
            jnp.zeros((3, MH), f32), ghead[:3, :heads], me * heads, 1
        )
        rest = jnp.concatenate(
            [
                grad_conv.reshape(KW + 1, devices, -1).transpose(1, 0, 2).reshape(devices, -1),
                jnp.broadcast_to(grad_head.reshape(1, -1), (devices, 3 * MH)),
            ],
            axis=1,
        )
        rest = jnp.pad(rest, ((0, 0), (0, held * rest_cols - rest_size)))
        return rest.reshape(width, rest_cols)

    dearly, dlate, grad_norm1 = [], [], []
    gconv, ghead = 0.0, 0.0
    for s in range(seqs):
        grad_mixed_in = dot_last(grad_mix[s], w_out)
        if s == seqs - 1:
            grad_w_out = sum(map(dot_first, mixed_in, grad_mix)).astype(bf16)
            grad_mixed_in, grad_w_out = lax.optimization_barrier((grad_mixed_in, grad_w_out))
            grad_w_out = scatter_dp(grad_w_out, 1)
            if groups > 1:
                grad_w_out = lax.psum(grad_w_out, "g")
            grad_w_out = grad_w_out.astype(bf16)
        if s == 0:
            grad_mixed_in, local = lax.optimization_barrier((grad_mixed_in, local))
            if seqs > 1:
                grad_mix.append(lax.all_gather(local, TEAM, axis=0, tiled=True))
            ffn = [scatter_near(near) for near in after(ffn, local)]
            mixed = [(hidden[n] + valid[n] * ffn[n]).astype(bf16) for n in range(seqs)]
            mixed = jnp.stack(mixed)
        dq, dk, dv = attend_back(lengths, start, q, k, v, grad_mixed_in, logs[s], span, s)
        if groups > 1:
            dk = lax.psum_scatter(dk, "g", scatter_dimension=1, tiled=True)
            dv = lax.psum_scatter(dv, "g", scatter_dimension=1, tiled=True)
        dq = rotate_back(dq[0], cosine, sine).astype(bf16)
        dk = rotate_back(dk[0], cosine, sine).astype(bf16)
        z = early[s * block_len : (s + 1) * block_len, :inner]
        sig_z = sigmoid(z)
        dz = grad_mixed_in[:, :inner] * ys[s] * (sig_z * (1.0 + z * (1.0 - sig_z)))
        dearly.append(jnp.concatenate([dz.astype(bf16), dq, dk, dv[0].astype(bf16)], axis=1))
        if s == seqs - 1:
            grad_early = dot_first(norm1, jnp.concatenate(dearly, axis=0)).astype(bf16)
            early_cuts = cuts_dp(grad_early, 0)
            grad_w_out = jnp.concatenate(
                [
                    grad_w_out[inner:].reshape(part, attn_rows, cut),
                    grad_w_out[:inner].reshape(part, mamba_rows, cut),
                ],
                axis=1,
            )
            grad_w_out = lax.dynamic_update_slice_in_dim(
                jnp.zeros((seq_size, out_rows, cut), bf16), grad_w_out, (me % ratio) * part, 0
            )
            grad_w_gu = lax.all_to_all(
                grad_w_gu.reshape(plane, held, 2 * line * ffn_block), PLANE, 0, 0, tiled=True
            )
            grad_mixed_in, early_cuts, grad_w_out, grad_w_gu = lax.optimization_barrier(
                (grad_mixed_in, early_cuts, grad_w_out, grad_w_gu)
            )
            grad_early = sum_cuts(early_cuts)
            grad_w_out = lax.all_to_all(grad_w_out, SEQ, 0, 0, tiled=True)
        back = functools.partial(core_back, seq=s, heads=heads, span=span)
        halo = halos[s : s + 1]
        dlate_s, gconv_s, ghead_s, dinit, dfirst = back(
            turn, early, late, grad_mixed_in, enters[s], halo, conv_own, head_own, nothing
        )
        if groups > 1:
            leave = entering(decays[s], dinit, True)
            dlate_s, gconv_s, ghead_s, dinit, dfirst = back(
                turn, early, late, grad_mixed_in, enters[s], halo, conv_own, head_own, leave
            )
            padded = jnp.concatenate([jnp.zeros((1, KW - 1, wide), f32), dfirst], axis=1)
            rim = sum(
                conv_own[j][None, None] * padded[:, KW - 1 - j : 2 * (KW - 1) - j]
                for j in range(KW)
            )
            rim = passed_along(rim.astype(bf16), -1).astype(f32)
            rim = jnp.pad(rim[0], ((block_len - KW + 1, 0), (0, 0)))
            step_gap = jnp.zeros((block_len, 128), f32)
            rim = jnp.concatenate([rim[:, :inner], step_gap, rim[:, inner:]], axis=1)
            dlate_s = (dlate_s.astype(f32) + rim).astype(bf16)
        gconv, ghead = gconv + gconv_s, ghead + ghead_s
        if s == 0:
            dlate_s, norm2, act = lax.optimization_barrier((dlate_s, norm2, act))
            grad_w_gu = sum(map(dot_first, norm2, grad_gu)).astype(bf16)
            grad_w_gu = grad_w_gu.reshape(dp, line, plane // dp, held, 2 * line * ffn_block)
            grad_w_gu = grad_w_gu.transpose(1, 0, 2, 3, 4).reshape(width, -1)
            dlate_s, grad_w_gu = lax.optimization_barrier((dlate_s, grad_w_gu))
            grad_w_gu = lax.psum_scatter(grad_w_gu, LINE, scatter_dimension=0, tiled=True)
        if s == seqs - 1:
            dlate_s, grad_early, grad_w_out = lax.optimization_barrier(
                (dlate_s, grad_early, grad_w_out)
            )
            grad_late = dot_first(norm1, jnp.concatenate([*dlate, dlate_s], axis=0))
            rest_at = inner + MH
            grad_late = grad_late + jnp.pad(
                small_grads(gconv, ghead),
                ((0, 0), (rest_at, grad_late.shape[1] - rest_at - rest_cols)),
            )
            late_cuts = cuts_dp(grad_late.astype(bf16), 0)
            dlate_s, late_cuts = lax.optimization_barrier((dlate_s, late_cuts))
            grad_late = sum_cuts(late_cuts)
        dlate.append(dlate_s)
        partial = (dot_last(dearly[s], w_early) + dot_last(dlate_s, w_late)).astype(bf16)
        if s == seqs - 1:
            grad_w_out = grad_w_out.reshape(groups, dp, ratio, out_rows, cut)[0]
            grad_w_out = lax.dynamic_index_in_dim(grad_w_out, my_seq // part, 1, keepdims=False)
            grad_w_out = lax.all_to_all(after(grad_w_out, partial), "dp", 0, 0, tiled=True)
            grad_w_out = grad_w_out.transpose(1, 0, 2).reshape(out_rows, width).astype(f32)
            grad_early = to_owners(grad_early)
        grad_norm1.append(lax.psum_scatter(partial, TEAM, scatter_dimension=0, tiled=True))
        if s == 0:
            grad_w_dn = sum(map(dot_first, act, after(grad_ffn, partial))).astype(bf16)
            grad_mix[1:], grad_w_dn, mixed = lax.optimization_barrier(
                (grad_mix[1:], grad_w_dn, mixed)
            )
            grad_down = lax.psum_scatter(grad_w_dn, LINE, scatter_dimension=0, tiled=True)
            grad_down = grad_down.astype(f32)
    grad_gate_up = (
        grad_w_gu.reshape(dp, plane // dp, held, 2, line, ffn_block)
        .transpose(2, 3, 0, 4, 1, 5)
        .reshape(held, -1)
        .astype(f32)
    )
    grad_late, grad_w_out, grad_early = lax.optimization_barrier(
        (grad_late, grad_w_out, grad_early)
    )
    grad_late = to_owners(grad_late)
    grad_z = grad_early[:, :, :inner].reshape(held, MI)
    grad_query = grad_early[:, :, inner:key_at].reshape(held, -1)
    grad_keyval = grad_early[:, :, key_at:].reshape(held, KV, team // KV, 2, HD)
    grad_keyval = jnp.sum(grad_keyval, axis=2).transpose(0, 2, 1, 3).reshape(held, -1)
    grad_x = grad_late[:, :, :inner].reshape(held, MI)
    grad_dt = jnp.sum(grad_late[:, :, inner : inner + MH], axis=1)
    grad_bc = jnp.sum(grad_late[:, :, inner + 128 :], axis=1)
    grad_in = jnp.concatenate([grad_z, grad_x, grad_bc], axis=1)

    grad_gains = [
        jnp.sum(w_in.astype(f32) * grad_in, 1)
        + jnp.sum(w_query.astype(f32) * grad_query, 1)
        + jnp.sum(w_keyval.astype(f32) * grad_keyval, 1)
        + jnp.sum(w_dt.astype(f32) * grad_dt, 1),
        jnp.sum(w_gate_up.astype(f32) * grad_gate_up, 1),
    ]
    grad_gains = jnp.stack(grad_gains) / gains.astype(f32)
    rest = jnp.sum(grad_late[:, :, rest_at : rest_at + rest_cols], axis=1).reshape(-1)
    conv_end = (KW + 1) * own_conv
    grad_conv = rest[:conv_end].reshape(KW + 1, own_conv)
    head_total = rest[conv_end:rest_size].reshape(3, MH)
    grad_tokens = []
    for s in range(seqs):
        _, norm1_pull = jax.vjp(lambda v: rms_norm(v, gain_all[0]), tokens[s].astype(f32))
        (grad_token_norm,) = norm1_pull(grad_norm1[s].astype(f32))
        grad_tokens.append((grad_hidden[s] + grad_token_norm).astype(bf16))
    grad_tokens = jnp.stack(grad_tokens)
    grad_attn_out, grad_mamba_out = grad_w_out[:attn_rows], grad_w_out[attn_rows:]
    return (
        mixed,
        grad_tokens,
        grad_gains,
        grad_query,
        grad_keyval,
        grad_attn_out,
        grad_in,
        grad_dt,
        grad_conv,
        head_total[:2],
        head_total[2],
        grad_mamba_out,
        grad_gate_up,
        grad_down,
    )


def solution(mesh):
    dp, seq = mesh.shape["dp"], mesh.shape["seq"]
    team = math.gcd(math.gcd(HQ, MH), seq)
    split = Mesh(mesh.devices.reshape(dp, seq // team, team // 2, 2), ALL)
    rows = P(ALL, None)
    cols = P(None, ALL)
    acts = P("dp", SEQ, None)
    return jax.shard_map(
        body,
        mesh=split,
        in_specs=(
            acts, P("dp"), cols, rows, rows, rows, rows, rows, cols, P(), rows, rows, rows, acts,
        ),
        out_specs=(
            acts, acts, cols, rows, rows, rows, rows, rows, cols, P(), P(), rows, rows, rows,
        ),
        check_vma=False,
    )
```

```python
import functools
import math

import jax
import jax.numpy as jnp
from jax import lax
from jax.experimental import pallas as pl
from jax.experimental.pallas import tpu as pltpu
from jax.sharding import Mesh
from jax.sharding import PartitionSpec as P

HQ = 8
KV = 2
HD = 128
MH = 48
MP = 64
NS = 256
KW = 4
MI = MH * MP

epsilon = 1e-05
rope_base = 100000000000.0
neg_big = -1e30
highest = lax.Precision.HIGHEST
bf16 = jnp.bfloat16
f32 = jnp.float32

ALL = ("dp", "g", "z", "c")
TEAM = ("z", "c")
PLANE = ("dp", "c")
LINE = ("g", "z")
SEQ = ("g", "z", "c")
SPREAD = ("dp", "g")


def rms_norm(values, gain):
    return values * lax.rsqrt(jnp.mean(values * values, -1, keepdims=True) + epsilon) * gain


def rope_tables(positions, head_size):
    half = head_size // 2
    freq = jnp.exp(jnp.arange(half, dtype=f32) * (-2.0 * math.log(rope_base) / head_size))
    angle = positions.astype(f32)[:, None] * freq[None, :]
    return (
        jnp.concatenate([jnp.cos(angle), jnp.cos(angle)], -1),
        jnp.concatenate([jnp.sin(angle), jnp.sin(angle)], -1),
    )


def rotate(values, cosine, sine):
    half = values.shape[-1] // 2
    turned = jnp.concatenate([-values[..., half:], values[..., :half]], -1)
    return values * cosine + turned * sine


def rotate_back(grads, cosine, sine):
    half = grads.shape[-1] // 2
    scaled = grads * sine
    return grads * cosine + jnp.concatenate([scaled[..., half:], -scaled[..., :half]], -1)


def dot(left, right, precision=None):
    return jnp.dot(left, right, preferred_element_type=f32, precision=precision)


def dot_first(left, right, precision=None):
    return lax.dot_general(
        left, right, (((0,), (0,)), ((), ())), preferred_element_type=f32, precision=precision
    )


def dot_last(left, right, precision=None):
    return lax.dot_general(
        left, right, (((1,), (1,)), ((), ())), preferred_element_type=f32, precision=precision
    )


def sigmoid(v):
    return 1.0 / (1.0 + jnp.exp(-v))


def softplus(v):
    return jnp.maximum(v, 0.0) + jnp.log(1.0 + jnp.exp(-jnp.abs(v)))


def cost(rows, gigaflops, arrays):
    return pl.CostEstimate(
        flops=int(rows * gigaflops * 1e9 / 2048),
        bytes_accessed=sum(a.size * a.dtype.itemsize for a in arrays),
        transcendentals=0,
    )


def params(count):
    return pltpu.CompilerParams(
        dimension_semantics=("arbitrary",) * count, vmem_limit_bytes=48 * 1024 * 1024
    )


def after(value, *others):
    return lax.optimization_barrier((value, *others))[0]


def assemble(scalars, sources, shapes, plan, count, name):
    def kernel(scalar_ref, *refs):
        sems = refs[-1]
        plan(scalar_ref, refs[: len(sources)], refs[len(sources) : -1], sems)

    anywhere = pl.BlockSpec(memory_space=pl.ANY)
    return pl.pallas_call(
        kernel,
        in_specs=[pl.BlockSpec(memory_space=pltpu.SMEM)] + [anywhere] * len(sources),
        out_specs=[pl.BlockSpec(memory_space=pltpu.VMEM)] * len(shapes),
        out_shape=[jax.ShapeDtypeStruct(shape, bf16) for shape in shapes],
        scratch_shapes=[pltpu.SemaphoreType.DMA((count,))],
        compiler_params=pltpu.CompilerParams(vmem_limit_bytes=48 * 1024 * 1024),
        cost_estimate=pl.CostEstimate(
            flops=0, bytes_accessed=4 * sum(math.prod(shape) for shape in shapes), transcendentals=0
        ),
        name=name,
    )(jnp.stack([jnp.asarray(v, jnp.int32) for v in scalars]), *sources)


def run_copies(pairs, sems):
    copies = [pltpu.make_async_copy(a, b, sems.at[i]) for i, (a, b) in enumerate(pairs)]
    for copy in copies:
        copy.start()
    for copy in copies:
        copy.wait()


def join_weights(blocks, others, inner, key_at, shared, kv_head):
    peers, here = lax.axis_size("dp"), lax.axis_index("dp")
    size = sum(part.shape[0] for part, k, _ in blocks if k == 0)
    width = size * peers
    own = inner + key_at
    keys_size = 2 * KV * HD
    many = len(blocks)

    def plan(scalar_ref, sources, outs, sems):
        early, late, rest = outs

        def pairs(turned):
            moves = []
            for i, (part, k, first) in enumerate(blocks):
                rows = part.shape[0]
                at = pl.ds(pl.multiple_of(scalar_ref[k] * size + first, rows), rows)
                source = sources[i]
                near, far = source.at[:, pl.ds(own, shared)], sources[many + i]
                steps, keys = (far, near) if turned else (near, far)
                moves.append((source.at[:, pl.ds(0, key_at)], early.at[at, pl.ds(0, key_at)]))
                moves.append((source.at[:, pl.ds(key_at, inner)], late.at[at, pl.ds(0, inner)]))
                moves.append((steps, late.at[at, pl.ds(inner, shared)]))
                for j in range(2):
                    lane = (j * KV + scalar_ref[peers]) * HD
                    if not turned:
                        keys_at = pl.multiple_of(lane, HD)
                        key_view = keys.at[:, pl.ds(keys_at, HD)]
                    else:
                        key_view = source.at[:, pl.ds(pl.multiple_of(own + lane, HD), HD)]
                    moves.append((key_view, early.at[at, pl.ds(key_at + j * HD, HD)]))
                tail = far if not turned else source
                tail_at = keys_size if not turned else own + keys_size
                moves.append((tail.at[:, pl.ds(tail_at, 128)], rest.at[at, :]))
            return moves

        @pl.when(scalar_ref[peers + 1] == 0)
        def _():
            run_copies(pairs(False), sems)

        @pl.when(scalar_ref[peers + 1] != 0)
        def _():
            run_copies(pairs(True), sems)

    scalars = [here ^ k for k in range(peers)] + [kv_head, lax.axis_index("c")]
    shapes = [(width, key_at + 2 * HD), (width, inner + shared), (width, shared - keys_size)]
    sources = [part for part, _, _ in blocks] + others
    return assemble(scalars, sources, shapes, plan, 6 * many, "join_weights")


def join_hidden(gathered, count, held, dp, width):
    line, _, columns = gathered.shape
    low = count * held
    rows = (gathered.shape[1] - low) * columns // width
    folds = width // columns

    def plan(scalar_ref, sources, outs, sems):
        moves = [
            (
                sources[0].at[:, pl.ds(i * held, held)],
                outs[0].at[scalar_ref[i], :, scalar_ref[count + i]],
            )
            for i in range(count)
        ]
        for i in range(folds):
            moves.append(
                (
                    sources[0].at[:, pl.ds(low + i * rows, rows)],
                    outs[1].at[:, :, pl.ds(i * columns, columns)],
                )
            )
        run_copies(moves, sems)

    near, core = lax.axis_index("dp"), lax.axis_index("c")
    scalars = [near ^ (i % dp) for i in range(count)] + [core ^ (i // dp) for i in range(count)]
    shapes = [(dp, line, count // dp, held, columns), (line, rows, width)]
    return assemble(scalars, [gathered], shapes, plan, count + folds, "join_hidden")


def join_rows(slots, place):
    count, rows, width = len(slots), *slots[0].shape

    def plan(scalar_ref, sources, outs, sems):
        run_copies([(sources[k], outs[0].at[scalar_ref[k]]) for k in range(count)], sems)

    scalars = [place ^ k for k in range(count)]
    whole = assemble(scalars, slots, [(count, rows, width)], plan, count, "join_rows")[0]
    return whole.reshape(count * rows, width)


def join_columns(pieces):
    peers, here = lax.axis_size("dp"), lax.axis_index("dp")
    rows, cut = pieces[0].shape

    def plan(scalar_ref, sources, outs, sems):
        run_copies(
            [
                (sources[k], outs[0].at[:, pl.ds(pl.multiple_of(scalar_ref[k] * cut, cut), cut)])
                for k in range(peers)
            ],
            sems,
        )

    scalars = [here ^ k for k in range(peers)]
    return assemble(scalars, pieces, [(rows, cut * peers)], plan, peers, "join_columns")[0]


def join_out(blocks, place, attn_rows, mamba_rows):
    peers, here = lax.axis_size("dp"), lax.axis_index("dp")
    parts, rows, cut = blocks[0].shape

    def plan(scalar_ref, sources, outs, sems):
        moves = []
        for k in range(peers):
            lane = pl.ds(pl.multiple_of(scalar_ref[k] * cut, cut), cut)
            for i in range(parts):
                at = scalar_ref[peers + i]
                low = pl.multiple_of(at * mamba_rows, 16)
                high = pl.multiple_of(parts * mamba_rows + at * attn_rows, 16)
                moves.append(
                    (
                        sources[k].at[i, pl.ds(attn_rows, mamba_rows)],
                        outs[0].at[pl.ds(low, mamba_rows), lane],
                    )
                )
                moves.append(
                    (
                        sources[k].at[i, pl.ds(0, attn_rows)],
                        outs[0].at[pl.ds(high, attn_rows), lane],
                    )
                )
        run_copies(moves, sems)

    scalars = [here ^ k for k in range(peers)] + [place ^ i for i in range(parts)]
    shape = (parts * rows, cut * peers)
    return assemble(scalars, blocks, [shape], plan, 2 * peers * parts, "join_out")[0]


def join_blocks(blocks):
    rows, width = blocks[0].shape

    def plan(scalar_ref, sources, outs, sems):
        run_copies(
            [(source, outs[0].at[pl.ds(i * rows, rows)]) for i, source in enumerate(sources)], sems
        )

    count = len(blocks)
    return assemble([0], blocks, [(count * rows, width)], plan, count, "join_blocks")[0]


def swap(block, axis, distance):
    return lax.ppermute(block, axis, [(i, i ^ distance) for i in range(lax.axis_size(axis))])


def gather_core(near):
    return join_blocks(near + [swap(piece, "c", 1) for piece in near])


def gather_plane(block):
    return gather_core(from_dp(block))


def scatter_core(partial):
    half = partial.shape[0] // 2
    near = partial[:half].astype(f32) + swap(partial[half:], "c", 1).astype(f32)
    return near.astype(bf16)


def scatter_near(near):
    near = jnp.split(near, lax.axis_size("dp"), axis=0)
    return sum(
        (swap(near[k], "dp", k) if k else near[k]).astype(f32) for k in range(len(near))
    )


def scatter_plane(partial):
    return scatter_near(scatter_core(partial))


def from_dp(block):
    return [block] + [swap(block, "dp", k) for k in range(1, lax.axis_size("dp"))]


def parts_dp(block):
    if lax.axis_size("dp") != 4:
        return [(part, k, 0) for k, part in enumerate(from_dp(block))]
    half = block.shape[0] // 2
    one, two = swap(block, "dp", 1), swap(block, "dp", 2)
    top, bottom = swap(one[:half], "dp", 2), swap(two[half:], "dp", 1)
    return [(block, 0, 0), (one, 1, 0), (two, 2, 0), (top, 3, 0), (bottom, 3, half)]


def cuts_dp(partial, axis):
    peers, here = lax.axis_size("dp"), lax.axis_index("dp")
    size = partial.shape[axis] // peers
    return [lax.dynamic_slice_in_dim(partial, (here ^ k) * size, size, axis) for k in range(peers)]


def sum_cuts(cuts):
    return sum((swap(cut, "dp", k) if k else cut).astype(f32) for k, cut in enumerate(cuts))


def scatter_dp(partial, axis):
    return sum_cuts(cuts_dp(partial, axis))


def attend_mask(length_ref, start_ref, seq, block, width, first):
    qpos = start_ref[0] + first + lax.broadcasted_iota(jnp.int32, (block, width), 0)
    kpos = lax.broadcasted_iota(jnp.int32, (block, width), 1)
    return (kpos <= qpos) & (kpos < length_ref[seq])


def attend_fore_kernel(
    length_ref, start_ref, q_ref, k_ref, v_ref, o_ref, log_ref, *, scale, block, seq
):
    at = pl.program_id(0)
    keys = k_ref[0]
    scores = dot_last(q_ref[0], keys) * scale
    allowed = attend_mask(length_ref, start_ref, seq, block, keys.shape[0], at * block)
    scores = jnp.where(allowed, scores, neg_big)
    top = jnp.max(scores, -1, keepdims=True)
    expo = jnp.exp(scores - top)
    total = jnp.sum(expo, -1, keepdims=True)
    prob = (expo * (1.0 / total)).astype(bf16)
    o_ref[0] = dot(prob, v_ref[0]).astype(bf16)
    log_ref[0] = jnp.broadcast_to(top + jnp.log(total), log_ref.shape[1:])


def attend_fore(length, start, q, k, v, block, seq):
    _, rows, width = q.shape
    kernel = functools.partial(
        attend_fore_kernel, scale=1.0 / math.sqrt(HD), block=block, seq=seq
    )
    qspec = pl.BlockSpec((1, block, width), lambda i: (seq, i, 0))
    ospec = pl.BlockSpec((1, block, width), lambda i: (0, i, 0))
    kspec = pl.BlockSpec((1, k.shape[1], width), lambda i: (seq, 0, 0))
    smem = pl.BlockSpec(memory_space=pltpu.SMEM)
    return pl.pallas_call(
        kernel,
        grid=(rows // block,),
        in_specs=[smem, smem, qspec, kspec, kspec],
        out_specs=[ospec, ospec],
        out_shape=[
            jax.ShapeDtypeStruct((1, rows, width), bf16),
            jax.ShapeDtypeStruct((1, rows, width), f32),
        ],
        compiler_params=params(1),
        cost_estimate=cost(rows, 7, (q, k, v)),
        name="attend_fore",
    )(length, start, q, k, v)


def attend_back_kernel(
    length_ref, start_ref, q_ref, k_ref, v_ref, do_ref, log_ref, dq_ref, dk_ref, dv_ref,
    *, scale, block, seq,
):
    at = pl.program_id(0)

    @pl.when(at == 0)
    def _():
        dk_ref[...] = jnp.zeros_like(dk_ref)
        dv_ref[...] = jnp.zeros_like(dv_ref)

    keys = k_ref[0]
    queries = q_ref[0]
    grad_out = do_ref[0].astype(bf16)
    scores = dot_last(queries, keys) * scale
    allowed = attend_mask(length_ref, start_ref, seq, block, keys.shape[0], at * block)
    scores = jnp.where(allowed, scores, neg_big)
    prob = jnp.exp(scores - log_ref[0][:, :1])
    grad_prob = dot_last(grad_out, v_ref[0])
    centre = jnp.sum(prob * grad_prob, -1, keepdims=True)
    grad_score = (prob * (grad_prob - centre)).astype(bf16)
    dq_ref[0] = dot(grad_score, keys) * scale
    dk_ref[0] += dot_first(grad_score, queries) * scale
    dv_ref[0] += dot_first(prob.astype(bf16), grad_out)


def attend_back(length, start, q, k, v, grad_out, logs, block, seq):
    _, rows, width = q.shape
    out_at = grad_out.shape[1] // width - 1
    kernel = functools.partial(
        attend_back_kernel, scale=1.0 / math.sqrt(HD), block=block, seq=seq
    )
    qspec = pl.BlockSpec((1, block, width), lambda i: (seq, i, 0))
    ospec = pl.BlockSpec((1, block, width), lambda i: (0, i, 0))
    kspec = pl.BlockSpec((1, k.shape[1], width), lambda i: (seq, 0, 0))
    gspec = pl.BlockSpec((1, k.shape[1], width), lambda i: (0, 0, 0))
    smem = pl.BlockSpec(memory_space=pltpu.SMEM)
    return pl.pallas_call(
        kernel,
        grid=(rows // block,),
        in_specs=[
            smem,
            smem,
            qspec,
            kspec,
            kspec,
            pl.BlockSpec((1, block, width), lambda i: (0, i, out_at)),
            ospec,
        ],
        out_specs=[ospec, gspec, gspec],
        out_shape=[
            jax.ShapeDtypeStruct((1, rows, width), f32),
            jax.ShapeDtypeStruct((1, *k.shape[1:]), f32),
            jax.ShapeDtypeStruct((1, *k.shape[1:]), f32),
        ],
        compiler_params=params(1),
        cost_estimate=cost(rows, 11, (q, k, v, logs)),
        name="attend_back",
    )(length, start, q, k, v, grad_out[None], logs)


def head_spread(heads):
    row = lax.broadcasted_iota(jnp.int32, (128, heads * MP), 0)
    col = lax.broadcasted_iota(jnp.int32, (128, heads * MP), 1)
    return (row == col // MP).astype(f32)


def triangle(span):
    row = lax.broadcasted_iota(jnp.int32, (span, span), 0)
    col = lax.broadcasted_iota(jnp.int32, (span, span), 1)
    return row >= col


def conv_pre(ext_ref, conv_ref, span):
    total = conv_ref[KW : KW + 1, :]
    for k in range(KW):
        total = total + conv_ref[k : k + 1, :] * ext_ref[pl.ds(8 - (KW - 1) + k, span), :]
    return total


def core_fore_kernel(
    turn_ref, x_ref, bc_ref, z_ref, dt_ref, halo_ref, conv_ref, head_ref, init_ref,
    gated_ref, y_ref, enter_ref, final_ref, decay_ref,
    ext, state, total, *, heads, span,
):
    inner = heads * MP
    at = pl.program_id(0)

    @pl.when(at == 0)
    def _():
        ext[0:8, :] = halo_ref[0]
        state[...] = init_ref[0]
        total[...] = jnp.zeros_like(total)

    ext[8:, :inner] = x_ref[...]
    ext[8:, inner:] = bc_ref[...]
    pre = conv_pre(ext, conv_ref, span)
    ext[0:8, :] = ext[span : span + 8, :]
    cv = pre * sigmoid(pre)
    xs = cv[:, :inner]
    bmat = cv[:, inner : inner + NS].astype(bf16)
    cmat = cv[:, inner + NS :].astype(bf16)
    spread = head_spread(heads)
    lower = triangle(span)
    step = softplus(pltpu.roll(dt_ref[...], 128 - turn_ref[0], 1) + head_ref[0:1, :])
    decay_log = -jnp.exp(head_ref[1:2, :]) * step
    cum = dot(lower.astype(f32), decay_log, highest)
    cum_t = cum.T
    step_t = step.T
    last = cum[span - 1 : span, :]
    enter = state[...]
    enter_ref[0, 0] = enter
    pair = dot_last(cmat, bmat)
    xb = xs.astype(bf16)
    parts = []
    for h in range(heads):
        diff = cum[:, h : h + 1] - cum_t[h : h + 1, :]
        decay = jnp.exp(jnp.where(lower, diff, neg_big))
        mixing = (pair * decay * step_t[h : h + 1, :]).astype(bf16)
        parts.append(dot(mixing, xb[:, h * MP : (h + 1) * MP]))
    y = jnp.concatenate(parts, axis=1)
    y = y + dot_last(cmat, enter.astype(bf16)) * dot(jnp.exp(cum), spread, highest)
    y = y + xs * dot(jnp.broadcast_to(head_ref[2:3, :], (8, 128)), spread, highest)[0:1, :]
    tail = dot(jnp.exp(last - cum) * step, spread, highest)
    keep = jnp.broadcast_to(jnp.exp(cum_t[:, span - 1 : span]), (128, NS))
    new_state = dot_first(spread, keep, highest) * enter + dot_first((xs * tail).astype(bf16), bmat)
    state[...] = new_state
    final_ref[0] = new_state
    total[...] = total[...] + last
    decay_ref[0] = total[...]
    z = z_ref[...]
    y_ref[...] = y
    gated_ref[...] = (y * (z * sigmoid(z))).astype(bf16)


def core_fore(turn, early, late, halo, conv, head, init, seq, rows, heads, span):
    inner = heads * MP
    wide = inner + 2 * NS
    count = rows // span
    first = seq * count

    def block(width, at):
        return pl.BlockSpec((span, width), lambda i: (first + i, at))

    def whole(*shape):
        return pl.BlockSpec(shape, lambda i: (0,) * len(shape))

    out = pl.BlockSpec((span, inner), lambda i: (i, 0))
    return pl.pallas_call(
        functools.partial(core_fore_kernel, heads=heads, span=span),
        grid=(count,),
        in_specs=[
            pl.BlockSpec(memory_space=pltpu.SMEM),
            block(inner, 0),
            block(2 * NS, (inner + 128) // (2 * NS)),
            block(inner, 0),
            block(128, inner // 128),
            whole(1, 8, wide),
            whole(8, wide),
            whole(8, 128),
            whole(1, inner, NS),
        ],
        out_specs=[
            out,
            out,
            pl.BlockSpec((1, 1, inner, NS), lambda i: (0, i, 0, 0)),
            whole(1, inner, NS),
            whole(1, 8, 128),
        ],
        out_shape=[
            jax.ShapeDtypeStruct((rows, inner), bf16),
            jax.ShapeDtypeStruct((rows, inner), f32),
            jax.ShapeDtypeStruct((1, count, inner, NS), f32),
            jax.ShapeDtypeStruct((1, inner, NS), f32),
            jax.ShapeDtypeStruct((1, 8, 128), f32),
        ],
        scratch_shapes=[
            pltpu.VMEM((span + 8, wide), f32),
            pltpu.VMEM((inner, NS), f32),
            pltpu.VMEM((8, 128), f32),
        ],
        compiler_params=params(1),
        cost_estimate=cost(rows, 26, (late, init)),
        name="core_fore",
    )(turn, late, late, early, late, halo, conv, head, init)


def core_back_kernel(
    turn_ref, x_ref, bc_ref, z_ref, dt_ref, dg_ref, enter_ref, halo_ref, conv_ref, head_ref, exit_ref,
    dlate_ref, gconv_ref, ghead_ref, dinit_ref, dfirst_ref,
    ext, dext, dstate, *, heads, span,
):
    inner = heads * MP
    at = pl.program_id(0)

    @pl.when(at == 0)
    def _():
        gconv_ref[...] = jnp.zeros_like(gconv_ref)
        ghead_ref[...] = jnp.zeros_like(ghead_ref)

    @pl.when(at == 0)
    def _():
        dext[span:, :] = jnp.zeros((8, dext.shape[1]), f32)
        dstate[...] = exit_ref[0]

    ext[0:8, :] = halo_ref[0, 0]
    ext[8:, :inner] = x_ref[...]
    ext[8:, inner:] = bc_ref[...]
    pre = conv_pre(ext, conv_ref, span)
    gate = sigmoid(pre)
    cv = pre * gate
    xs = cv[:, :inner]
    bmat = cv[:, inner : inner + NS].astype(bf16)
    cmat = cv[:, inner + NS :].astype(bf16)
    xb = xs.astype(bf16)
    z = z_ref[...]
    dy = dg_ref[...] * (z * sigmoid(z))
    dyb = dy.astype(bf16)
    spread = head_spread(heads)
    lower = triangle(span)
    raw = pltpu.roll(dt_ref[...], 128 - turn_ref[0], 1) + head_ref[0:1, :]
    step = softplus(raw)
    rate = -jnp.exp(head_ref[1:2, :])
    decay_log = rate * step
    cum = dot(lower.astype(f32), decay_log, highest)
    cum_t = cum.T
    step_t = step.T
    last = cum[span - 1 : span, :]
    enter = enter_ref[0, 0]
    leave = dstate[...]
    pair = dot_last(cmat, bmat)
    dpair = jnp.zeros((span, span), f32)
    lane = lax.broadcasted_iota(jnp.int32, (span, 128), 1)
    line = lax.broadcasted_iota(jnp.int32, (128, span), 0)
    row_sums = jnp.zeros((span, 128), f32)
    col_sums = jnp.zeros((128, span), f32)
    parts = []
    for h in range(heads):
        diff = cum[:, h : h + 1] - cum_t[h : h + 1, :]
        decay = jnp.exp(jnp.where(lower, diff, neg_big))
        now = step_t[h : h + 1, :]
        cut = slice(h * MP, (h + 1) * MP)
        dmix = dot_last(dyb[:, cut], xb[:, cut]) * decay
        both = dmix * pair
        dmix_now = dmix * now
        dpair = dpair + dmix_now
        row_sums = jnp.where(lane == h, jnp.sum(both * now, 1, keepdims=True), row_sums)
        col_sums = jnp.where(line == h, jnp.sum(both, 0, keepdims=True), col_sums)
        mixing = (pair * decay * now).astype(bf16)
        parts.append(dot_first(mixing, dyb[:, cut]))
    dxs = jnp.concatenate(parts, axis=1)
    dstep = col_sums.T
    dcum = row_sums - dstep * step
    dpb = dpair.astype(bf16)
    dcm = dot(dpb, bmat)
    dbm = dot_first(dpb, cmat)
    grown = dot(jnp.exp(cum), spread, highest)
    enter_b = enter.astype(bf16)
    leave_b = leave.astype(bf16)
    dgrown = (dy * grown).astype(bf16)
    dcum = dcum + dot_last(dy * dot_last(cmat, enter_b) * grown, spread, highest)
    dcm = dcm + dot(dgrown, enter_b)
    fade = jnp.exp(last - cum)
    tail = dot(fade * step, spread, highest)
    into = dot_last(bmat, leave_b)
    dxs = dxs + into * tail
    owed = dot_last(xs * into, spread, highest) * fade
    dstep = dstep + owed
    owed = owed * step
    dcum = dcum - owed
    dbm = dbm + dot((xs * tail).astype(bf16), leave_b)
    held = dot(spread, enter * leave, highest)
    held = dot_last(jnp.ones((8, NS), f32), held, highest)[0:1, :]
    dlast = jnp.sum(owed, 0, keepdims=True) + jnp.exp(last) * held
    keep = jnp.broadcast_to(jnp.exp(cum_t[:, span - 1 : span]), (128, NS))
    new_dstate = dot_first(spread, keep, highest) * leave + dot_first(dgrown, cmat)
    dstate[...] = new_dstate
    dinit_ref[0] = new_dstate
    dlog = dot_first(lower.astype(f32), dcum, highest) + dlast
    dstep = dstep + dlog * rate
    ddt = dstep * sigmoid(raw)
    dlate_ref[:, inner : inner + 128] = pltpu.roll(ddt, turn_ref[0], 1).astype(bf16)
    skip = dot(jnp.broadcast_to(head_ref[2:3, :], (8, 128)), spread, highest)[0:1, :]
    dxs = dxs + skip * dy
    ghead_ref[0:1, :] += jnp.sum(ddt, 0, keepdims=True)
    ghead_ref[1:2, :] += jnp.sum(dlog * decay_log, 0, keepdims=True)
    ghead_ref[2:3, :] += jnp.sum(dot_last(dy * xs, spread, highest), 0, keepdims=True)
    slope = gate * (1.0 + pre * (1.0 - gate))
    dpre = jnp.concatenate([dxs, dbm, dcm], axis=1) * slope
    dext[0:span, :] = dpre
    gconv_ref[KW : KW + 1, :] += jnp.sum(dpre, 0, keepdims=True)
    dxbc = jnp.zeros_like(dpre)
    for k in range(KW):
        dxbc = dxbc + conv_ref[k : k + 1, :] * dext[pl.ds(KW - 1 - k, span), :]
        gconv_ref[k : k + 1, :] += jnp.sum(
            dpre * ext[pl.ds(8 - (KW - 1) + k, span), :], 0, keepdims=True
        )
    dlate_ref[:, :inner] = dxbc[:, :inner].astype(bf16)
    dlate_ref[:, inner + 128 :] = dxbc[:, inner:].astype(bf16)
    dext[span:, :] = dext[0:8, :]
    dfirst_ref[0] = dext[0:8, :]


def core_back(turn, early, late, dmixed, enter, halos, conv, head, leave, seq, heads, span):
    rows = dmixed.shape[0]
    inner = heads * MP
    wide = inner + 2 * NS
    count = rows // span
    first = seq * count

    def block(width, at):
        return pl.BlockSpec((span, width), lambda i: (first + count - 1 - i, at))

    def own(width):
        return pl.BlockSpec((span, width), lambda i: (count - 1 - i, 0))

    def whole(*shape):
        return pl.BlockSpec(shape, lambda i: (0,) * len(shape))

    return pl.pallas_call(
        functools.partial(core_back_kernel, heads=heads, span=span),
        grid=(count,),
        in_specs=[
            pl.BlockSpec(memory_space=pltpu.SMEM),
            block(inner, 0),
            block(2 * NS, (inner + 128) // (2 * NS)),
            block(inner, 0),
            block(128, inner // 128),
            own(inner),
            pl.BlockSpec((1, 1, inner, NS), lambda i: (0, count - 1 - i, 0, 0)),
            pl.BlockSpec((1, 1, 8, wide), lambda i: (0, count - 1 - i, 0, 0)),
            whole(8, wide),
            whole(8, 128),
            whole(1, inner, NS),
        ],
        out_specs=[
            own(late.shape[1]),
            whole(8, wide),
            whole(8, 128),
            whole(1, inner, NS),
            whole(1, 8, wide),
        ],
        out_shape=[
            jax.ShapeDtypeStruct((rows, late.shape[1]), bf16),
            jax.ShapeDtypeStruct((8, wide), f32),
            jax.ShapeDtypeStruct((8, 128), f32),
            jax.ShapeDtypeStruct((1, inner, NS), f32),
            jax.ShapeDtypeStruct((1, 8, wide), f32),
        ],
        scratch_shapes=[
            pltpu.VMEM((span + 8, wide), f32),
            pltpu.VMEM((span + 8, wide), f32),
            pltpu.VMEM((inner, NS), f32),
        ],
        compiler_params=params(1),
        cost_estimate=cost(rows, 60, (late, enter)),
        name="core_back",
    )(turn, late, late, early, late, dmixed, enter, halos, conv, head, leave)


def passed_along(block, distance):
    devices = range(lax.axis_size("g"))
    route = [(i - distance, i) for i in devices if i - distance in devices]
    return lax.ppermute(block, "g", route)


def entering(decay, local, reverse):
    peers, here = lax.axis_size("g"), lax.axis_index("g")
    decays = lax.all_gather(decay, "g")
    locals_ = lax.all_gather(local.astype(bf16), "g")
    state = jnp.zeros_like(local)
    for k in range(peers):
        at = peers - 1 - k if reverse else k
        reached = (at > here) if reverse else (at < here)
        state = jnp.where(reached, decays[at] * state + locals_[at].astype(f32), state)
    return state


def head_decay(decay_log, heads):
    keep = jnp.exp(decay_log[:, 0, :heads])
    return jnp.repeat(keep, MP, axis=1)[:, :, None]


def body(
    tokens, lengths, gains, w_query, w_keyval, w_attn_out, w_in, w_dt, conv_params, head_params,
    w_mamba_out, w_gate_up, w_down, cotangent,
):
    seqs, rows_seq, width = tokens.shape
    dp, groups, team = lax.axis_size("dp"), lax.axis_size("g"), lax.axis_size(TEAM)
    devices, line, plane = lax.axis_size(ALL), lax.axis_size(LINE), lax.axis_size(PLANE)
    seq_size = groups * team
    me = lax.axis_index(TEAM)
    heads = MH // team
    inner = heads * MP
    query = HQ * HD // team
    block_len = rows_seq * team
    rows = seqs * block_len
    held = w_query.shape[0]
    span = math.gcd(256, block_len)
    start = (lax.axis_index("g") * block_len).astype(jnp.int32).reshape(1)
    kv_head = me * (HQ // team) * KV // HQ

    core = lax.axis_index("c")
    conv_flat = conv_params.reshape(-1)
    conv_cols = -(-conv_flat.shape[0] // held)
    conv_flat = jnp.pad(conv_flat, (0, conv_cols * held - conv_flat.shape[0]))
    shared = 128 + 2 * NS
    keys_size = 2 * KV * HD
    packed = jnp.concatenate(
        [
            jnp.pad(w_dt, ((0, 0), (0, 128 - MH))),
            w_in[:, 2 * MI :],
            w_keyval,
            gains.T,
            conv_flat.reshape(held, conv_cols),
            jnp.zeros((held, shared - keys_size - 2 - conv_cols), bf16),
        ],
        axis=1,
    )
    w_big = jnp.concatenate(
        [
            w_in[:, :MI].reshape(held, team, inner),
            w_query.reshape(held, team, query),
            w_in[:, MI : 2 * MI].reshape(held, team, inner),
            jnp.tile(packed.reshape(held, 2, shared), (1, team // 2, 1)),
        ],
        axis=2,
    ).transpose(1, 0, 2)
    slots = []
    for k in range(team):
        slot = lax.dynamic_index_in_dim(w_big, me ^ k, 0, keepdims=False)
        route = [(i, i ^ k) for i in range(team)]
        slots.append(lax.ppermute(slot, TEAM, route) if k else slot)
    w_big = slots
    ffn_block = w_down.shape[0]
    w_gu = w_gate_up.reshape(held, 2, dp, line, plane // dp, ffn_block).transpose(4, 2, 0, 1, 3, 5)
    w_gu = w_gu.reshape(plane // dp, dp, held, 2 * line * ffn_block)
    mine_dp = lax.axis_index("dp")
    slots = []
    for j in range(2):
        for k in range(dp):
            slot = lax.dynamic_slice(
                w_gu, (core ^ j, mine_dp ^ k, 0, 0), (1, 1, held, 2 * line * ffn_block)
            )[0, 0]
            if j or k:
                route = [(2 * a + b, 2 * (a ^ k) + (b ^ j)) for a in range(dp) for b in range(2)]
                slot = lax.ppermute(slot, PLANE, route)
            slots.append(slot)
    w_gu = slots
    ratio = team // dp
    part = seq_size // ratio
    attn_rows, mamba_rows = w_attn_out.shape[0], w_mamba_out.shape[0]
    out_rows = attn_rows + mamba_rows
    cut = width // dp
    w_out = jnp.concatenate([w_attn_out, w_mamba_out], axis=0)
    w_out = w_out.reshape(out_rows, dp, cut)
    quarters = []
    for k in range(dp):
        quarter = lax.dynamic_index_in_dim(w_out, mine_dp ^ k, 1, keepdims=False)
        quarters.append(swap(quarter, "dp", k) if k else quarter)
    w_big, w_gu, quarters = lax.optimization_barrier((w_big, w_gu, quarters))
    w_big = join_rows(w_big, me)
    if groups > 1:
        w_big = lax.all_gather(w_big, "g", axis=0, tiled=True)
    block_tokens = lax.all_gather(after(tokens, w_big), TEAM, axis=1, tiled=True)
    block_tokens = block_tokens.reshape(rows, width)
    positions = start[0] + jnp.arange(block_len, dtype=jnp.int32)
    cosine, sine = rope_tables(positions, HD)
    blocks = parts_dp(w_big)
    key_at = inner + query
    others = [swap(part[:, inner + key_at :], "c", 1) for part, _, _ in blocks]
    columns = 2 * line * ffn_block
    folded = [w_down[:, i * columns : (i + 1) * columns] for i in range(width // columns)]
    w_ffn = jnp.concatenate([*w_gu, *folded], axis=0)
    w_out = jnp.stack(quarters)
    others, w_ffn, w_out, cosine, sine = lax.optimization_barrier(
        (others, w_ffn, w_out, cosine, sine)
    )
    w_early, w_late, rest = join_weights(blocks, others, inner, key_at, shared, kv_head)
    gain_all = rest[:, :2].astype(f32).T
    conv_all = rest[:, 2 : 2 + conv_cols]
    conv_all = conv_all.reshape(devices, held * conv_cols)[:, : conv_params.size]
    conv_all = (
        conv_all.reshape(devices, KW + 1, -1).transpose(1, 0, 2).reshape(KW + 1, -1).astype(f32)
    )
    conv_own = jnp.concatenate(
        [lax.dynamic_slice_in_dim(conv_all, me * inner, inner, 1), conv_all[:, MI:]], axis=1
    )
    conv_own = jnp.pad(conv_own, ((0, 8 - KW - 1), (0, 0)))
    head_own = jnp.pad(
        lax.dynamic_slice_in_dim(head_params, me * heads, heads, 1), ((0, 5), (0, 128 - heads))
    )
    turn = (me * heads).astype(jnp.int32).reshape(1)
    block_tokens, w_ffn, w_early, w_late, gain_all = lax.optimization_barrier(
        (block_tokens, w_ffn, w_early, w_late, gain_all)
    )
    w_ffn = lax.all_gather(w_ffn, LINE, axis=0, tiled=False).reshape(line, -1, columns)
    my_seq = lax.axis_index(SEQ)
    if part == dp and groups == 1:
        parts = []
        for k in range(part):
            block = lax.dynamic_index_in_dim(w_out, mine_dp ^ (me % part) ^ k, 0, keepdims=False)
            route = [(i, ratio * ((i % part) ^ k) + i // part) for i in range(team)]
            parts.append(lax.ppermute(block, TEAM, route))
        w_out = jnp.stack(parts)
    else:
        order = mine_dp ^ jnp.arange(dp)
        w_out = jnp.take(w_out, order, axis=0)
        mine = (jnp.arange(ratio) == my_seq // part)[None, :, None, None]
        w_out = jnp.where(mine, w_out[:, None], jnp.zeros((), bf16))
        w_out = jnp.broadcast_to(
            w_out.reshape(1, team, out_rows, cut), (groups, team, out_rows, cut)
        ).reshape(-1, out_rows, cut)
        w_out = lax.all_to_all(w_out, SEQ, 0, 0, tiled=True)
        w_out = lax.dynamic_slice_in_dim(w_out, (me % ratio) * part, part, 0)
        w_out = jnp.concatenate(
            [w_out[:, attn_rows:].reshape(-1, cut), w_out[:, :attn_rows].reshape(-1, cut)], axis=0
        )

    own_positions = my_seq * rows_seq + jnp.arange(rows_seq, dtype=jnp.int32)
    valid = (own_positions[None, :] < lengths[:, None]).astype(f32)[:, :, None]
    cot = cotangent.astype(f32)

    norm1 = rms_norm(block_tokens.astype(f32), gain_all[0]).astype(bf16)
    early = dot(norm1, w_early)
    late = dot(norm1, w_late)
    early, late, w_out = lax.optimization_barrier((early, late, w_out))
    if w_out.ndim == 3:
        w_out = join_out(from_dp(w_out), me // ratio, attn_rows, mamba_rows)
    else:
        w_out = join_columns(from_dp(w_out))
    q = rotate(early[:, inner:key_at].reshape(seqs, block_len, HD), cosine, sine).astype(bf16)
    k = rotate(
        early[:, key_at : key_at + HD].reshape(seqs, block_len, HD), cosine, sine
    ).astype(bf16)
    v = early[:, key_at + HD :].reshape(seqs, block_len, HD).astype(bf16)
    if groups > 1:
        k = lax.all_gather(k, "g", axis=1, tiled=True)
        v = lax.all_gather(v, "g", axis=1, tiled=True)
    wide = inner + 2 * NS
    ends = late.reshape(seqs, block_len // span, span, -1)[:, :, span - 8 :, :]
    ends = jnp.concatenate([ends[..., :inner], ends[..., inner + 128 :]], axis=-1)
    if groups > 1:
        before = passed_along(ends[:, -1].astype(bf16), 1).astype(f32)
    else:
        before = jnp.zeros((seqs, 8, wide), f32)
    halos = jnp.concatenate([before[:, None], ends[:, :-1]], axis=1)
    nothing = jnp.zeros((1, inner, NS), f32)
    mixed_in, ys, enters, decays, logs, mix = [], [], [], [], [], []
    for s in range(seqs):
        fore = functools.partial(core_fore, seq=s, rows=block_len, heads=heads, span=span)
        halo = before[s : s + 1]
        gated, y, enter, final, decay_log = fore(
            turn, early, late, halo, conv_own, head_own, nothing
        )
        if groups > 1:
            decays.append(head_decay(decay_log, heads))
            init = entering(decays[s], final, False)
            gated, y, enter, final, _ = fore(turn, early, late, halo, conv_own, head_own, init)
        attn, log = attend_fore(lengths, start, q, k, v, span, s)
        mixed_in.append(jnp.concatenate([gated, attn[0]], axis=1))
        ys.append(y)
        enters.append(enter)
        logs.append(log)
        partial = dot(mixed_in[s], w_out).astype(bf16)
        mix.append(partial)
        if s == 0:
            early, late, _ = lax.optimization_barrier((early, late, partial))
            grad_ffn = [
                gather_plane((valid[n] * after(cot[n], partial)).astype(bf16)) for n in range(seqs)
            ]
    mix[0], mix[-1], w_ffn = lax.optimization_barrier((mix[0], mix[-1], w_ffn))
    mix = [lax.psum_scatter(partial, TEAM, scatter_dimension=0, tiled=True) for partial in mix]
    mix[0], *grad_ffn = lax.optimization_barrier((mix[0], *grad_ffn))
    w_gu, w_dn = join_hidden(w_ffn, plane, held, dp, width)
    w_gu, w_dn = w_gu.reshape(width, -1), w_dn.reshape(-1, width)

    units = w_dn.shape[0]
    hidden, norm2, act, ffn, grad_gu, grad_hidden, grad_mix = [], [], [], [], [], [], []
    def enter_ffn(s):
        hidden.append(tokens[s].astype(f32) + valid[s] * mix[s].astype(f32))
        norm2_f, pull = jax.vjp(lambda h: rms_norm(h, gain_all[1]), hidden[s])
        return norm2_f.astype(bf16), pull

    block, pull = enter_ffn(0)
    for s in range(seqs):
        near = from_dp(block)
        if s > 0:
            near, local = lax.optimization_barrier((near, local))
            grad_mix.append(lax.all_gather(local, TEAM, axis=0, tiled=True))
        norm2.append(gather_core(near))
        gate_up = dot(norm2[s], w_gu)
        gate, upper = gate_up[:, :units], gate_up[:, units:]
        sig_gate = sigmoid(gate)
        act.append((gate * sig_gate * upper).astype(bf16))
        grad_act = dot_last(grad_ffn[s], w_dn)
        grad_gate = grad_act * upper * (sig_gate * (1.0 + gate * (1.0 - sig_gate)))
        grad_upper = grad_act * gate * sig_gate
        grad_gu.append(jnp.concatenate([grad_gate, grad_upper], 1).astype(bf16))
        partial = dot_last(grad_gu[s], w_gu).astype(bf16)
        ffn.append(dot(act[s], w_dn).astype(bf16))
        near = scatter_core(partial)
        if s < seqs - 1:
            mix[s + 1] = after(mix[s + 1], partial)
            block, next_pull = enter_ffn(s + 1)
            block, near = lax.optimization_barrier((block, near))
        else:
            ffn = [scatter_core(part_ffn) for part_ffn in ffn]
            grad_mix[0], near, ffn = lax.optimization_barrier((grad_mix[0], near, ffn))
        (grad_hidden_norm,) = pull(scatter_near(near))
        if s < seqs - 1:
            pull = next_pull
        grad_hidden.append(cot[s] + grad_hidden_norm)
        local = (valid[s] * grad_hidden[s]).astype(bf16)

    own_conv = conv_params.shape[1]
    rest_size = (KW + 1) * own_conv + 3 * MH
    rest_cols = -(-rest_size // held)

    def to_owners(partial):
        if groups > 1:
            partial = lax.psum_scatter(partial, "g", scatter_dimension=0, tiled=True)
        partial = partial.astype(bf16).reshape(team, held, -1)
        return lax.all_to_all(partial, TEAM, 0, 0, tiled=True).transpose(1, 0, 2).astype(f32)

    def small_grads(gconv, ghead):
        grad_conv = jnp.concatenate(
            [
                lax.dynamic_update_slice_in_dim(
                    jnp.zeros((KW + 1, MI), f32), gconv[: KW + 1, :inner], me * inner, 1
                ),
                gconv[: KW + 1, inner:],
            ],
            axis=1,
        )
        grad_head = lax.dynamic_update_slice_in_dim(
            jnp.zeros((3, MH), f32), ghead[:3, :heads], me * heads, 1
        )
        rest = jnp.concatenate(
            [
                grad_conv.reshape(KW + 1, devices, -1).transpose(1, 0, 2).reshape(devices, -1),
                jnp.broadcast_to(grad_head.reshape(1, -1), (devices, 3 * MH)),
            ],
            axis=1,
        )
        rest = jnp.pad(rest, ((0, 0), (0, held * rest_cols - rest_size)))
        return rest.reshape(width, rest_cols)

    dearly, dlate, grad_norm1 = [], [], []
    gconv, ghead = 0.0, 0.0
    for s in range(seqs):
        grad_mixed_in = dot_last(grad_mix[s], w_out)
        if s == seqs - 1:
            grad_w_out = sum(map(dot_first, mixed_in, grad_mix)).astype(bf16)
            grad_mixed_in, grad_w_out = lax.optimization_barrier((grad_mixed_in, grad_w_out))
            grad_w_out = scatter_dp(grad_w_out, 1)
            if groups > 1:
                grad_w_out = lax.psum(grad_w_out, "g")
            grad_w_out = grad_w_out.astype(bf16)
        if s == 0:
            grad_mixed_in, local = lax.optimization_barrier((grad_mixed_in, local))
            if seqs > 1:
                grad_mix.append(lax.all_gather(local, TEAM, axis=0, tiled=True))
            ffn = [scatter_near(near) for near in after(ffn, local)]
            mixed = [(hidden[n] + valid[n] * ffn[n]).astype(bf16) for n in range(seqs)]
            mixed = jnp.stack(mixed)
        dq, dk, dv = attend_back(lengths, start, q, k, v, grad_mixed_in, logs[s], span, s)
        if groups > 1:
            dk = lax.psum_scatter(dk, "g", scatter_dimension=1, tiled=True)
            dv = lax.psum_scatter(dv, "g", scatter_dimension=1, tiled=True)
        dq = rotate_back(dq[0], cosine, sine).astype(bf16)
        dk = rotate_back(dk[0], cosine, sine).astype(bf16)
        z = early[s * block_len : (s + 1) * block_len, :inner]
        sig_z = sigmoid(z)
        dz = grad_mixed_in[:, :inner] * ys[s] * (sig_z * (1.0 + z * (1.0 - sig_z)))
        dearly.append(jnp.concatenate([dz.astype(bf16), dq, dk, dv[0].astype(bf16)], axis=1))
        if s == seqs - 1:
            grad_early = dot_first(norm1, jnp.concatenate(dearly, axis=0)).astype(bf16)
            early_cuts = cuts_dp(grad_early, 0)
            grad_w_out = jnp.concatenate(
                [
                    grad_w_out[inner:].reshape(part, attn_rows, cut),
                    grad_w_out[:inner].reshape(part, mamba_rows, cut),
                ],
                axis=1,
            )
            grad_w_out = lax.dynamic_update_slice_in_dim(
                jnp.zeros((seq_size, out_rows, cut), bf16), grad_w_out, (me % ratio) * part, 0
            )
            grad_w_gu = lax.all_to_all(
                grad_w_gu.reshape(plane, held, 2 * line * ffn_block), PLANE, 0, 0, tiled=True
            )
            grad_mixed_in, early_cuts, grad_w_out, grad_w_gu = lax.optimization_barrier(
                (grad_mixed_in, early_cuts, grad_w_out, grad_w_gu)
            )
            grad_early = sum_cuts(early_cuts)
            grad_w_out = lax.all_to_all(grad_w_out, SEQ, 0, 0, tiled=True)
        back = functools.partial(core_back, seq=s, heads=heads, span=span)
        halo = halos[s : s + 1]
        dlate_s, gconv_s, ghead_s, dinit, dfirst = back(
            turn, early, late, grad_mixed_in, enters[s], halo, conv_own, head_own, nothing
        )
        if groups > 1:
            leave = entering(decays[s], dinit, True)
            dlate_s, gconv_s, ghead_s, dinit, dfirst = back(
                turn, early, late, grad_mixed_in, enters[s], halo, conv_own, head_own, leave
            )
            padded = jnp.concatenate([jnp.zeros((1, KW - 1, wide), f32), dfirst], axis=1)
            rim = sum(
                conv_own[j][None, None] * padded[:, KW - 1 - j : 2 * (KW - 1) - j]
                for j in range(KW)
            )
            rim = passed_along(rim.astype(bf16), -1).astype(f32)
            rim = jnp.pad(rim[0], ((block_len - KW + 1, 0), (0, 0)))
            step_gap = jnp.zeros((block_len, 128), f32)
            rim = jnp.concatenate([rim[:, :inner], step_gap, rim[:, inner:]], axis=1)
            dlate_s = (dlate_s.astype(f32) + rim).astype(bf16)
        gconv, ghead = gconv + gconv_s, ghead + ghead_s
        if s == 0:
            dlate_s, norm2, act = lax.optimization_barrier((dlate_s, norm2, act))
            grad_w_gu = sum(map(dot_first, norm2, grad_gu)).astype(bf16)
            grad_w_gu = grad_w_gu.reshape(dp, line, plane // dp, held, 2 * line * ffn_block)
            grad_w_gu = grad_w_gu.transpose(1, 0, 2, 3, 4).reshape(width, -1)
            dlate_s, grad_w_gu = lax.optimization_barrier((dlate_s, grad_w_gu))
            grad_w_gu = lax.psum_scatter(grad_w_gu, LINE, scatter_dimension=0, tiled=True)
        if s == seqs - 1:
            dlate_s, grad_early, grad_w_out = lax.optimization_barrier(
                (dlate_s, grad_early, grad_w_out)
            )
            grad_w_out = grad_w_out.reshape(groups, dp, ratio, out_rows, cut)[0]
            grad_w_out = lax.dynamic_index_in_dim(grad_w_out, my_seq // part, 1, keepdims=False)
            grad_w_out = lax.all_to_all(grad_w_out, "dp", 0, 0, tiled=True)
            grad_late = dot_first(norm1, jnp.concatenate([*dlate, dlate_s], axis=0))
            rest_at = inner + MH
            grad_late = grad_late + jnp.pad(
                small_grads(gconv, ghead),
                ((0, 0), (rest_at, grad_late.shape[1] - rest_at - rest_cols)),
            )
            late_cuts = cuts_dp(grad_late.astype(bf16), 0)
            dlate_s, late_cuts, grad_w_out = lax.optimization_barrier(
                (dlate_s, late_cuts, grad_w_out)
            )
            grad_late = sum_cuts(late_cuts)
        dlate.append(dlate_s)
        partial = (dot_last(dearly[s], w_early) + dot_last(dlate_s, w_late)).astype(bf16)
        if s == seqs - 1:
            grad_w_out = grad_w_out.transpose(1, 0, 2).reshape(out_rows, width).astype(f32)
            grad_early = to_owners(grad_early)
        grad_norm1.append(lax.psum_scatter(partial, TEAM, scatter_dimension=0, tiled=True))
        if s == 0:
            grad_w_dn = sum(map(dot_first, act, after(grad_ffn, partial))).astype(bf16)
            grad_mix[1:], grad_w_dn, mixed = lax.optimization_barrier(
                (grad_mix[1:], grad_w_dn, mixed)
            )
            grad_down = lax.psum_scatter(grad_w_dn, LINE, scatter_dimension=0, tiled=True)
            grad_down = grad_down.astype(f32)
    grad_gate_up = (
        grad_w_gu.reshape(dp, plane // dp, held, 2, line, ffn_block)
        .transpose(2, 3, 0, 4, 1, 5)
        .reshape(held, -1)
        .astype(f32)
    )
    grad_late, grad_w_out, grad_early = lax.optimization_barrier(
        (grad_late, grad_w_out, grad_early)
    )
    grad_late = to_owners(grad_late)
    grad_z = grad_early[:, :, :inner].reshape(held, MI)
    grad_query = grad_early[:, :, inner:key_at].reshape(held, -1)
    grad_keyval = grad_early[:, :, key_at:].reshape(held, KV, team // KV, 2, HD)
    grad_keyval = jnp.sum(grad_keyval, axis=2).transpose(0, 2, 1, 3).reshape(held, -1)
    grad_x = grad_late[:, :, :inner].reshape(held, MI)
    grad_dt = jnp.sum(grad_late[:, :, inner : inner + MH], axis=1)
    grad_bc = jnp.sum(grad_late[:, :, inner + 128 :], axis=1)
    grad_in = jnp.concatenate([grad_z, grad_x, grad_bc], axis=1)

    grad_gains = [
        jnp.sum(w_in.astype(f32) * grad_in, 1)
        + jnp.sum(w_query.astype(f32) * grad_query, 1)
        + jnp.sum(w_keyval.astype(f32) * grad_keyval, 1)
        + jnp.sum(w_dt.astype(f32) * grad_dt, 1),
        jnp.sum(w_gate_up.astype(f32) * grad_gate_up, 1),
    ]
    grad_gains = jnp.stack(grad_gains) / gains.astype(f32)
    rest = jnp.sum(grad_late[:, :, rest_at : rest_at + rest_cols], axis=1).reshape(-1)
    conv_end = (KW + 1) * own_conv
    grad_conv = rest[:conv_end].reshape(KW + 1, own_conv)
    head_total = rest[conv_end:rest_size].reshape(3, MH)
    grad_tokens = []
    for s in range(seqs):
        _, norm1_pull = jax.vjp(lambda v: rms_norm(v, gain_all[0]), tokens[s].astype(f32))
        (grad_token_norm,) = norm1_pull(grad_norm1[s].astype(f32))
        grad_tokens.append((grad_hidden[s] + grad_token_norm).astype(bf16))
    grad_tokens = jnp.stack(grad_tokens)
    grad_attn_out, grad_mamba_out = grad_w_out[:attn_rows], grad_w_out[attn_rows:]
    return (
        mixed,
        grad_tokens,
        grad_gains,
        grad_query,
        grad_keyval,
        grad_attn_out,
        grad_in,
        grad_dt,
        grad_conv,
        head_total[:2],
        head_total[2],
        grad_mamba_out,
        grad_gate_up,
        grad_down,
    )


def solution(mesh):
    dp, seq = mesh.shape["dp"], mesh.shape["seq"]
    team = math.gcd(math.gcd(HQ, MH), seq)
    split = Mesh(mesh.devices.reshape(dp, seq // team, team // 2, 2), ALL)
    rows = P(ALL, None)
    cols = P(None, ALL)
    acts = P("dp", SEQ, None)
    return jax.shard_map(
        body,
        mesh=split,
        in_specs=(
            acts, P("dp"), cols, rows, rows, rows, rows, rows, cols, P(), rows, rows, rows, acts,
        ),
        out_specs=(
            acts, acts, cols, rows, rows, rows, rows, rows, cols, P(), P(), rows, rows, rows,
        ),
        check_vma=False,
    )
```
